128 devices in a mesh: blocks: 32 (over y, z, core), wide: 4 (over x).
Axes of the slice: x: 4, y: 4, z: 4, core: 2. Of those that a mesh axis runs over, the one named last changes fastest.
Arguments:
- thermal_anomaly: float32 [480, 61440], P('wide', 'blocks'), may hold values from -6 to 6
- saltiness_anomaly: float32 [480, 61440], P('wide', 'blocks'), may hold values from -6 to 6
- zonal_current_layers: float32 [480, 61440], P('wide', 'blocks'), may hold values from -6 to 6
- meridional_current_layers: float32 [480, 61440], P('wide', 'blocks'), may hold values from -6 to 6
- sea_elevation: float32 [480, 7680], P('wide', 'blocks'), may hold values from -6 to 6
- zonal_current_average: float32 [480, 7680], P('wide', 'blocks'), may hold values from -3 to 3
- meridional_current_average: float32 [480, 7680], P('wide', 'blocks'), may hold values from -3 to 3
- water_tile_flags: int32 [8, 128], P('wide', 'blocks'), may hold values 0 or 1
- diffusivity_selector: int32 [480, 7680], P('wide', 'blocks'), may hold values from 0 to 7
- second_order_diffusivity: float32 [8], replicated, may hold values from 0.03 to 0.12
- fourth_order_diffusivity: float32 [8], replicated, may hold values from 0.004 to 0.016
Outputs:
- temperature_next: float32 [480, 61440], P('wide', 'blocks')
- salinity_next: float32 [480, 61440], P('wide', 'blocks')
- zonal_next: float32 [480, 61440], P('wide', 'blocks')
- meridional_next: float32 [480, 61440], P('wide', 'blocks')
- height_next: float32 [480, 7680], P('wide', 'blocks')
- zonal_transport_next: float32 [480, 7680], P('wide', 'blocks')
- meridional_transport_next: float32 [480, 7680], P('wide', 'blocks')
The draws below stay inside these ranges and needn't reach their ends.
All inputs are finite; a program needn't handle non-finite values. No bound on the sum of `water_tile_flags` on one device may be relied on, other than what follows from the above.
Results may differ from the reference program's by a relative error of at most 0.00002.
Values sent between devices are 32-bit elements; how exact they have to be, the bound alone decides.
A program may use at most 128 MiB of HBM per device.

```python
import math
import jax
import jax.numpy as jnp

BLOCK = 60
DEPTH_LAYERS = 8
NCOEF = 8
NSUB = 4
LONGITUDE_SPAN = 7680
LATITUDE_SPAN = 480
GBX = 128
GBY = 8


def touch_ends(result, rng, low, top_value):
    place = [jax.random.randint(jax.random.fold_in(rng, axis), (), 0, length) for axis, length in enumerate(result.shape)]
    main_axis = result.shape.index(max(result.shape))
    next_to = place[:main_axis] + [(place[main_axis] + 1) % result.shape[main_axis]] + place[main_axis + 1:]
    return result.at[tuple(place)].set(low).at[tuple(next_to)].set(top_value)


def block_scale(own_key, shape, cuts, least, high):
    def one(dim, shards_of):
        heights = jax.random.uniform(jax.random.fold_in(jax.random.fold_in(own_key, 6), dim), (shards_of,), jnp.float32, least / len(cuts), high / len(cuts))
        return jnp.repeat(jnp.exp(heights), shape[dim] // shards_of).reshape((-1,) + (1,) * (len(shape) - dim - 1))

    loudness = one(*cuts[0])
    for cut in cuts[1:]:
        loudness = loudness * one(*cut)
    return loudness


def scatter_about(stream_key, extent, width, bound, cuts=(), held_as=jnp.bfloat16):
    drawn = width * jax.random.normal(stream_key, extent, jnp.float32)
    if cuts:
        drawn = drawn * block_scale(stream_key, extent, cuts, -0.22, 0.18)
    return jnp.clip(drawn, -bound, bound).astype(held_as)


def setup_inputs(seed: int = 0) -> dict:
    splits = jax.random.split(jax.random.key(seed), 12)
    thermal_anomaly = scatter_about(splits[0], (LATITUDE_SPAN, LONGITUDE_SPAN * DEPTH_LAYERS), 1.0, 6.0, ((0, 4), (1, 32)), jnp.float32)
    saltiness_anomaly = scatter_about(splits[1], (LATITUDE_SPAN, LONGITUDE_SPAN * DEPTH_LAYERS), 1.0, 6.0, ((0, 4), (1, 32)), jnp.float32)
    zonal_current_layers = scatter_about(splits[2], (LATITUDE_SPAN, LONGITUDE_SPAN * DEPTH_LAYERS), 1.0, 6.0, ((0, 4), (1, 32)), jnp.float32)
    meridional_current_layers = scatter_about(splits[3], (LATITUDE_SPAN, LONGITUDE_SPAN * DEPTH_LAYERS), 1.0, 6.0, ((0, 4), (1, 32)), jnp.float32)
    sea_elevation = scatter_about(splits[4], (LATITUDE_SPAN, LONGITUDE_SPAN), 1.0, 6.0, ((0, 4), (1, 32)), jnp.float32)
    zonal_current_average = scatter_about(splits[5], (LATITUDE_SPAN, LONGITUDE_SPAN), 0.5, 3.0, ((0, 4), (1, 32)), jnp.float32)
    meridional_current_average = scatter_about(splits[6], (LATITUDE_SPAN, LONGITUDE_SPAN), 0.5, 3.0, ((0, 4), (1, 32)), jnp.float32)
    water_tile_flags = touch_ends((jax.random.randint(splits[7], (GBY, GBX), 0, 4) < 3).astype(jnp.int32), jax.random.fold_in(splits[7], 1), 0, 1)
    diffusivity_selector = touch_ends(jax.random.randint(splits[8], (LATITUDE_SPAN, LONGITUDE_SPAN), 0, NCOEF), jax.random.fold_in(splits[8], 1), 0, NCOEF - 1).astype(jnp.int32)
    second_order_diffusivity = jnp.clip(jnp.exp(jax.random.uniform(splits[9], (NCOEF,), jnp.float32, math.log(0.03), math.log(0.12))), 0.03, 0.12)
    fourth_order_diffusivity = jnp.clip(jnp.exp(jax.random.uniform(splits[10], (NCOEF,), jnp.float32, math.log(0.004), math.log(0.016))), 0.004, 0.016)
    return dict(thermal_anomaly=thermal_anomaly, saltiness_anomaly=saltiness_anomaly, zonal_current_layers=zonal_current_layers, meridional_current_layers=meridional_current_layers, sea_elevation=sea_elevation, zonal_current_average=zonal_current_average, meridional_current_average=meridional_current_average, water_tile_flags=water_tile_flags, diffusivity_selector=diffusivity_selector, second_order_diffusivity=second_order_diffusivity, fourth_order_diffusivity=fourth_order_diffusivity)


def block_cells(land_blocks):
    rows, cols = land_blocks.shape
    spread = jnp.broadcast_to(land_blocks.astype(jnp.float32)[:, None, :, None], (rows, BLOCK, cols, BLOCK))
    return spread.reshape(rows * BLOCK, cols * BLOCK)


def lookup(indices, table):
    hits = (indices[None] == jnp.arange(table.shape[0], dtype=jnp.int32)[:, None, None]).astype(jnp.float32)
    return jnp.sum(hits * table[:, None, None], axis=0)


def extend_global(horizontal_sheets, rim_depth, parity):
    zonal_ext = jnp.concatenate([horizontal_sheets[:, :, -rim_depth:], horizontal_sheets, horizontal_sheets[:, :, :rim_depth]], axis=2)
    south_rows = jnp.zeros((horizontal_sheets.shape[0], rim_depth, zonal_ext.shape[2]), jnp.float32)
    north_rows = zonal_ext[:, -rim_depth:, :][:, ::-1, ::-1] * parity[:, None, None]
    return jnp.concatenate([south_rows, zonal_ext, north_rows], axis=1)


def masked_laplace(field_pad, wet_pad):
    centre = field_pad[..., 1:-1, 1:-1]
    flux_sum = wet_pad[2:, 1:-1] * (field_pad[..., 2:, 1:-1] - centre)
    flux_sum = flux_sum + wet_pad[:-2, 1:-1] * (field_pad[..., :-2, 1:-1] - centre)
    flux_sum = flux_sum + wet_pad[1:-1, 2:] * (field_pad[..., 1:-1, 2:] - centre)
    flux_sum = flux_sum + wet_pad[1:-1, :-2] * (field_pad[..., 1:-1, :-2] - centre)
    return wet_pad[1:-1, 1:-1] * flux_sum


def baroclinic(field_pad, wet_pad, kappa_cells, bihar_cells, water_present):
    lap_once = masked_laplace(field_pad, wet_pad)
    lap_twice = masked_laplace(lap_once, wet_pad[1:-1, 1:-1])
    centre = field_pad[..., 2:-2, 2:-2]
    east_slope = field_pad[..., 2:-2, 3:-1] - field_pad[..., 2:-2, 1:-3]
    north_slope = field_pad[..., 3:-1, 2:-2] - field_pad[..., 1:-3, 2:-2]
    zonal_own = field_pad[2, ..., 2:-2, 2:-2]
    merid_own = field_pad[3, ..., 2:-2, 2:-2]
    tendency = -0.05 * (zonal_own * east_slope + merid_own * north_slope) + kappa_cells * lap_once[..., 1:-1, 1:-1] - bihar_cells * lap_twice
    return water_present * (centre + tendency)


def separate_layers(merged):
    rows = merged.shape[0]
    return merged.reshape(rows, merged.shape[1] // DEPTH_LAYERS, DEPTH_LAYERS).transpose(2, 0, 1)


def from_levels(stacked):
    return stacked.transpose(1, 2, 0).reshape(stacked.shape[1], stacked.shape[2] * DEPTH_LAYERS)


def reference(thermal_anomaly, saltiness_anomaly, zonal_current_layers, meridional_current_layers, sea_elevation, zonal_current_average, meridional_current_average, water_tile_flags, diffusivity_selector, second_order_diffusivity, fourth_order_diffusivity):
    thermal_layers = separate_layers(thermal_anomaly)
    saltiness_layers = separate_layers(saltiness_anomaly)
    westeast_layer_flow = separate_layers(zonal_current_layers)
    southnorth_layer_flow = separate_layers(meridional_current_layers)
    water_present = block_cells(water_tile_flags)
    kappa_cells = lookup(diffusivity_selector, second_order_diffusivity)
    bihar_cells = lookup(diffusivity_selector, fourth_order_diffusivity)
    wet_pad = extend_global(water_present[None], 2, jnp.ones((1,), jnp.float32))[0]
    parity = jnp.array([1.0, 1.0, -1.0, -1.0], jnp.float32)
    levels = []
    for layer_position in range(DEPTH_LAYERS):
        horizontal_sheets = jnp.stack([thermal_layers[layer_position], saltiness_layers[layer_position], westeast_layer_flow[layer_position], southnorth_layer_flow[layer_position]]) * water_present
        extended = extend_global(horizontal_sheets, 2, parity)
        levels.append(baroclinic(extended, wet_pad, kappa_cells, bihar_cells, water_present))
    updated = jnp.stack(levels, axis=1)
    mean_zonal = jnp.mean(updated[2], axis=0)
    mean_merid = jnp.mean(updated[3], axis=0)
    height = water_present * sea_elevation
    zonal_t = water_present * (zonal_current_average + mean_zonal)
    merid_t = water_present * (meridional_current_average + mean_merid)
    vector_parity = jnp.array([-1.0, -1.0], jnp.float32)
    scalar_parity = jnp.ones((1,), jnp.float32)
    for substep in range(NSUB):
        extended = extend_global(jnp.stack([zonal_t, merid_t]), 1, vector_parity)
        divergence = (extended[0, 1:-1, 2:] - extended[0, 1:-1, :-2]) + (extended[1, 2:, 1:-1] - extended[1, :-2, 1:-1])
        height = height - 0.3 * water_present * divergence
        height_ext = extend_global(height[None], 1, scalar_parity)[0]
        zonal_t = water_present * (zonal_t - 0.3 * (height_ext[1:-1, 2:] - height_ext[1:-1, :-2]))
        merid_t = water_present * (merid_t - 0.3 * (height_ext[2:, 1:-1] - height_ext[:-2, 1:-1]))
    zonal_next = water_present * (updated[2] - mean_zonal + zonal_t)
    merid_next = water_present * (updated[3] - mean_merid + merid_t)
    return from_levels(updated[0]), from_levels(updated[1]), from_levels(zonal_next), from_levels(merid_next), height, zonal_t, merid_t
```

```python
import functools

import jax
import jax.numpy as jnp
from jax import lax
from jax.experimental import pallas as pl
from jax.experimental.pallas import tpu as pltpu
from jax.sharding import PartitionSpec as P

BLOCK = 60
LEVELS = 8
NSUB = 4
ROWS = 120
COLS = 240
LANES = COLS * LEVELS
TILES = LANES // 128
RING = TILES + 1
PAD = 16
BAND = ROWS + 2 * PAD
MESH = pl.DeviceIdType.MESH
VMEM_BYTES = 56 * 1024 * 1024


def lanes_of(shape=(8, 128)):
    return lax.broadcasted_iota(jnp.int32, shape, 1)


def rows_of(shape=(8, 128)):
    return lax.broadcasted_iota(jnp.int32, shape, 0)


def lane_xor(tile, bit):
    keep = (lanes_of(tile.shape) // bit) % 2 == 0
    return jnp.where(keep, pltpu.roll(tile, 128 - bit, 1), pltpu.roll(tile, bit, 1))


def row_xor(tile, bit):
    keep = (rows_of(tile.shape) // bit) % 2 == 0
    return jnp.where(keep, pltpu.roll(tile, 8 - bit, 0), pltpu.roll(tile, bit, 0))


def turn_lanes(tile, bits):
    for bit in bits:
        tile = lane_xor(tile, bit)
    return tile


def turn_rows(tile):
    for bit in (1, 2, 4):
        tile = row_xor(tile, bit)
    return tile


class Neighbours:
    def __init__(self, nb, nw, send, recv):
        self.send, self.recv = send, recv
        b, x = lax.axis_index("blocks"), lax.axis_index("wide")
        self.b, self.x = b, x
        self.top, self.inner, self.above = x == nw - 1, x < nw - 1, x > 0
        self.east, self.west = lax.rem(b + 1, nb), lax.rem(b + nb - 1, nb)
        self.fold = nb - 1 - b
        self.fold_east = lax.rem(2 * nb - 2 - b, nb)
        self.fold_west = lax.rem(nb - b, nb)
        self.own_east = jnp.logical_and(self.top, self.fold_east == b)
        self.own_west = jnp.logical_and(self.top, self.fold_west == b)
        self.far_east = jnp.logical_and(self.top, self.fold_east != b)
        self.far_west = jnp.logical_and(self.top, self.fold_west != b)

    def barrier(self):
        sem = pltpu.get_barrier_semaphore()

        def greet(b, x):
            pl.semaphore_signal(sem, inc=1, device_id=(b, x), device_id_type=MESH)

        b, x = self.b, self.x
        greet(self.east, x)
        greet(self.west, x)

        @pl.when(self.inner)
        def _():
            greet(b, x + 1)
            greet(self.east, x + 1)
            greet(self.west, x + 1)

        @pl.when(self.top)
        def _():
            greet(self.fold, x)

        @pl.when(self.far_east)
        def _():
            greet(self.fold_east, x)

        @pl.when(self.far_west)
        def _():
            greet(self.fold_west, x)

        @pl.when(self.above)
        def _():
            greet(b, x - 1)
            greet(self.east, x - 1)
            greet(self.west, x - 1)

        own = jnp.logical_or(self.own_east, self.own_west)

        @pl.when(x == 0)
        def _():
            pl.semaphore_wait(sem, 5)

        @pl.when(own)
        def _():
            pl.semaphore_wait(sem, 7)

        @pl.when(jnp.logical_and(self.above, jnp.logical_not(own)))
        def _():
            pl.semaphore_wait(sem, 8)

    def copy(self, src, dst, way, slot, b, x):
        return pltpu.make_async_remote_copy(
            src_ref=src,
            dst_ref=dst,
            send_sem=self.send.at[way],
            recv_sem=self.recv.at[slot],
            device_id=(b, x),
            device_id_type=MESH,
        )

    def wire(self, north, south, east, west, rn, rs, rw, re):
        b, x = self.b, self.x
        top_rows, low_rows = pl.ds(ROWS - 8, 8), pl.ds(0, 8)
        mid, lo, hi = pl.ds(8, ROWS), pl.ds(0, 8), pl.ds(ROWS + 8, 8)
        c = self.copy
        return dict(
            always=[
                c(east, rw.at[mid], 0, 0, self.east, x),
                c(west, re.at[mid], 1, 1, self.west, x),
            ],
            inner=[
                c(north, rs, 2, 2, b, x + 1),
                c(east.at[top_rows], rw.at[lo], 4, 4, self.east, x + 1),
                c(west.at[top_rows], re.at[lo], 5, 5, self.west, x + 1),
            ],
            above=[
                c(south, rn, 3, 3, b, x - 1),
                c(east.at[low_rows], rw.at[hi], 6, 6, self.east, x - 1),
                c(west.at[low_rows], re.at[hi], 7, 7, self.west, x - 1),
            ],
            top=[c(north, rn, 2, 3, self.fold, x)],
            far_east=[c(east.at[top_rows], re.at[hi], 4, 7, self.fold_east, x)],
            far_west=[c(west.at[top_rows], rw.at[hi], 5, 6, self.fold_west, x)],
        )

    def start(self, wires, north, south, east, west, rn, rs, rw, re):
        def go(name, cond):
            @pl.when(cond)
            def _():
                for copy in wires[name]:
                    copy.start()

        go("inner", self.inner)
        go("top", self.top)
        go("above", self.above)
        go("far_east", self.far_east)
        go("far_west", self.far_west)
        for copy in wires["always"]:
            copy.start()

        @pl.when(self.own_east)
        def _():
            re[pl.ds(ROWS + 8, 8), :] = east[pl.ds(ROWS - 8, 8), :]

        @pl.when(self.own_west)
        def _():
            rw[pl.ds(ROWS + 8, 8), :] = west[pl.ds(ROWS - 8, 8), :]

    def finish(self, wires):
        w = wires
        for copy in w["always"]:
            copy.wait_recv()
            copy.wait_send()
        w["top"][0].wait_recv()

        @pl.when(self.above)
        def _():
            for copy in w["inner"]:
                copy.wait_recv()
            for copy in w["above"]:
                copy.wait_send()

        @pl.when(jnp.logical_not(self.own_east))
        def _():
            w["far_east"][0].wait_recv()
            w["far_east"][0].wait_send()

        @pl.when(jnp.logical_not(self.own_west))
        def _():
            w["far_west"][0].wait_recv()
            w["far_west"][0].wait_send()

        w["top"][0].wait_send()


def block_row(flags, row, tile):
    low, high = (128 * tile) // (BLOCK * LEVELS), (128 * tile + 127) // (BLOCK * LEVELS)
    value = jnp.full((8, 128), flags[row, low].astype(jnp.float32))
    if low != high:
        value = jnp.where(
            lanes_of() < BLOCK * LEVELS * high - 128 * tile,
            value,
            flags[row, high].astype(jnp.float32),
        )
    return value


def exchange_state_kernel(
    nb, nw, flags, t, s, u, v, hn, hs, hw, he,
    edge_rows, edge_cols, npack, spack, wpack, epack, rn, rs, rw, re, load, send, recv,
):
    fields = (t, s, u, v)
    loads = []
    for f, field in enumerate(fields):
        for side, at in enumerate((0, ROWS - 8)):
            loads.append(pltpu.make_async_copy(
                field.at[pl.ds(at, 8), :], edge_rows.at[f, side], load.at[4 * f + side]))
        for side, at in enumerate((0, LANES - 128)):
            loads.append(pltpu.make_async_copy(
                field.at[:, pl.ds(at, 128)], edge_cols.at[f, side], load.at[4 * f + 2 + side]))
    for copy in loads:
        copy.start()
    near = Neighbours(nb, nw, send, recv)
    near.barrier()
    for copy in loads:
        copy.wait()

    lane = lanes_of()
    for k in range(TILES):
        at = pl.ds(128 * k, 128)
        low, high = block_row(flags, 0, k), block_row(flags, 1, k)
        for f in range(4):
            spack[pl.ds(2 * f, 2), at] = (edge_rows[f, 0, :, at] * low)[0:2]
            npack[pl.ds(2 * f, 2), at] = (edge_rows[f, 1, :, at] * high)[6:8]
    for row, pack in ((0, spack), (1, npack)):
        tail = jnp.zeros((8, 128), jnp.float32)
        for j in range(4):
            tail = jnp.where(lane // 32 == j, flags[row, j].astype(jnp.float32), tail)
        pack[:, pl.ds(LANES, 128)] = tail
    lane_c, row_c = lanes_of((ROWS, 128)), rows_of((ROWS, 128))
    for side, col, pack in ((0, 0, wpack), (1, 3, epack)):
        w = jnp.where(row_c < BLOCK, flags[0, col].astype(jnp.float32), flags[1, col].astype(jnp.float32))
        out = w
        for f in range(4):
            shift = (16 * f + (16 if side else 0)) % 128
            moved = pltpu.roll(edge_cols[f, side], shift, 1) if shift else edge_cols[f, side]
            out = jnp.where(lane_c // 16 == f, moved * w, out)
        pack[...] = out

    wires = near.wire(npack, spack, epack, wpack, rn, rs, rw, re)
    near.start(wires, npack, spack, epack, wpack, rn, rs, rw, re)
    near.finish(wires)

    hs[...] = rs[...]
    hw[...] = rw[...]
    he[...] = re[...]

    @pl.when(near.x == 0)
    def _():
        hs[...] = jnp.zeros(hs.shape, jnp.float32)
        hw[0:8, :] = jnp.zeros((8, 128), jnp.float32)
        he[0:8, :] = jnp.zeros((8, 128), jnp.float32)

    @pl.when(near.inner)
    def _():
        hn[...] = rn[...]

    @pl.when(near.top)
    def _():
        sign = jnp.where(rows_of() < 4, 1.0, -1.0)
        for k in range(TILES):
            tile = turn_lanes(rn[:, pl.ds(128 * (TILES - 1 - k), 128)], (8, 16, 32, 64))
            hn[:, pl.ds(128 * k, 128)] = sign * row_xor(tile, 1)
        hn[:, pl.ds(LANES, 128)] = turn_lanes(rn[:, pl.ds(LANES, 128)], (32, 64))
        flow = jnp.where(lanes_of() // 32 == 1, -1.0, 1.0)
        for got, out in ((rw, hw), (re, he)):
            out[pl.ds(ROWS + 8, 8), :] = flow * turn_rows(lane_xor(got[pl.ds(ROWS + 8, 8), :], 8))


def expand(tile, part):
    index = lanes_of() // LEVELS + 16 * part
    return jnp.take_along_axis(tile, index, axis=1, mode="promise_in_bounds")


def baroclinic_kernel(
    flags, ktab, btab, sel, hn, hs, hw, he, t, s, u, v,
    tn, sn, un, vn, um, vm,
    field, once, part, wet, mix, fade, out, load, store,
):
    loads = [
        [
            pltpu.make_async_copy(
                src.at[:, pl.ds(128 * k, 128)], field.at[f, k, pl.ds(PAD, ROWS), :], load.at[f, k])
            for k in range(TILES)
        ]
        for f, src in enumerate((t, s, u, v))
    ]
    for some in loads:
        for copy in some:
            copy.start()
    lane, sub = lanes_of(), rows_of()

    low_tiles = [block_row(flags, 0, k) for k in range(TILES)]
    high_tiles = [block_row(flags, 1, k) for k in range(TILES)]
    for k in range(TILES):
        def fill(e, carry, k=k):
            base = pl.multiple_of(8 * e, 8)
            wet[k, pl.ds(base, 8), :] = jnp.where(sub + base < PAD + BLOCK, low_tiles[k], high_tiles[k])
            return carry
        lax.fori_loop(2, 2 + TILES, fill, 0)
        low, high = (128 * k) // (BLOCK * LEVELS), (128 * k + 127) // (BLOCK * LEVELS)
        for got, base in ((hs, PAD - 8), (hn, PAD + ROWS)):
            tail = got[:, pl.ds(LANES, 128)]
            value = jnp.broadcast_to(tail[:, 32 * low:32 * low + 1], (8, 128))
            if low != high:
                value = jnp.where(lane < BLOCK * LEVELS * high - 128 * k, value,
                                  jnp.broadcast_to(tail[:, 32 * high:32 * high + 1], (8, 128)))
            wet[k, pl.ds(base, 8), :] = value
    lane_h = lanes_of((ROWS + 16, 128))
    ends = pl.ds(PAD - 8, ROWS + 16)
    west, east = hw[...], he[...]
    wet[TILES, ends, :] = jnp.where(lane_h < 64, pltpu.roll(east, 64, 1), west)
    for f in range(4):
        right = pltpu.roll(east, (128 - 16 * f) % 128, 1) if f else east
        field[f, TILES, ends, :] = jnp.where(lane_h < 64, right, pltpu.roll(west, 112 - 16 * f, 1))
        for k in range(TILES):
            field[f, k, PAD - 2:PAD, :] = hs[2 * f:2 * f + 2, 128 * k:128 * k + 128]
            field[f, k, PAD + ROWS:PAD + ROWS + 2, :] = hn[2 * f:2 * f + 2, 128 * k:128 * k + 128]

    for half, width in ((0, 128), (1, COLS - 128)):
        index = sel[:, 128 * half:128 * half + width]
        kappa = jnp.full(index.shape, ktab[0])
        bihar = jnp.full(index.shape, btab[0])
        for n in range(1, 8):
            kappa = jnp.where(index == n, ktab[n], kappa)
            bihar = jnp.where(index == n, btab[n], bihar)
        mix[0, half, PAD:PAD + ROWS, 0:width] = kappa
        mix[1, half, PAD:PAD + ROWS, 0:width] = bihar

    for some in loads:
        for copy in some:
            copy.wait()

    def mask(e, carry):
        rows = pl.ds(pl.multiple_of(8 * e, 8), 8)
        for k in range(TILES):
            w = wet[k, rows, :]
            for f in range(4):
                field[f, k, rows, :] = field[f, k, rows, :] * w
        return carry

    lax.fori_loop(2, 2 + TILES, mask, 0)

    def first(e, carry):
        base = pl.multiple_of(8 * e, 8)
        here, above, below = pl.ds(base, 8), pl.ds(base + 1, 8), pl.ds(base - 1, 8)
        turned = {}

        def ring(ref, key, k):
            if (key, k) not in turned:
                tile = ref[k, here, :]
                turned[key, k] = (tile, pltpu.roll(tile, 128 - LEVELS, 1), pltpu.roll(tile, LEVELS, 1))
            return turned[key, k]

        def around(ref, key, k):
            tile, left, right = ring(ref, key, k)
            east = jnp.where(lane < 128 - LEVELS, left, ring(ref, key, (k + 1) % RING)[1])
            west = jnp.where(lane < LEVELS, ring(ref, key, (k - 1) % RING)[2], right)
            return tile, east, west, ref[k, above, :], ref[k, below, :]

        for k in range(RING):
            w, we, ww, wn, ws = around(wet, "wet", k)
            count = w * ((we + ww) + (wn + ws))
            if k < TILES:
                kappa = expand(mix[0, k // 8, here, :], k % 8)
                bihar = expand(mix[1, k // 8, here, :], k % 8)
                both = kappa + bihar * count
                fade[k, here, :] = bihar * w
                zonal = 0.05 * ring(field.at[2], 2, k)[0]
                merid = 0.05 * ring(field.at[3], 3, k)[0]
            for f in range(4):
                c, fe, fw, fn, fs = around(field.at[f], f, k)
                lap = w * ((fe + fw) + (fn + fs)) - count * c
                once[f, k, here, :] = lap
                if k < TILES:
                    part[f, k, here, :] = (c - (zonal * (fe - fw) + merid * (fn - fs))) + both * lap
        return carry

    lax.fori_loop(1, 3 + TILES, first, 0)

    def second(e, carry):
        base = pl.multiple_of(8 * e, 8)
        here, above, below = pl.ds(base, 8), pl.ds(base + 1, 8), pl.ds(base - 1, 8)
        rows = pl.ds(pl.multiple_of(base - PAD, 8), 8)
        turned = {}

        def ring(f, k):
            if (f, k) not in turned:
                tile = once[f, k, here, :]
                turned[f, k] = (pltpu.roll(tile, 128 - LEVELS, 1), pltpu.roll(tile, LEVELS, 1))
            return turned[f, k]

        for f in range(4):
            for k in range(TILES):
                left, right = ring(f, k)
                east = jnp.where(lane < 128 - LEVELS, left, ring(f, (k + 1) % RING)[0])
                west = jnp.where(lane < LEVELS, ring(f, (k - 1) % RING)[1], right)
                total = (east + west) + (once[f, k, above, :] + once[f, k, below, :])
                out[f, rows, 128 * k:128 * k + 128] = part[f, k, here, :] - fade[k, here, :] * total
        for f, ref in enumerate((tn, sn, un, vn)):
            pltpu.make_async_copy(out.at[f, rows, :], ref.at[rows, :], store.at[f]).start()
        return carry

    lax.fori_loop(2, 2 + TILES, second, 0)

    span = 128 * LEVELS
    pick = jnp.where(
        lax.broadcasted_iota(jnp.int32, (span, 128), 0) // LEVELS
        == lax.broadcasted_iota(jnp.int32, (span, 128), 1),
        1.0 / LEVELS, 0.0).astype(jnp.bfloat16)
    for f, mean in ((2, um), (3, vm)):
        for half in range(2):
            width = span if half == 0 else LANES - span
            rest = out[f, :, span * half:span * half + width]
            total = None
            for _ in range(3):
                piece = rest.astype(jnp.bfloat16)
                rest = rest - piece.astype(jnp.float32)
                term = jnp.dot(piece, pick[:width], preferred_element_type=jnp.float32)
                total = term if total is None else total + term
            mean[:, 128 * half:128 * half + 128] = total

    for f, ref in enumerate((tn, sn, un, vn)):
        pltpu.make_async_copy(out.at[f], ref, store.at[f]).wait()


def substeps_kernel(
    nb, nw, flags, um, vm, zavg, mavg, elev, height, zonal, merid,
    plane, wpack, epack, rn, rs, rw, re, send, recv,
):
    near = Neighbours(nb, nw, send, recv)
    near.barrier()
    shape = (ROWS, COLS)
    row, col = rows_of(shape), lanes_of(shape)
    w = jnp.zeros(shape, jnp.float32)
    for i in range(2):
        for j in range(4):
            here = jnp.logical_and(row // BLOCK == i, col // BLOCK == j)
            w = jnp.where(here, flags[i, j].astype(jnp.float32), w)
    plane[:, :, 128:256] = jnp.zeros((4, ROWS + 16, 128), jnp.float32)
    plane[0, 0:ROWS, 0:COLS] = w * (zavg[...] + um[:, 0:COLS])
    plane[1, 0:ROWS, 0:COLS] = w * (mavg[...] + vm[:, 0:COLS])
    plane[2, 0:ROWS, 0:COLS] = w * elev[...]
    plane[3, 0:ROWS, 0:COLS] = w
    lane = lanes_of((ROWS, 128))
    right = jnp.zeros((ROWS, 128), jnp.float32)
    left = jnp.zeros((ROWS, 128), jnp.float32)
    for p in range(4):
        right = jnp.where(lane // 8 == p, pltpu.roll(plane[p, 0:ROWS, 128:256], 8 * p + 24, 1), right)
        first = plane[p, 0:ROWS, 0:128]
        left = jnp.where(lane // 8 == p, pltpu.roll(first, 8 * p, 1) if p else first, left)
    epack[...] = right
    wpack[...] = left

    north, south = plane.at[:, pl.ds(ROWS - 8, 8), :], plane.at[:, pl.ds(0, 8), :]
    wires = near.wire(north, south, epack, wpack, rn, rs, rw, re)
    near.start(wires, north, south, epack, wpack, rn, rs, rw, re)
    near.finish(wires)

    @pl.when(near.x == 0)
    def _():
        rs[...] = jnp.zeros(rs.shape, jnp.float32)
        rw[0:8, :] = jnp.zeros((8, 128), jnp.float32)
        re[0:8, :] = jnp.zeros((8, 128), jnp.float32)

    @pl.when(near.top)
    def _():
        reverse = (1, 2, 4, 8, 16, 32, 64)
        for p in range(4):
            sign = -1.0 if p < 2 else 1.0
            first = sign * turn_rows(turn_lanes(rn[p, :, 128:256], reverse))
            last = sign * turn_rows(turn_lanes(rn[p, :, 0:128], reverse))
            rn[p] = pltpu.roll(jnp.concatenate([first, last], axis=1), COLS, 1)
        flow = jnp.where(lanes_of() < 16, -1.0, 1.0)
        for got in (rw, re):
            tile = got[pl.ds(ROWS + 8, 8), :]
            got[pl.ds(ROWS + 8, 8), :] = flow * turn_rows(turn_lanes(tile, (1, 2, 4)))

    plane[:, ROWS:ROWS + 8, :] = rn[...]
    plane[:, ROWS + 8:ROWS + 16, :] = rs[...]
    spans = ((0, 8, ROWS), (ROWS, ROWS + 8, 8), (ROWS + 8, 0, 8))
    for to, at, count in spans:
        lane = lanes_of((count, 128))
        west, east = rw[at:at + count, :], re[at:at + count, :]
        for p in range(4):
            halo = jnp.where(lane < 120, pltpu.roll(east, 112 - 8 * p, 1), pltpu.roll(west, 120 - 8 * p, 1))
            plane[p, to:to + count, 128:256] = jnp.where(lane < 112, plane[p, to:to + count, 128:256], halo)

    zt, mt, h, w = plane[0], plane[1], plane[2], plane[3]
    across, along = 256, ROWS + 16
    for _ in range(NSUB):
        spread = (pltpu.roll(zt, across - 1, 1) - pltpu.roll(zt, 1, 1)) + (
            pltpu.roll(mt, along - 1, 0) - pltpu.roll(mt, 1, 0))
        h = h - 0.3 * w * spread
        zt = w * (zt - 0.3 * (pltpu.roll(h, across - 1, 1) - pltpu.roll(h, 1, 1)))
        mt = w * (mt - 0.3 * (pltpu.roll(h, along - 1, 0) - pltpu.roll(h, 1, 0)))
    height[...] = h[0:ROWS]
    zonal[...] = zt[0:ROWS]
    merid[...] = mt[0:ROWS]


def finish_kernel(un, vn, um, vm, zt, mt, h, zonal, merid, height, zonal_t, merid_t):
    for new, mean, after, to in ((un, um, zt, zonal), (vn, vm, mt, merid)):
        count = new.shape[0]
        for r in range(0, count, 8):
            for half in range(2):
                at = slice(128 * half, 128 * half + 128)
                change = after[r:r + 8, at] - mean[r:r + 8, at]
                for k in range(8 * half, min(8 * half + 8, TILES)):
                    to[r:r + 8, 128 * k:128 * k + 128] = (
                        new[r:r + 8, 128 * k:128 * k + 128] + expand(change, k % 8))
    height[...] = h[:, 0:COLS]
    zonal_t[...] = zt[:, 0:COLS]
    merid_t[...] = mt[:, 0:COLS]


def per_device(nb, nw, t, s, u, v, elev, zavg, mavg, flags, sel, ktab, btab):
    f32 = jnp.float32
    vmem = pl.BlockSpec(memory_space=pltpu.VMEM)
    smem = pl.BlockSpec(memory_space=pltpu.SMEM)
    hbm = pl.BlockSpec(memory_space=pl.ANY)
    side = jax.ShapeDtypeStruct((ROWS + 16, 128), f32)
    cap = jax.ShapeDtypeStruct((8, LANES + 128), f32)
    hn, hs, hw, he = pl.pallas_call(
        functools.partial(exchange_state_kernel, nb, nw),
        out_shape=(cap, cap, side, side),
        in_specs=[smem] + [hbm] * 4,
        out_specs=(vmem,) * 4,
        scratch_shapes=[
            pltpu.VMEM((4, 2, 8, LANES), f32),
            pltpu.VMEM((4, 2, ROWS, 128), f32),
            pltpu.VMEM((8, LANES + 128), f32),
            pltpu.VMEM((8, LANES + 128), f32),
            pltpu.VMEM((ROWS, 128), f32),
            pltpu.VMEM((ROWS, 128), f32),
            pltpu.VMEM((8, LANES + 128), f32),
            pltpu.VMEM((8, LANES + 128), f32),
            pltpu.VMEM((ROWS + 16, 128), f32),
            pltpu.VMEM((ROWS + 16, 128), f32),
            pltpu.SemaphoreType.DMA((16,)),
            pltpu.SemaphoreType.DMA((8,)),
            pltpu.SemaphoreType.DMA((8,)),
        ],
        compiler_params=pltpu.CompilerParams(
            collective_id=0, has_side_effects=True, vmem_limit_bytes=VMEM_BYTES),
        name="exchange_state",
    )(flags, t, s, u, v)

    big = jax.ShapeDtypeStruct((ROWS, LANES), f32)
    plane = jax.ShapeDtypeStruct((ROWS, 256), f32)
    tn, sn, un, vn, um, vm = pl.pallas_call(
        baroclinic_kernel,
        out_shape=(big,) * 4 + (plane,) * 2,
        in_specs=[smem] * 3 + [vmem] * 5 + [hbm] * 4,
        out_specs=(hbm,) * 4 + (vmem,) * 2,
        scratch_shapes=[
            pltpu.VMEM((4, RING, BAND, 128), f32),
            pltpu.VMEM((4, RING, BAND, 128), f32),
            pltpu.VMEM((4, TILES, BAND, 128), f32),
            pltpu.VMEM((RING, BAND, 128), f32),
            pltpu.VMEM((2, 2, BAND, 128), f32),
            pltpu.VMEM((TILES, BAND, 128), f32),
            pltpu.VMEM((4, ROWS, LANES), f32),
            pltpu.SemaphoreType.DMA((4, TILES)),
            pltpu.SemaphoreType.DMA((4,)),
        ],
        compiler_params=pltpu.CompilerParams(vmem_limit_bytes=VMEM_BYTES),
        name="baroclinic",
    )(flags, ktab, btab, sel, hn, hs, hw, he, t, s, u, v)

    height, zt, mt = pl.pallas_call(
        functools.partial(substeps_kernel, nb, nw),
        out_shape=(plane,) * 3,
        in_specs=[smem] + [vmem] * 5,
        out_specs=(vmem,) * 3,
        scratch_shapes=[
            pltpu.VMEM((4, ROWS + 16, 256), f32),
            pltpu.VMEM((ROWS, 128), f32),
            pltpu.VMEM((ROWS, 128), f32),
            pltpu.VMEM((4, 8, 256), f32),
            pltpu.VMEM((4, 8, 256), f32),
            pltpu.VMEM((ROWS + 16, 128), f32),
            pltpu.VMEM((ROWS + 16, 128), f32),
            pltpu.SemaphoreType.DMA((8,)),
            pltpu.SemaphoreType.DMA((8,)),
        ],
        compiler_params=pltpu.CompilerParams(
            collective_id=1, has_side_effects=True, vmem_limit_bytes=VMEM_BYTES),
        name="substeps",
    )(flags, um, vm, zavg, mavg, elev)

    step = 24
    wide = pl.BlockSpec((step, LANES), lambda i: (i, 0))
    flat = pl.BlockSpec((step, 256), lambda i: (i, 0))
    last = pl.BlockSpec((step, COLS), lambda i: (i, 0))
    small = jax.ShapeDtypeStruct((ROWS, COLS), f32)
    zonal, merid, height, zt, mt = pl.pallas_call(
        finish_kernel,
        grid=(ROWS // step,),
        out_shape=(big, big, small, small, small),
        in_specs=[wide, wide] + [flat] * 5,
        out_specs=(wide, wide, last, last, last),
        compiler_params=pltpu.CompilerParams(vmem_limit_bytes=VMEM_BYTES),
        name="finish",
    )(un, vn, um, vm, zt, mt, height)
    return tn, sn, zonal, merid, height, zt, mt


def solution(mesh):
    grid = P("wide", "blocks")
    return jax.shard_map(
        functools.partial(per_device, mesh.shape["blocks"], mesh.shape["wide"]),
        mesh=mesh,
        in_specs=(grid,) * 9 + (P(), P()),
        out_specs=(grid,) * 7,
        check_vma=False,
    )
```

```python
import functools

import jax
import jax.numpy as jnp
from jax import lax
from jax.experimental import pallas as pl
from jax.experimental.pallas import tpu as pltpu
from jax.sharding import PartitionSpec as P

BLOCK = 60
LEVELS = 8
NSUB = 4
ROWS = 120
COLS = 240
LANES = COLS * LEVELS
TILES = LANES // 128
RING = TILES + 1
PAD = 16
BAND = ROWS + 2 * PAD
MESH = pl.DeviceIdType.MESH
VMEM_BYTES = 56 * 1024 * 1024


def lanes_of(shape=(8, 128)):
    return lax.broadcasted_iota(jnp.int32, shape, 1)


def rows_of(shape=(8, 128)):
    return lax.broadcasted_iota(jnp.int32, shape, 0)


def lane_xor(tile, bit):
    keep = (lanes_of(tile.shape) // bit) % 2 == 0
    return jnp.where(keep, pltpu.roll(tile, 128 - bit, 1), pltpu.roll(tile, bit, 1))


def row_xor(tile, bit):
    keep = (rows_of(tile.shape) // bit) % 2 == 0
    return jnp.where(keep, pltpu.roll(tile, 8 - bit, 0), pltpu.roll(tile, bit, 0))


def turn_lanes(tile, bits):
    for bit in bits:
        tile = lane_xor(tile, bit)
    return tile


def turn_rows(tile):
    for bit in (1, 2, 4):
        tile = row_xor(tile, bit)
    return tile


class Neighbours:
    def __init__(self, nb, nw):
        b, x = lax.axis_index("blocks"), lax.axis_index("wide")
        self.b, self.x = b, x
        self.top, self.inner, self.above = x == nw - 1, x < nw - 1, x > 0
        self.east, self.west = lax.rem(b + 1, nb), lax.rem(b + nb - 1, nb)
        self.fold = nb - 1 - b
        self.fold_east = lax.rem(2 * nb - 2 - b, nb)
        self.fold_west = lax.rem(nb - b, nb)
        self.own_east = jnp.logical_and(self.top, self.fold_east == b)
        self.own_west = jnp.logical_and(self.top, self.fold_west == b)
        self.far_east = jnp.logical_and(self.top, self.fold_east != b)
        self.far_west = jnp.logical_and(self.top, self.fold_west != b)

    def greet(self):
        sem = pltpu.get_barrier_semaphore()

        def greet(b, x):
            pl.semaphore_signal(sem, inc=1, device_id=(b, x), device_id_type=MESH)

        b, x = self.b, self.x
        greet(self.east, x)
        greet(self.west, x)

        @pl.when(self.inner)
        def _():
            greet(b, x + 1)
            greet(self.east, x + 1)
            greet(self.west, x + 1)

        @pl.when(self.top)
        def _():
            greet(self.fold, x)

        @pl.when(self.far_east)
        def _():
            greet(self.fold_east, x)

        @pl.when(self.far_west)
        def _():
            greet(self.fold_west, x)

        @pl.when(self.above)
        def _():
            greet(b, x - 1)
            greet(self.east, x - 1)
            greet(self.west, x - 1)

    def meet(self):
        sem = pltpu.get_barrier_semaphore()
        x = self.x
        own = jnp.logical_or(self.own_east, self.own_west)

        @pl.when(x == 0)
        def _():
            pl.semaphore_wait(sem, 5)

        @pl.when(own)
        def _():
            pl.semaphore_wait(sem, 7)

        @pl.when(jnp.logical_and(self.above, jnp.logical_not(own)))
        def _():
            pl.semaphore_wait(sem, 8)

    def wire(self, north, south, east, west, rn, rs, rw, re, send, recv):
        b, x = self.b, self.x
        top_rows, low_rows = pl.ds(ROWS - 8, 8), pl.ds(0, 8)
        mid, lo, hi = pl.ds(8, ROWS), pl.ds(0, 8), pl.ds(ROWS + 8, 8)

        def c(src, dst, way, slot, to_b, to_x):
            return pltpu.make_async_remote_copy(
                src_ref=src, dst_ref=dst, send_sem=send.at[way], recv_sem=recv.at[slot],
                device_id=(to_b, to_x), device_id_type=MESH)

        return dict(
            always=[
                c(east, rw.at[mid], 0, 0, self.east, x),
                c(west, re.at[mid], 1, 1, self.west, x),
            ],
            inner=[
                c(north, rs, 2, 2, b, x + 1),
                c(east.at[top_rows], rw.at[lo], 4, 4, self.east, x + 1),
                c(west.at[top_rows], re.at[lo], 5, 5, self.west, x + 1),
            ],
            above=[
                c(south, rn, 3, 3, b, x - 1),
                c(east.at[low_rows], rw.at[hi], 6, 6, self.east, x - 1),
                c(west.at[low_rows], re.at[hi], 7, 7, self.west, x - 1),
            ],
            top=[c(north, rn, 2, 3, self.fold, x)],
            far_east=[c(east.at[top_rows], re.at[hi], 4, 7, self.fold_east, x)],
            far_west=[c(west.at[top_rows], rw.at[hi], 5, 6, self.fold_west, x)],
        )

    def start(self, wires, east, west, rw, re):
        def go(name, cond):
            @pl.when(cond)
            def _():
                for copy in wires[name]:
                    copy.start()

        go("inner", self.inner)
        go("top", self.top)
        go("above", self.above)
        go("far_east", self.far_east)
        go("far_west", self.far_west)
        for copy in wires["always"]:
            copy.start()

        @pl.when(self.own_east)
        def _():
            re[pl.ds(ROWS + 8, 8), :] = east[pl.ds(ROWS - 8, 8), :]

        @pl.when(self.own_west)
        def _():
            rw[pl.ds(ROWS + 8, 8), :] = west[pl.ds(ROWS - 8, 8), :]

    def finish(self, wires):
        w = wires
        for copy in w["always"]:
            copy.wait_recv()
            copy.wait_send()
        w["top"][0].wait_recv()

        @pl.when(self.above)
        def _():
            for copy in w["inner"]:
                copy.wait_recv()
            for copy in w["above"]:
                copy.wait_send()

        @pl.when(jnp.logical_not(self.own_east))
        def _():
            w["far_east"][0].wait_recv()
            w["far_east"][0].wait_send()

        @pl.when(jnp.logical_not(self.own_west))
        def _():
            w["far_west"][0].wait_recv()
            w["far_west"][0].wait_send()

        w["top"][0].wait_send()


def block_row(flags, row, tile):
    low, high = (128 * tile) // (BLOCK * LEVELS), (128 * tile + 127) // (BLOCK * LEVELS)
    value = jnp.full((8, 128), flags[row, low].astype(jnp.float32))
    if low != high:
        value = jnp.where(
            lanes_of() < BLOCK * LEVELS * high - 128 * tile,
            value,
            flags[row, high].astype(jnp.float32),
        )
    return value


def expand(tile, part):
    index = lanes_of() // LEVELS + 16 * part
    return jnp.take_along_axis(tile, index, axis=1, mode="promise_in_bounds")


def step_kernel(
    nb, nw, flags_in, ktab_in, btab_in, sel_in, t, s, u, v, zavg_in, mavg_in, elev_in,
    tn, sn, un, vn, du, dv, height, zonal, merid,
    flags, ktab, btab, sel, zavg, mavg, elev,
    edge_rows, edge_cols, npack, spack, wpack, epack, rn, rs, rw, re,
    field, once, part, wet, count, both, fade, mix,
    plane, wpack2, epack2, rn2, rs2, rw2, re2,
    small, load, send, recv, send2, recv2,
):
    sources = (t, s, u, v)
    results = (tn, sn, un, vn)
    near = Neighbours(nb, nw)
    near.greet()

    tables = [
        pltpu.make_async_copy(src, dst, small.at[i])
        for i, (src, dst) in enumerate(
            ((flags_in, flags), (ktab_in, ktab), (btab_in, btab), (sel_in, sel),
             (zavg_in, zavg), (mavg_in, mavg), (elev_in, elev)))
    ]
    edges = []
    for f, src in enumerate(sources):
        for side, at in enumerate((0, ROWS - 8)):
            edges.append(pltpu.make_async_copy(
                src.at[pl.ds(at, 8), :], edge_rows.at[f, side], small.at[8 + 4 * f + side]))
        for side, at in enumerate((0, LANES - 128)):
            edges.append(pltpu.make_async_copy(
                src.at[:, pl.ds(at, 128)], edge_cols.at[f, side], small.at[10 + 4 * f + side]))
    loads = [
        [
            pltpu.make_async_copy(
                src.at[:, pl.ds(128 * k, 128)], field.at[f, k, pl.ds(PAD, ROWS), :], load.at[f, k])
            for k in range(TILES)
        ]
        for f, src in enumerate(sources)
    ]
    tables[0].start()
    for copy in edges:
        copy.start()
    for copy in tables[1:]:
        copy.start()
    for f in (2, 3, 0, 1):
        for copy in loads[f]:
            copy.start()

    lane, sub = lanes_of(), rows_of()
    tables[0].wait()
    for copy in edges:
        copy.wait()
    for k in range(TILES):
        at = pl.ds(128 * k, 128)
        low, high = block_row(flags, 0, k), block_row(flags, 1, k)
        for f in range(4):
            spack[pl.ds(2 * f, 2), at] = (edge_rows[f, 0, :, at] * low)[0:2]
            npack[pl.ds(2 * f, 2), at] = (edge_rows[f, 1, :, at] * high)[6:8]
    for row, pack in ((0, spack), (1, npack)):
        tail = jnp.zeros((8, 128), jnp.float32)
        for j in range(4):
            tail = jnp.where(lane // 32 == j, flags[row, j].astype(jnp.float32), tail)
        pack[:, pl.ds(LANES, 128)] = tail
    lane_c, row_c = lanes_of((ROWS, 128)), rows_of((ROWS, 128))
    for side, col, pack in ((0, 0, wpack), (1, 3, epack)):
        w = jnp.where(row_c < BLOCK, flags[0, col].astype(jnp.float32), flags[1, col].astype(jnp.float32))
        packed = w
        for f in range(4):
            shift = (16 * f + (16 if side else 0)) % 128
            moved = pltpu.roll(edge_cols[f, side], shift, 1) if shift else edge_cols[f, side]
            packed = jnp.where(lane_c // 16 == f, moved * w, packed)
        pack[...] = packed
    near.meet()
    wires = near.wire(npack, spack, epack, wpack, rn, rs, rw, re, send, recv)
    near.start(wires, epack, wpack, rw, re)

    def fill(e, carry):
        base = pl.multiple_of(8 * e, 8)
        lower = sub + base < PAD + BLOCK
        for k in range(TILES):
            wet[k, pl.ds(base, 8), :] = jnp.where(lower, block_row(flags, 0, k), block_row(flags, 1, k))
        return carry

    lax.fori_loop(2, 2 + ROWS // 8, fill, 0)
    for copy in tables[1:]:
        copy.wait()
    for half, width in ((0, 128), (1, COLS - 128)):
        index = sel[:, 128 * half:128 * half + width]
        kappa = jnp.full(index.shape, ktab[0])
        bihar = jnp.full(index.shape, btab[0])
        for n in range(1, 8):
            kappa = jnp.where(index == n, ktab[n], kappa)
            bihar = jnp.where(index == n, btab[n], bihar)
        mix[0, half, PAD:PAD + ROWS, 0:width] = kappa
        mix[1, half, PAD:PAD + ROWS, 0:width] = bihar

    def around(ref, turned, key, k, base):
        here, above, below = pl.ds(base, 8), pl.ds(base + 1, 8), pl.ds(base - 1, 8)

        def ring(k):
            if (key, k) not in turned:
                tile = ref[k, here, :]
                turned[key, k] = (tile, pltpu.roll(tile, 128 - LEVELS, 1), pltpu.roll(tile, LEVELS, 1))
            return turned[key, k]

        tile, left, right = ring(k)
        east = jnp.where(lane < 128 - LEVELS, left, ring((k + 1) % RING)[1])
        west = jnp.where(lane < LEVELS, ring((k - 1) % RING)[2], right)
        return tile, east, west, ref[k, above, :], ref[k, below, :]

    def weigh(e, tiles):
        base = pl.multiple_of(8 * e, 8)
        here = pl.ds(base, 8)
        turned = {}
        for k in tiles:
            w, we, ww, wn, ws = around(wet, turned, "wet", k, base)
            total = w * ((we + ww) + (wn + ws))
            count[k, here, :] = total
            if k < TILES:
                kappa = expand(mix[0, k // 8, here, :], k % 8)
                bihar = expand(mix[1, k // 8, here, :], k % 8)
                both[k, here, :] = kappa + bihar * total
                fade[k, here, :] = bihar * w

    def mask(e, which):
        rows = pl.ds(pl.multiple_of(8 * e, 8), 8)
        for k in range(TILES):
            w = wet[k, rows, :]
            for f in which:
                field[f, k, rows, :] = field[f, k, rows, :] * w

    def first(e, tiles, which):
        base = pl.multiple_of(8 * e, 8)
        here = pl.ds(base, 8)
        turned = {}
        for k in tiles:
            w, total = wet[k, here, :], count[k, here, :]
            if k < TILES:
                mixing = both[k, here, :]
                zonal_own = 0.05 * field[2, k, here, :]
                merid_own = 0.05 * field[3, k, here, :]
            for f in which:
                c, fe, fw, fn, fs = around(field.at[f], turned, f, k, base)
                lap = w * ((fe + fw) + (fn + fs)) - total * c
                once[f, k, here, :] = lap
                if k < TILES:
                    part[f, k, here, :] = (
                        c - (zonal_own * (fe - fw) + merid_own * (fn - fs))) + mixing * lap

    def second(e, tiles, which):
        base = pl.multiple_of(8 * e, 8)
        here = pl.ds(base, 8)
        rows = pl.ds(pl.multiple_of(base - PAD, 8), 8)
        turned = {}
        for k in tiles:
            for f in which:
                _, le, lw, ln, ls = around(once.at[f], turned, f, k, base)
                results[f][rows, 128 * k:128 * k + 128] = (
                    part[f, k, here, :] - fade[k, here, :] * ((le + lw) + (ln + ls)))

    def each(low, high, *steps):
        def body(e, carry):
            for step in steps:
                step(e)
            return carry
        lax.fori_loop(low, high, body, 0)

    end = 2 + ROWS // 8
    flows, tracers = (2, 3), (0, 1)
    inside, everywhere, rim = range(TILES), range(RING), (0, TILES - 1, TILES)

    each(2, end, lambda e: weigh(e, inside))
    for f in flows:
        for copy in loads[f]:
            copy.wait()
    each(2, end, lambda e: mask(e, flows))
    each(2, end, lambda e: first(e, inside, flows))
    each(3, end - 1, lambda e: second(e, range(1, TILES - 1), flows))

    near.finish(wires)

    @pl.when(near.x == 0)
    def _():
        rs[...] = jnp.zeros(rs.shape, jnp.float32)
        rw[0:8, :] = jnp.zeros((8, 128), jnp.float32)
        re[0:8, :] = jnp.zeros((8, 128), jnp.float32)

    @pl.when(near.top)
    def _():
        sign = jnp.where(sub < 4, 1.0, -1.0)
        tiles = [rn[:, pl.ds(128 * (TILES - 1 - k), 128)] for k in range(TILES)]
        for k in range(TILES):
            rn[:, pl.ds(128 * k, 128)] = sign * row_xor(turn_lanes(tiles[k], (8, 16, 32, 64)), 1)
        rn[:, pl.ds(LANES, 128)] = turn_lanes(rn[:, pl.ds(LANES, 128)], (32, 64))
        flow = jnp.where(lane // 32 == 1, -1.0, 1.0)
        for got in (rw, re):
            tile = got[pl.ds(ROWS + 8, 8), :]
            got[pl.ds(ROWS + 8, 8), :] = flow * turn_rows(lane_xor(tile, 8))

    for k in range(TILES):
        low, high = (128 * k) // (BLOCK * LEVELS), (128 * k + 127) // (BLOCK * LEVELS)
        for got, base in ((rs, PAD - 8), (rn, PAD + ROWS)):
            tail = got[:, pl.ds(LANES, 128)]
            value = jnp.broadcast_to(tail[:, 32 * low:32 * low + 1], (8, 128))
            if low != high:
                value = jnp.where(lane < BLOCK * LEVELS * high - 128 * k, value,
                                  jnp.broadcast_to(tail[:, 32 * high:32 * high + 1], (8, 128)))
            wet[k, pl.ds(base, 8), :] = value
    lane_h = lanes_of((ROWS + 16, 128))
    ends = pl.ds(PAD - 8, ROWS + 16)
    west, east = rw[...], re[...]
    wet[TILES, ends, :] = jnp.where(lane_h < 64, pltpu.roll(east, 64, 1), west)
    for f in range(4):
        right = pltpu.roll(east, (128 - 16 * f) % 128, 1) if f else east
        field[f, TILES, ends, :] = jnp.where(lane_h < 64, right, pltpu.roll(west, 112 - 16 * f, 1))
        for k in range(TILES):
            field[f, k, PAD - 2:PAD, :] = rs[2 * f:2 * f + 2, 128 * k:128 * k + 128]
            field[f, k, PAD + ROWS:PAD + ROWS + 2, :] = rn[2 * f:2 * f + 2, 128 * k:128 * k + 128]

    def brink(i):
        return 1 + i + (end - 4) * (i // 2)

    each(0, 4, lambda i: weigh(brink(i), everywhere))
    each(3, end - 1, lambda e: weigh(e, rim))
    each(0, 4, lambda i: first(brink(i), everywhere, flows))
    each(3, end - 1, lambda e: first(e, rim, flows))
    each(0, 2, lambda i: second(2 + i * (end - 3), inside, flows))
    each(3, end - 1, lambda e: second(e, rim[:2], flows))

    span = 128 * LEVELS
    pick = jnp.where(
        lax.broadcasted_iota(jnp.int32, (span, 128), 0) // LEVELS
        == lax.broadcasted_iota(jnp.int32, (span, 128), 1),
        1.0 / LEVELS, 0.0).astype(jnp.bfloat16)

    def average(i, carry):
        rows = pl.ds(pl.multiple_of(40 * i, 8), 40)
        for new, mean in ((un, du), (vn, dv)):
            for half in range(2):
                width = span if half == 0 else LANES - span
                values = new[rows, span * half:span * half + width]
                coarse = values.astype(jnp.bfloat16)
                fine = (values - coarse.astype(jnp.float32)).astype(jnp.bfloat16)
                mean[rows, 128 * half:128 * half + 128] = (
                    jnp.dot(coarse, pick[:width], preferred_element_type=jnp.float32)
                    + jnp.dot(fine, pick[:width], preferred_element_type=jnp.float32))
        return carry

    lax.fori_loop(0, ROWS // 40, average, 0)

    shape = (ROWS, COLS)
    row, col = rows_of(shape), lanes_of(shape)
    w = jnp.zeros(shape, jnp.float32)
    for i in range(2):
        for j in range(4):
            here = jnp.logical_and(row // BLOCK == i, col // BLOCK == j)
            w = jnp.where(here, flags[i, j].astype(jnp.float32), w)
    plane[:, :, 128:256] = jnp.zeros((4, ROWS + 16, 128), jnp.float32)
    plane[0, 0:ROWS, 0:COLS] = w * (zavg[...] + du[:, 0:COLS])
    plane[1, 0:ROWS, 0:COLS] = w * (mavg[...] + dv[:, 0:COLS])
    plane[2, 0:ROWS, 0:COLS] = w * elev[...]
    plane[3, 0:ROWS, 0:COLS] = w
    right = jnp.zeros((ROWS, 128), jnp.float32)
    left = jnp.zeros((ROWS, 128), jnp.float32)
    for p in range(4):
        right = jnp.where(lane_c // 8 == p, pltpu.roll(plane[p, 0:ROWS, 128:256], 8 * p + 24, 1), right)
        begin = plane[p, 0:ROWS, 0:128]
        left = jnp.where(lane_c // 8 == p, pltpu.roll(begin, 8 * p, 1) if p else begin, left)
    epack2[...] = right
    wpack2[...] = left
    north, south = plane.at[:, pl.ds(ROWS - 8, 8), :], plane.at[:, pl.ds(0, 8), :]
    wires2 = near.wire(north, south, epack2, wpack2, rn2, rs2, rw2, re2, send2, recv2)
    near.start(wires2, epack2, wpack2, rw2, re2)

    for f in tracers:
        for copy in loads[f]:
            copy.wait()
    each(2, end, lambda e: mask(e, tracers))
    each(1, end + 1, lambda e: first(e, everywhere, tracers))
    each(2, end, lambda e: second(e, inside, tracers))

    near.finish(wires2)

    @pl.when(near.x == 0)
    def _():
        rs2[...] = jnp.zeros(rs2.shape, jnp.float32)
        rw2[0:8, :] = jnp.zeros((8, 128), jnp.float32)
        re2[0:8, :] = jnp.zeros((8, 128), jnp.float32)

    @pl.when(near.top)
    def _():
        reverse = (1, 2, 4, 8, 16, 32, 64)
        for p in range(4):
            sign = -1.0 if p < 2 else 1.0
            start = sign * turn_rows(turn_lanes(rn2[p, :, 128:256], reverse))
            last = sign * turn_rows(turn_lanes(rn2[p, :, 0:128], reverse))
            rn2[p] = pltpu.roll(jnp.concatenate([start, last], axis=1), COLS, 1)
        flow = jnp.where(lane < 16, -1.0, 1.0)
        for got in (rw2, re2):
            tile = got[pl.ds(ROWS + 8, 8), :]
            got[pl.ds(ROWS + 8, 8), :] = flow * turn_rows(turn_lanes(tile, (1, 2, 4)))

    plane[:, ROWS:ROWS + 8, :] = rn2[...]
    plane[:, ROWS + 8:ROWS + 16, :] = rs2[...]
    for to, at, number in ((0, 8, ROWS), (ROWS, ROWS + 8, 8), (ROWS + 8, 0, 8)):
        lane_p = lanes_of((number, 128))
        west, east = rw2[at:at + number, :], re2[at:at + number, :]
        for p in range(4):
            halo = jnp.where(lane_p < 120, pltpu.roll(east, 112 - 8 * p, 1), pltpu.roll(west, 120 - 8 * p, 1))
            plane[p, to:to + number, 128:256] = jnp.where(
                lane_p < 112, plane[p, to:to + number, 128:256], halo)

    zt, mt, h, w = plane[0], plane[1], plane[2], plane[3]
    across, along = 256, ROWS + 16
    for _ in range(NSUB):
        spread = (pltpu.roll(zt, across - 1, 1) - pltpu.roll(zt, 1, 1)) + (
            pltpu.roll(mt, along - 1, 0) - pltpu.roll(mt, 1, 0))
        h = h - 0.3 * w * spread
        zt = w * (zt - 0.3 * (pltpu.roll(h, across - 1, 1) - pltpu.roll(h, 1, 1)))
        mt = w * (mt - 0.3 * (pltpu.roll(h, along - 1, 0) - pltpu.roll(h, 1, 0)))
    zt, mt = zt[0:ROWS], mt[0:ROWS]
    du[...] = zt - du[...]
    dv[...] = mt - dv[...]
    height[...] = h[0:ROWS, 0:COLS]
    zonal[...] = zt[:, 0:COLS]
    merid[...] = mt[:, 0:COLS]


def finish_kernel(
    tn, sn, un, vn, du, dv, height, zonal, merid,
    t_out, s_out, u_out, v_out, height_out, zonal_out, merid_out, done, sems,
):
    copies = [
        pltpu.make_async_copy(src, dst, sems.at[i])
        for i, (src, dst) in enumerate(
            ((tn, t_out), (sn, s_out), (height, height_out), (zonal, zonal_out), (merid, merid_out)))
    ]
    for copy in copies:
        copy.start()
    step = 24
    for i in range(ROWS // step):
        for f, (new, change, out) in enumerate(((un, du, u_out), (vn, dv, v_out))):
            for r in range(step * i, step * i + step, 8):
                for half in range(2):
                    tile = change[r:r + 8, 128 * half:128 * half + 128]
                    for k in range(8 * half, min(8 * half + 8, TILES)):
                        at = slice(128 * k, 128 * k + 128)
                        done[f, r:r + 8, at] = new[r:r + 8, at] + expand(tile, k % 8)
            rows = pl.ds(step * i, step)
            copies.append(pltpu.make_async_copy(done.at[f, rows, :], out.at[rows, :], sems.at[5 + 2 * i + f]))
            copies[-1].start()
    for copy in copies:
        copy.wait()


def per_device(nb, nw, t, s, u, v, elev, zavg, mavg, flags, sel, ktab, btab):
    f32 = jnp.float32
    vmem = pl.BlockSpec(memory_space=pltpu.VMEM)
    hbm = pl.BlockSpec(memory_space=pl.ANY)
    scratch = lambda *shape: pltpu.VMEM(shape, f32)
    dma = lambda *shape: pltpu.SemaphoreType.DMA(shape)
    parts = pl.pallas_call(
        functools.partial(step_kernel, nb, nw),
        out_shape=(pltpu.VMEM((ROWS, LANES), f32),) * 4
        + (pltpu.VMEM((ROWS, 256), f32),) * 2
        + (pltpu.VMEM((ROWS, COLS), f32),) * 3,
        in_specs=[hbm] * 11,
        out_specs=(vmem,) * 9,
        scratch_shapes=[
            pltpu.SMEM((2, 4), jnp.int32),
            pltpu.SMEM((8,), f32),
            pltpu.SMEM((8,), f32),
            pltpu.VMEM((ROWS, COLS), jnp.int32),
            scratch(ROWS, COLS), scratch(ROWS, COLS), scratch(ROWS, COLS),
            scratch(4, 2, 8, LANES), scratch(4, 2, ROWS, 128),
            scratch(8, LANES + 128), scratch(8, LANES + 128), scratch(ROWS, 128), scratch(ROWS, 128),
            scratch(8, LANES + 128), scratch(8, LANES + 128), scratch(ROWS + 16, 128), scratch(ROWS + 16, 128),
            scratch(4, RING, BAND, 128), scratch(4, RING, BAND, 128), scratch(4, TILES, BAND, 128),
            scratch(RING, BAND, 128), scratch(RING, BAND, 128),
            scratch(TILES, BAND, 128), scratch(TILES, BAND, 128), scratch(2, 2, BAND, 128),
            scratch(4, ROWS + 16, 256), scratch(ROWS, 128), scratch(ROWS, 128),
            scratch(4, 8, 256), scratch(4, 8, 256), scratch(ROWS + 16, 128), scratch(ROWS + 16, 128),
            dma(24), dma(4, TILES), dma(8), dma(8), dma(8), dma(8),
        ],
        compiler_params=pltpu.CompilerParams(
            collective_id=0, has_side_effects=True, vmem_limit_bytes=VMEM_BYTES),
        name="step",
    )(flags, ktab, btab, sel, t, s, u, v, zavg, mavg, elev)
    parts = [pltpu.with_memory_space_constraint(part, pltpu.VMEM) for part in parts]

    big = jax.ShapeDtypeStruct((ROWS, LANES), f32)
    flat = jax.ShapeDtypeStruct((ROWS, COLS), f32)
    return pl.pallas_call(
        finish_kernel,
        out_shape=(big,) * 4 + (flat,) * 3,
        in_specs=[vmem] * 9,
        out_specs=(hbm,) * 7,
        scratch_shapes=[scratch(2, ROWS, LANES), dma(15)],
        compiler_params=pltpu.CompilerParams(vmem_limit_bytes=VMEM_BYTES),
        name="finish",
    )(*parts)


def solution(mesh):
    grid = P("wide", "blocks")
    return jax.shard_map(
        functools.partial(per_device, mesh.shape["blocks"], mesh.shape["wide"]),
        mesh=mesh,
        in_specs=(grid,) * 9 + (P(), P()),
        out_specs=(grid,) * 7,
        check_vma=False,
    )
```

```python
import functools

import jax
import jax.numpy as jnp
from jax import lax
from jax.experimental import pallas as pl
from jax.experimental.pallas import tpu as pltpu
from jax.sharding import PartitionSpec as P

BLOCK = 60
LEVELS = 8
NSUB = 4
ROWS = 120
COLS = 240
LANES = COLS * LEVELS
TILES = LANES // 128
RING = TILES + 1
PAD = 16
BAND = ROWS + 2 * PAD
MESH = pl.DeviceIdType.MESH
VMEM_BYTES = 56 * 1024 * 1024


def lanes_of(shape=(8, 128)):
    return lax.broadcasted_iota(jnp.int32, shape, 1)


def rows_of(shape=(8, 128)):
    return lax.broadcasted_iota(jnp.int32, shape, 0)


def lane_xor(tile, bit):
    keep = (lanes_of(tile.shape) // bit) % 2 == 0
    return jnp.where(keep, pltpu.roll(tile, 128 - bit, 1), pltpu.roll(tile, bit, 1))


def row_xor(tile, bit):
    keep = (rows_of(tile.shape) // bit) % 2 == 0
    return jnp.where(keep, pltpu.roll(tile, 8 - bit, 0), pltpu.roll(tile, bit, 0))


def turn_lanes(tile, bits):
    for bit in bits:
        tile = lane_xor(tile, bit)
    return tile


def turn_rows(tile):
    for bit in (1, 2, 4):
        tile = row_xor(tile, bit)
    return tile


class Neighbours:
    def __init__(self, nb, nw):
        b, x = lax.axis_index("blocks"), lax.axis_index("wide")
        self.b, self.x = b, x
        self.top, self.inner, self.above = x == nw - 1, x < nw - 1, x > 0
        self.east, self.west = lax.rem(b + 1, nb), lax.rem(b + nb - 1, nb)
        self.fold = nb - 1 - b
        self.fold_east = lax.rem(2 * nb - 2 - b, nb)
        self.fold_west = lax.rem(nb - b, nb)
        self.own_east = jnp.logical_and(self.top, self.fold_east == b)
        self.own_west = jnp.logical_and(self.top, self.fold_west == b)
        self.far_east = jnp.logical_and(self.top, self.fold_east != b)
        self.far_west = jnp.logical_and(self.top, self.fold_west != b)

    def greet(self):
        sem = pltpu.get_barrier_semaphore()

        def greet(b, x):
            pl.semaphore_signal(sem, inc=1, device_id=(b, x), device_id_type=MESH)

        b, x = self.b, self.x
        greet(self.east, x)
        greet(self.west, x)

        @pl.when(self.inner)
        def _():
            greet(b, x + 1)
            greet(self.east, x + 1)
            greet(self.west, x + 1)

        @pl.when(self.top)
        def _():
            greet(self.fold, x)

        @pl.when(self.far_east)
        def _():
            greet(self.fold_east, x)

        @pl.when(self.far_west)
        def _():
            greet(self.fold_west, x)

        @pl.when(self.above)
        def _():
            greet(b, x - 1)
            greet(self.east, x - 1)
            greet(self.west, x - 1)

    def meet(self):
        sem = pltpu.get_barrier_semaphore()
        x = self.x
        own = jnp.logical_or(self.own_east, self.own_west)

        @pl.when(x == 0)
        def _():
            pl.semaphore_wait(sem, 5)

        @pl.when(own)
        def _():
            pl.semaphore_wait(sem, 7)

        @pl.when(jnp.logical_and(self.above, jnp.logical_not(own)))
        def _():
            pl.semaphore_wait(sem, 8)

    def wire(self, north, south, east, west, rn, rs, rw, re, send, recv):
        b, x = self.b, self.x
        top_rows, low_rows = pl.ds(ROWS - 8, 8), pl.ds(0, 8)
        mid, lo, hi = pl.ds(8, ROWS), pl.ds(0, 8), pl.ds(ROWS + 8, 8)

        def c(src, dst, way, slot, to_b, to_x):
            return pltpu.make_async_remote_copy(
                src_ref=src, dst_ref=dst, send_sem=send.at[way], recv_sem=recv.at[slot],
                device_id=(to_b, to_x), device_id_type=MESH)

        return dict(
            always=[
                c(east, rw.at[mid], 0, 0, self.east, x),
                c(west, re.at[mid], 1, 1, self.west, x),
            ],
            inner=[
                c(north, rs, 2, 2, b, x + 1),
                c(east.at[top_rows], rw.at[lo], 4, 4, self.east, x + 1),
                c(west.at[top_rows], re.at[lo], 5, 5, self.west, x + 1),
            ],
            above=[
                c(south, rn, 3, 3, b, x - 1),
                c(east.at[low_rows], rw.at[hi], 6, 6, self.east, x - 1),
                c(west.at[low_rows], re.at[hi], 7, 7, self.west, x - 1),
            ],
            top=[c(north, rn, 2, 3, self.fold, x)],
            far_east=[c(east.at[top_rows], re.at[hi], 4, 7, self.fold_east, x)],
            far_west=[c(west.at[top_rows], rw.at[hi], 5, 6, self.fold_west, x)],
        )

    def start(self, wires, east, west, rw, re):
        def go(name, cond):
            @pl.when(cond)
            def _():
                for copy in wires[name]:
                    copy.start()

        go("inner", self.inner)
        go("top", self.top)
        go("above", self.above)
        go("far_east", self.far_east)
        go("far_west", self.far_west)
        for copy in wires["always"]:
            copy.start()

        @pl.when(self.own_east)
        def _():
            re[pl.ds(ROWS + 8, 8), :] = east[pl.ds(ROWS - 8, 8), :]

        @pl.when(self.own_west)
        def _():
            rw[pl.ds(ROWS + 8, 8), :] = west[pl.ds(ROWS - 8, 8), :]

    def finish(self, wires):
        w = wires
        for copy in w["always"]:
            copy.wait_recv()
            copy.wait_send()
        w["top"][0].wait_recv()

        @pl.when(self.above)
        def _():
            for copy in w["inner"]:
                copy.wait_recv()
            for copy in w["above"]:
                copy.wait_send()

        @pl.when(jnp.logical_not(self.own_east))
        def _():
            w["far_east"][0].wait_recv()
            w["far_east"][0].wait_send()

        @pl.when(jnp.logical_not(self.own_west))
        def _():
            w["far_west"][0].wait_recv()
            w["far_west"][0].wait_send()

        w["top"][0].wait_send()


def block_row(flags, row, tile):
    low, high = (128 * tile) // (BLOCK * LEVELS), (128 * tile + 127) // (BLOCK * LEVELS)
    value = jnp.full((8, 128), flags[row, low].astype(jnp.float32))
    if low != high:
        value = jnp.where(
            lanes_of() < BLOCK * LEVELS * high - 128 * tile,
            value,
            flags[row, high].astype(jnp.float32),
        )
    return value


def expand(tile, part):
    index = lanes_of() // LEVELS + 16 * part
    return jnp.take_along_axis(tile, index, axis=1, mode="promise_in_bounds")


def step_kernel(
    nb, nw, flags_in, ktab_in, btab_in, sel_in, t, s, u, v, zavg_in, mavg_in, elev_in,
    tn, sn, un, vn, du, dv, height, zonal, merid,
    flags, ktab, btab, sel, zavg, mavg, elev,
    raw, npack, spack, wpack, epack, rn, rs, rw, re,
    field, once, part, wet, count, wide_k, wide_b, mix, pick, mean,
    plane, wpack2, epack2, rn2, rs2, rw2, re2,
    small, load, send, recv, send2, recv2,
):
    sources = (t, s, u, v)
    results = (tn, sn, un, vn)
    near = Neighbours(nb, nw)
    near.greet()

    tables = [
        pltpu.make_async_copy(src, dst, small.at[i])
        for i, (src, dst) in enumerate(
            ((flags_in, flags), (ktab_in, ktab), (btab_in, btab), (sel_in, sel),
             (zavg_in, zavg), (mavg_in, mavg), (elev_in, elev)))
    ]
    loads = [pltpu.make_async_copy(src, raw.at[f], load.at[f]) for f, src in enumerate(sources)]
    tables[0].start()
    for copy in loads:
        copy.start()
    for copy in tables[1:]:
        copy.start()

    lane, sub = lanes_of(), rows_of()
    end = 2 + ROWS // 8
    middle = 2 + BLOCK // 8
    split = BLOCK % 8
    early, late = range(2, middle), range(middle + 1, end)
    flows, tracers = (2, 3), (0, 1)
    inside, everywhere, rim = range(TILES), range(RING), (0, TILES - 1, TILES)

    tables[0].wait()
    lows = [block_row(flags, 0, k) for k in inside] + [jnp.zeros((8, 128), jnp.float32)]
    highs = [block_row(flags, 1, k) for k in inside] + [jnp.zeros((8, 128), jnp.float32)]

    def beside(tiles, k):
        left = pltpu.roll(tiles[k], 128 - LEVELS, 1)
        next_left = pltpu.roll(tiles[(k + 1) % RING], 128 - LEVELS, 1)
        right = pltpu.roll(tiles[k], LEVELS, 1)
        last_right = pltpu.roll(tiles[(k - 1) % RING], LEVELS, 1)
        return jnp.where(lane < 128 - LEVELS, left, next_left) + jnp.where(lane < LEVELS, last_right, right)

    for k in inside:
        low, high = lows[k], highs[k]
        side_low, side_high = beside(lows, k), beside(highs, k)
        count_low, count_high = low * (side_low + (low + low)), high * (side_high + (high + high))
        mixed = jnp.where(sub < split, low, high)
        north = jnp.where(sub < split - 1, low, high)
        south = jnp.where(sub < split + 1, low, high)
        for e in early:
            wet[k, 8 * e:8 * e + 8, :] = low
            count[k, 8 * e:8 * e + 8, :] = count_low
        for e in late:
            wet[k, 8 * e:8 * e + 8, :] = high
            count[k, 8 * e:8 * e + 8, :] = count_high
        wet[k, 8 * middle:8 * middle + 8, :] = mixed
        count[k, 8 * middle:8 * middle + 8, :] = mixed * (
            jnp.where(sub < split, side_low, side_high) + (north + south))

    for copy in loads:
        copy.wait()
    for k in inside:
        at = slice(128 * k, 128 * k + 128)
        south, north = jnp.zeros((8, 128), jnp.float32), jnp.zeros((8, 128), jnp.float32)
        for f in range(4):
            below, above = raw[f, 0:8, at], raw[f, ROWS - 8:ROWS, at]
            south = jnp.where(sub // 2 == f, pltpu.roll(below, 2 * f, 0) if f else below, south)
            north = jnp.where(sub // 2 == f, pltpu.roll(above, 2 * f + 2, 0) if f < 3 else above, north)
        spack[k] = south * lows[k]
        npack[k] = north * highs[k]
    for row, pack in ((0, spack), (1, npack)):
        tail = jnp.zeros((8, 128), jnp.float32)
        for j in range(4):
            tail = jnp.where(lane // 32 == j, flags[row, j].astype(jnp.float32), tail)
        pack[TILES] = tail
    lane_c, row_c = lanes_of((ROWS, 128)), rows_of((ROWS, 128))
    for side, col, pack in ((0, 0, wpack), (1, 3, epack)):
        w = jnp.where(row_c < BLOCK, flags[0, col].astype(jnp.float32), flags[1, col].astype(jnp.float32))
        packed = jnp.ones((ROWS, 128), jnp.float32)
        for f in range(4):
            shift = (16 * f + (16 if side else 0)) % 128
            tile = raw[f, :, (LANES - 128) * side:(LANES - 128) * side + 128]
            packed = jnp.where(lane_c // 16 == f, pltpu.roll(tile, shift, 1) if shift else tile, packed)
        pack[...] = packed * w
    near.meet()
    into = pl.ds(8, 8)
    wires = near.wire(
        npack, spack, epack, wpack, rn.at[:, into, :], rs.at[:, into, :], rw, re, send, recv)
    near.start(wires, epack, wpack, rw, re)

    for copy in tables[1:]:
        copy.wait()
    for half, width in ((0, 128), (1, COLS - 128)):
        for r in range(0, ROWS, 40):
            index = sel[r:r + 40, 128 * half:128 * half + width]
            kappa = jnp.full(index.shape, ktab[0])
            bihar = jnp.full(index.shape, btab[0])
            for n in range(1, 8):
                hit = index == n
                kappa = jnp.where(hit, ktab[n], kappa)
                bihar = jnp.where(hit, btab[n], bihar)
            mix[0, half, PAD + r:PAD + r + 40, 0:width] = kappa
            mix[1, half, PAD + r:PAD + r + 40, 0:width] = bihar

    own = pl.ds(PAD, ROWS)
    for half, width in ((0, 128), (1, COLS - 128)):
        w = jnp.zeros((ROWS, 128), jnp.float32)
        for i in range(2):
            for j in range(4):
                here = jnp.logical_and(row_c // BLOCK == i, (lane_c + 128 * half) // BLOCK == j)
                w = jnp.where(here, flags[i, j].astype(jnp.float32), w)
        if width < 128:
            for p in range(3):
                plane[p, half, own, :] = jnp.zeros((ROWS, 128), jnp.float32)
        plane[3, half, own, :] = w
        at = slice(128 * half, 128 * half + width)
        for p, ref in ((0, zavg), (1, mavg), (2, elev)):
            plane[p, half, own, 0:width] = w[:, 0:width] * ref[:, at]

    def pack_planes(which, right, left):
        for p in which:
            right = jnp.where(lane_c // 8 == p, pltpu.roll(plane[p, 1, own, :], 8 * p + 24, 1), right)
            begin = plane[p, 0, own, :]
            left = jnp.where(lane_c // 8 == p, pltpu.roll(begin, 8 * p, 1) if p else begin, left)
        epack2[...] = right
        wpack2[...] = left

    pack_planes((2, 3), jnp.zeros((ROWS, 128), jnp.float32), jnp.zeros((ROWS, 128), jnp.float32))
    span = 128 * LEVELS
    pick[...] = jnp.where(
        lax.broadcasted_iota(jnp.int32, (span, 128), 0) // LEVELS
        == lax.broadcasted_iota(jnp.int32, (span, 128), 1),
        1.0 / LEVELS, 0.0).astype(jnp.bfloat16)

    def around(ref, turned, key, k, base):
        here, above, below = pl.ds(base, 8), pl.ds(base + 1, 8), pl.ds(base - 1, 8)

        def ring(k):
            if (key, k) not in turned:
                tile = ref[k, here, :]
                turned[key, k] = (tile, pltpu.roll(tile, 128 - LEVELS, 1), pltpu.roll(tile, LEVELS, 1))
            return turned[key, k]

        tile, left, right = ring(k)
        east = jnp.where(lane < 128 - LEVELS, left, ring((k + 1) % RING)[1])
        west = jnp.where(lane < LEVELS, ring((k - 1) % RING)[2], right)
        return tile, east, west, ref[k, above, :], ref[k, below, :]

    def at_tile(e):
        return 8 * e if isinstance(e, int) else pl.multiple_of(8 * e, 8)

    def weigh(e, tiles, same):
        base = at_tile(e)
        turned = {}
        for k in tiles:
            w, we, ww, wn, ws = around(wet, turned, "wet", k, base)
            total = w * ((we + ww) + (wn + ws))
            for to in same:
                count[k, 8 * to:8 * to + 8, :] = total

    def mask(e, which):
        base = at_tile(e)
        rows, here = pl.ds(base - PAD, 8), pl.ds(base, 8)
        for k in inside:
            w = wet[k, here, :]
            for f in which:
                field[f, k, here, :] = raw[f, rows, 128 * k:128 * k + 128] * w

    def first(e, tiles, which, fresh=False, whole=True):
        base = at_tile(e)
        here = pl.ds(base, 8)
        turned = {}
        for k in tiles:
            w, total = wet[k, here, :], count[k, here, :]
            full = whole and k < TILES
            if full:
                if fresh:
                    kappa = expand(mix[0, k // 8, here, :], k % 8)
                    bihar = expand(mix[1, k // 8, here, :], k % 8)
                    wide_k[k, here, :] = kappa
                    wide_b[k, here, :] = bihar
                else:
                    kappa, bihar = wide_k[k, here, :], wide_b[k, here, :]
                mixing = kappa + bihar * total
                zonal_own = 0.05 * field[2, k, here, :]
                merid_own = 0.05 * field[3, k, here, :]
            for f in which:
                c, fe, fw, fn, fs = around(field.at[f], turned, f, k, base)
                lap = w * ((fe + fw) + (fn + fs)) - total * c
                once[f, k, here, :] = lap
                if full:
                    part[f, k, here, :] = (
                        c - (zonal_own * (fe - fw) + merid_own * (fn - fs))) + mixing * lap

    def second(e, tiles, which):
        base = at_tile(e)
        here, rows = pl.ds(base, 8), pl.ds(base - PAD, 8)
        turned = {}
        for k in tiles:
            fade = wide_b[k, here, :] * wet[k, here, :]
            for f in which:
                _, le, lw, ln, ls = around(once.at[f], turned, f, k, base)
                results[f][rows, 128 * k:128 * k + 128] = (
                    part[f, k, here, :] - fade * ((le + lw) + (ln + ls)))

    def by_three(low, high, step):
        def body(i, carry):
            for j in range(3):
                step(low + 3 * i + j)
            return carry
        lax.fori_loop(0, (high - low) // 3, body, 0)

    by_three(2, end, lambda e: mask(e, flows))
    by_three(2, end, lambda e: first(e, inside, flows, fresh=True))
    by_three(3, end - 2, lambda e: second(e, range(1, TILES - 1), flows))
    second(end - 2, range(1, TILES - 1), flows)

    near.finish(wires)

    @pl.when(near.x == 0)
    def _():
        rs[:, 8:16, :] = jnp.zeros((RING, 8, 128), jnp.float32)
        rw[0:8, :] = jnp.zeros((8, 128), jnp.float32)
        re[0:8, :] = jnp.zeros((8, 128), jnp.float32)

    @pl.when(near.top)
    def _():
        sign = jnp.where(sub < 4, 1.0, -1.0)
        tiles = [rn[TILES - 1 - k, 8:16, :] for k in inside]
        for k in inside:
            rn[k, 8:16, :] = sign * row_xor(turn_lanes(tiles[k], (8, 16, 32, 64)), 1)
        rn[TILES, 8:16, :] = turn_lanes(rn[TILES, 8:16, :], (32, 64))
        flow = jnp.where(lane // 32 == 1, -1.0, 1.0)
        for got in (rw, re):
            tile = got[ROWS + 8:ROWS + 16, :]
            got[ROWS + 8:ROWS + 16, :] = flow * turn_rows(lane_xor(tile, 8))

    for got, base in ((rs, PAD - 8), (rn, PAD + ROWS)):
        tail = got[TILES, 8:16, :]
        flag = [jnp.broadcast_to(tail[:, 32 * j:32 * j + 1], (8, 128)) for j in range(4)]
        for k in inside:
            low, high = (128 * k) // (BLOCK * LEVELS), (128 * k + 127) // (BLOCK * LEVELS)
            value = flag[low]
            if low != high:
                value = jnp.where(lane < BLOCK * LEVELS * high - 128 * k, value, flag[high])
            wet[k, base:base + 8, :] = value
    lane_h = lanes_of((ROWS + 16, 128))
    ends = slice(PAD - 8, PAD + ROWS + 8)
    west, east = rw[...], re[...]
    wet[TILES, ends, :] = jnp.where(lane_h < 64, pltpu.roll(east, 64, 1), west)

    def halo(which):
        west, east = rw[...], re[...]
        for f in which:
            right = pltpu.roll(east, (128 - 16 * f) % 128, 1) if f else east
            field[f, TILES, ends, :] = jnp.where(lane_h < 64, right, pltpu.roll(west, 112 - 16 * f, 1))
            for k in inside:
                field[f, k, PAD - 8:PAD, :] = rs[k, 2 * f + 2:2 * f + 10, :]
                field[f, k, PAD + ROWS:PAD + ROWS + 8, :] = rn[k, 2 * f + 8:2 * f + 16, :]

    halo(flows)

    for e in (1, 2, end - 1, end):
        weigh(e, everywhere, (e,))
    weigh(3, rim, early[1:])
    weigh(middle, rim, (middle,))
    weigh(middle + 1, rim, late[:-1])
    for e in (1, 2, end - 1, end):
        first(e, everywhere, flows, whole=1 < e < end)
    for e in range(3, end - 1):
        first(e, rim, flows)
    for e in (2, end - 1):
        second(e, inside, flows)
    for e in range(3, end - 1):
        second(e, rim[:2], flows)

    for half in range(2):
        width = span if half == 0 else LANES - span
        pieces = []
        for new in (un, vn):
            values = new[:, span * half:span * half + width]
            coarse = values.astype(jnp.bfloat16)
            pieces += [coarse, (values - coarse.astype(jnp.float32)).astype(jnp.bfloat16)]
        means = jnp.dot(
            jnp.concatenate(pieces, axis=0), pick[0:width, :], preferred_element_type=jnp.float32)
        for f in range(2):
            value = means[256 * f:256 * f + ROWS] + means[256 * f + 128:256 * f + 128 + ROWS]
            mean[f, half] = value
            plane[f, half, own, :] = plane[f, half, own, :] + value

    pack_planes((0, 1), epack2[...], wpack2[...])
    north = plane.at[:, :, pl.ds(PAD + ROWS - 8, 8), :]
    south = plane.at[:, :, pl.ds(PAD, 8), :]
    wires2 = near.wire(north, south, epack2, wpack2, rn2, rs2, rw2, re2, send2, recv2)
    near.start(wires2, epack2, wpack2, rw2, re2)

    halo(tracers)
    by_three(2, end, lambda e: mask(e, tracers))
    for e in (1, end):
        first(e, everywhere, tracers, whole=False)
    by_three(2, end, lambda e: first(e, everywhere, tracers))
    by_three(2, end, lambda e: second(e, inside, tracers))

    near.finish(wires2)

    @pl.when(near.x == 0)
    def _():
        rs2[...] = jnp.zeros(rs2.shape, jnp.float32)
        rw2[0:8, :] = jnp.zeros((8, 128), jnp.float32)
        re2[0:8, :] = jnp.zeros((8, 128), jnp.float32)

    @pl.when(near.top)
    def _():
        reverse = (1, 2, 4, 8, 16, 32, 64)
        for p in range(4):
            sign = -1.0 if p < 2 else 1.0
            start = sign * turn_rows(turn_lanes(rn2[p, 1], reverse))
            last = sign * turn_rows(turn_lanes(rn2[p, 0], reverse))
            start, last = pltpu.roll(start, 112, 1), pltpu.roll(last, 112, 1)
            rn2[p, 0] = jnp.where(lane < 112, start, last)
            rn2[p, 1] = jnp.where(lane < 112, last, start)
        flow = jnp.where(lane < 16, -1.0, 1.0)
        for got in (rw2, re2):
            tile = got[ROWS + 8:ROWS + 16, :]
            got[ROWS + 8:ROWS + 16, :] = flow * turn_rows(turn_lanes(tile, (1, 2, 4)))

    for p in range(4):
        for half in range(2):
            plane[p, half, PAD - 8:PAD, :] = rs2[p, half]
            plane[p, half, PAD + ROWS:PAD + ROWS + 8, :] = rn2[p, half]
    west, east = rw2[...], re2[...]
    for p in range(4):
        beyond = jnp.where(lane_h < 120, pltpu.roll(east, 112 - 8 * p, 1), pltpu.roll(west, 120 - 8 * p, 1))
        plane[p, 1, ends, :] = jnp.where(lane_h < 112, plane[p, 1, ends, :], beyond)

    def pair(p, e):
        tiles = [plane[p, half, 8 * e:8 * e + 8, :] for half in range(2)]
        left = [pltpu.roll(tile, 127, 1) for tile in tiles]
        right = [pltpu.roll(tile, 1, 1) for tile in tiles]
        return tiles, [
            jnp.where(lane < 127, left[half], left[1 - half]) - jnp.where(lane < 1, right[1 - half], right[half])
            for half in range(2)
        ]

    def rows_apart(p, half, e):
        return plane[p, half, 8 * e + 1:8 * e + 9, :] - plane[p, half, 8 * e - 1:8 * e + 7, :]

    for _ in range(NSUB):
        for e in range(1, end + 1):
            _, across = pair(0, e)
            for half in range(2):
                here = (half, slice(8 * e, 8 * e + 8), slice(None))
                spread = across[half] + rows_apart(1, half, e)
                plane[(2,) + here] = plane[(2,) + here] - 0.3 * plane[(3,) + here] * spread
        for e in range(1, end + 1):
            _, across = pair(2, e)
            for half in range(2):
                here = (half, slice(8 * e, 8 * e + 8), slice(None))
                w = plane[(3,) + here]
                plane[(0,) + here] = w * (plane[(0,) + here] - 0.3 * across[half])
                plane[(1,) + here] = w * (plane[(1,) + here] - 0.3 * rows_apart(2, half, e))
    for half, width in ((0, 128), (1, COLS - 128)):
        at = slice(128 * half, 128 * half + 128)
        du[:, at] = plane[0, half, own, :] - mean[0, half]
        dv[:, at] = plane[1, half, own, :] - mean[1, half]
        at = slice(128 * half, 128 * half + width)
        for p, ref in ((0, zonal), (1, merid), (2, height)):
            ref[:, at] = plane[p, half, own, 0:width]


def finish_kernel(
    tn, sn, un, vn, du, dv, height, zonal, merid,
    t_out, s_out, u_out, v_out, height_out, zonal_out, merid_out, done, sems,
):
    copies = [
        pltpu.make_async_copy(src, dst, sems.at[i])
        for i, (src, dst) in enumerate(
            ((tn, t_out), (sn, s_out), (height, height_out), (zonal, zonal_out), (merid, merid_out)))
    ]
    for copy in copies:
        copy.start()
    step = 24
    for i in range(ROWS // step):
        for f, (new, change, out) in enumerate(((un, du, u_out), (vn, dv, v_out))):
            for r in range(step * i, step * i + step, 8):
                for half in range(2):
                    tile = change[r:r + 8, 128 * half:128 * half + 128]
                    for k in range(8 * half, min(8 * half + 8, TILES)):
                        at = slice(128 * k, 128 * k + 128)
                        done[f, r:r + 8, at] = new[r:r + 8, at] + expand(tile, k % 8)
            rows = pl.ds(step * i, step)
            copies.append(pltpu.make_async_copy(done.at[f, rows, :], out.at[rows, :], sems.at[5 + 2 * i + f]))
            copies[-1].start()
    for copy in copies:
        copy.wait()


def per_device(nb, nw, t, s, u, v, elev, zavg, mavg, flags, sel, ktab, btab):
    f32 = jnp.float32
    vmem = pl.BlockSpec(memory_space=pltpu.VMEM)
    hbm = pl.BlockSpec(memory_space=pl.ANY)
    scratch = lambda *shape: pltpu.VMEM(shape, f32)
    dma = lambda *shape: pltpu.SemaphoreType.DMA(shape)
    parts = pl.pallas_call(
        functools.partial(step_kernel, nb, nw),
        out_shape=(pltpu.VMEM((ROWS, LANES), f32),) * 2
        + (pltpu.VMEM((ROWS + 8, LANES), f32),) * 2
        + (pltpu.VMEM((ROWS, 256), f32),) * 2
        + (pltpu.VMEM((ROWS, COLS), f32),) * 3,
        in_specs=[hbm] * 11,
        out_specs=(vmem,) * 9,
        scratch_shapes=[
            pltpu.SMEM((2, 4), jnp.int32),
            pltpu.SMEM((8,), f32),
            pltpu.SMEM((8,), f32),
            pltpu.VMEM((ROWS, COLS), jnp.int32),
            scratch(ROWS, COLS), scratch(ROWS, COLS), scratch(ROWS, COLS),
            scratch(4, ROWS, LANES),
            scratch(RING, 8, 128), scratch(RING, 8, 128), scratch(ROWS, 128), scratch(ROWS, 128),
            scratch(RING, 24, 128), scratch(RING, 24, 128), scratch(ROWS + 16, 128), scratch(ROWS + 16, 128),
            scratch(4, RING, BAND, 128), scratch(4, RING, BAND, 128), scratch(4, TILES, BAND, 128),
            scratch(RING, BAND, 128), scratch(RING, BAND, 128),
            scratch(TILES, BAND, 128), scratch(TILES, BAND, 128), scratch(2, 2, BAND, 128),
            pltpu.VMEM((128 * LEVELS, 128), jnp.bfloat16), scratch(2, 2, ROWS, 128),
            scratch(4, 2, BAND, 128), scratch(ROWS, 128), scratch(ROWS, 128),
            scratch(4, 2, 8, 128), scratch(4, 2, 8, 128), scratch(ROWS + 16, 128), scratch(ROWS + 16, 128),
            dma(7), dma(4), dma(8), dma(8), dma(8), dma(8),
        ],
        compiler_params=pltpu.CompilerParams(
            collective_id=0, has_side_effects=True, vmem_limit_bytes=VMEM_BYTES),
        name="step",
    )(flags, ktab, btab, sel, t, s, u, v, zavg, mavg, elev)
    parts = [pltpu.with_memory_space_constraint(part, pltpu.VMEM) for part in parts]

    big = jax.ShapeDtypeStruct((ROWS, LANES), f32)
    flat = jax.ShapeDtypeStruct((ROWS, COLS), f32)
    return pl.pallas_call(
        finish_kernel,
        out_shape=(big,) * 4 + (flat,) * 3,
        in_specs=[vmem] * 9,
        out_specs=(hbm,) * 7,
        scratch_shapes=[scratch(2, ROWS, LANES), dma(15)],
        compiler_params=pltpu.CompilerParams(vmem_limit_bytes=VMEM_BYTES),
        name="finish",
    )(*parts)


def solution(mesh):
    grid = P("wide", "blocks")
    return jax.shard_map(
        functools.partial(per_device, mesh.shape["blocks"], mesh.shape["wide"]),
        mesh=mesh,
        in_specs=(grid,) * 9 + (P(), P()),
        out_specs=(grid,) * 7,
        check_vma=False,
    )
```

```python
import functools

import jax
import jax.numpy as jnp
from jax import lax
from jax.experimental import pallas as pl
from jax.experimental.pallas import tpu as pltpu
from jax.sharding import PartitionSpec as P

BLOCK = 60
LEVELS = 8
NSUB = 4
ROWS = 120
COLS = 240
LANES = COLS * LEVELS
TILES = LANES // 128
RING = TILES + 1
PAD = 16
BAND = ROWS + 2 * PAD
MESH = pl.DeviceIdType.MESH
VMEM_BYTES = 56 * 1024 * 1024


def lanes_of(shape=(8, 128)):
    return lax.broadcasted_iota(jnp.int32, shape, 1)


def rows_of(shape=(8, 128)):
    return lax.broadcasted_iota(jnp.int32, shape, 0)


def pick_lanes(tile, index):
    return jnp.take_along_axis(tile, index, axis=1, mode="promise_in_bounds")


def row_xor(tile, bit):
    keep = (rows_of(tile.shape) // bit) % 2 == 0
    return jnp.where(keep, pltpu.roll(tile, 8 - bit, 0), pltpu.roll(tile, bit, 0))


def turn_rows(tile):
    for bit in (1, 2, 4):
        tile = row_xor(tile, bit)
    return tile


class Neighbours:
    def __init__(self, nb, nw):
        b, x = lax.axis_index("blocks"), lax.axis_index("wide")
        self.b, self.x = b, x
        self.top, self.inner, self.above = x == nw - 1, x < nw - 1, x > 0
        self.east, self.west = lax.rem(b + 1, nb), lax.rem(b + nb - 1, nb)
        self.fold = nb - 1 - b
        self.fold_east = lax.rem(2 * nb - 2 - b, nb)
        self.fold_west = lax.rem(nb - b, nb)
        self.own_east = jnp.logical_and(self.top, self.fold_east == b)
        self.own_west = jnp.logical_and(self.top, self.fold_west == b)
        self.far_east = jnp.logical_and(self.top, self.fold_east != b)
        self.far_west = jnp.logical_and(self.top, self.fold_west != b)

    def greet(self):
        sem = pltpu.get_barrier_semaphore()

        def greet(b, x):
            pl.semaphore_signal(sem, inc=1, device_id=(b, x), device_id_type=MESH)

        b, x = self.b, self.x
        greet(self.east, x)
        greet(self.west, x)

        @pl.when(self.inner)
        def _():
            greet(b, x + 1)
            greet(self.east, x + 1)
            greet(self.west, x + 1)

        @pl.when(self.top)
        def _():
            greet(self.fold, x)

        @pl.when(self.far_east)
        def _():
            greet(self.fold_east, x)

        @pl.when(self.far_west)
        def _():
            greet(self.fold_west, x)

        @pl.when(self.above)
        def _():
            greet(b, x - 1)
            greet(self.east, x - 1)
            greet(self.west, x - 1)

    def meet(self):
        sem = pltpu.get_barrier_semaphore()
        x = self.x
        own = jnp.logical_or(self.own_east, self.own_west)

        @pl.when(x == 0)
        def _():
            pl.semaphore_wait(sem, 5)

        @pl.when(own)
        def _():
            pl.semaphore_wait(sem, 7)

        @pl.when(jnp.logical_and(self.above, jnp.logical_not(own)))
        def _():
            pl.semaphore_wait(sem, 8)

    def wire(self, north, south, east, west, rn, rs, rw, re, send, recv):
        b, x = self.b, self.x

        def c(src, dst, way, slot, to_b, to_x):
            return pltpu.make_async_remote_copy(
                src_ref=src, dst_ref=dst, send_sem=send.at[way], recv_sem=recv.at[slot],
                device_id=(to_b, to_x), device_id_type=MESH)

        return dict(
            always=[
                c(east[0], rw[0], 0, 0, self.east, x),
                c(west[0], re[0], 1, 1, self.west, x),
            ],
            inner=[
                c(east[1], rw[1], 4, 4, self.east, x + 1),
                c(west[1], re[1], 5, 5, self.west, x + 1),
                c(north, rs, 2, 2, b, x + 1),
            ],
            above=[
                c(east[2], rw[2], 6, 6, self.east, x - 1),
                c(west[2], re[2], 7, 7, self.west, x - 1),
                c(south, rn, 3, 3, b, x - 1),
            ],
            top=[c(north, rn, 2, 3, self.fold, x)],
            far_east=[c(east[1], re[2], 4, 7, self.fold_east, x)],
            far_west=[c(west[1], rw[2], 5, 6, self.fold_west, x)],
        )

    def start(self, wires, east, west, rw, re):
        def go(name, cond):
            @pl.when(cond)
            def _():
                for copy in wires[name]:
                    copy.start()

        for copy in wires["always"]:
            copy.start()
        go("far_east", self.far_east)
        go("far_west", self.far_west)
        go("top", self.top)
        go("inner", self.inner)
        go("above", self.above)

        @pl.when(self.own_east)
        def _():
            re[2][...] = east[1][...]

        @pl.when(self.own_west)
        def _():
            rw[2][...] = west[1][...]

    def finish(self, wires):
        w = wires
        for copy in w["always"]:
            copy.wait_recv()
            copy.wait_send()
        w["top"][0].wait_recv()

        @pl.when(self.above)
        def _():
            for copy in w["inner"]:
                copy.wait_recv()
            for copy in w["above"]:
                copy.wait_send()

        @pl.when(jnp.logical_not(self.own_east))
        def _():
            w["far_east"][0].wait_recv()
            w["far_east"][0].wait_send()

        @pl.when(jnp.logical_not(self.own_west))
        def _():
            w["far_west"][0].wait_recv()
            w["far_west"][0].wait_send()

        w["top"][0].wait_send()


def block_row(flags, row, tile):
    low, high = (128 * tile) // (BLOCK * LEVELS), (128 * tile + 127) // (BLOCK * LEVELS)
    value = jnp.full((8, 128), flags[row, low].astype(jnp.float32))
    if low != high:
        value = jnp.where(
            lanes_of() < BLOCK * LEVELS * high - 128 * tile,
            value,
            flags[row, high].astype(jnp.float32),
        )
    return value


def expand(tile, part):
    index = lanes_of() // LEVELS + 16 * part
    return pick_lanes(tile, index)


def halves(values):
    coarse = values.astype(jnp.bfloat16)
    return [coarse, (values - coarse.astype(jnp.float32)).astype(jnp.bfloat16)]


def step_kernel(
    nb, nw, flags_in, ktab_in, btab_in, sel_in, t, s, u, v, zavg_in, mavg_in, elev_in,
    tn, sn, un, vn, du, dv, height, zonal, merid,
    flags, ktab, btab, sel, zavg, mavg, elev,
    raw, npack, spack, wpack, epack, rn, rs, rw, re,
    field, once, part, wet, count, wide_k, wide_b, pick, spread_out, mean, base_plane,
    end_field, end_own, end_k, end_b, end_wet, end_side, end_once, end_part, end_new,
    plane, wpack2, epack2, rn2, rs2, rw2, re2,
    small, load, send, recv, send2, recv2,
):
    f32, bf16 = jnp.float32, jnp.bfloat16
    sources = (t, s, u, v)
    results = (tn, sn, un, vn)
    near = Neighbours(nb, nw)
    near.greet()

    tables = [
        pltpu.make_async_copy(src, dst, small.at[i])
        for i, (src, dst) in enumerate(
            ((flags_in, flags), (ktab_in, ktab), (btab_in, btab), (sel_in, sel),
             (elev_in, elev), (zavg_in, zavg), (mavg_in, mavg)))
    ]
    loads = [pltpu.make_async_copy(src, raw.at[f], load.at[f]) for f, src in enumerate(sources)]
    for copy in tables:
        copy.start()
    for copy in loads:
        copy.start()

    lane, sub = lanes_of(), rows_of()
    lane_c, row_c = lanes_of((ROWS, 128)), rows_of((ROWS, 128))
    lane_h = lanes_of((ROWS + 16, 128))
    end = 2 + ROWS // 8
    middle = 2 + BLOCK // 8
    split = BLOCK % 8
    early, late = range(2, middle), range(middle + 1, end)
    flows, tracers = (2, 3), (0, 1)
    inside, everywhere, rim = range(TILES), range(RING), (0, TILES - 1, TILES)
    ends = slice(PAD - 8, PAD + ROWS + 8)
    own = pl.ds(PAD, ROWS)
    span = 128 * LEVELS

    pick[...] = jnp.where(
        lax.broadcasted_iota(jnp.int32, (span, 128), 0) // LEVELS
        == lax.broadcasted_iota(jnp.int32, (span, 128), 1), 1.0 / LEVELS, 0.0).astype(bf16)
    spread_out[...] = jnp.where(
        lax.broadcasted_iota(jnp.int32, (256, span), 0) % 128
        == lax.broadcasted_iota(jnp.int32, (256, span), 1) // LEVELS, 1.0, 0.0).astype(bf16)

    tables[0].wait()
    lows = [block_row(flags, 0, k) for k in inside]
    highs = [block_row(flags, 1, k) for k in inside]

    def beside(tiles, k):
        left = pltpu.roll(tiles[k], 128 - LEVELS, 1)
        next_left = pltpu.roll(tiles[(k + 1) % TILES], 128 - LEVELS, 1)
        right = pltpu.roll(tiles[k], LEVELS, 1)
        last_right = pltpu.roll(tiles[(k - 1) % TILES], LEVELS, 1)
        return jnp.where(lane < 128 - LEVELS, left, next_left) + jnp.where(lane < LEVELS, last_right, right)

    for k in inside:
        low, high = lows[k], highs[k]
        side_low, side_high = beside(lows, k), beside(highs, k)
        count_low, count_high = low * (side_low + (low + low)), high * (side_high + (high + high))
        mixed = jnp.where(sub < split, low, high)
        north = jnp.where(sub < split - 1, low, high)
        south = jnp.where(sub < split + 1, low, high)
        for e in early:
            wet[k, 8 * e:8 * e + 8, :] = low
            count[k, 8 * e:8 * e + 8, :] = count_low
        for e in late:
            wet[k, 8 * e:8 * e + 8, :] = high
            count[k, 8 * e:8 * e + 8, :] = count_high
        wet[k, 8 * middle:8 * middle + 8, :] = mixed
        count[k, 8 * middle:8 * middle + 8, :] = mixed * (
            jnp.where(sub < split, side_low, side_high) + (north + south))

    for copy in tables[1:]:
        copy.wait()
    for half, width in ((0, 128), (1, COLS - 128)):
        w = jnp.zeros((ROWS, 128), f32)
        for i in range(2):
            for j in range(4):
                here = jnp.logical_and(row_c // BLOCK == i, (lane_c + 128 * half) // BLOCK == j)
                w = jnp.where(here, flags[i, j].astype(f32), w)
        plane[3, half, own, :] = w
        if width < 128:
            plane[2, half, own, :] = jnp.zeros((ROWS, 128), f32)
            base_plane[:, half] = jnp.zeros((2, ROWS, 128), f32)
        at = slice(128 * half, 128 * half + width)
        plane[2, half, own, 0:width] = w[:, 0:width] * elev[:, at]
        base_plane[0, half, :, 0:width] = w[:, 0:width] * zavg[:, at]
        base_plane[1, half, :, 0:width] = w[:, 0:width] * mavg[:, at]

    for half, width in ((0, 128), (1, COLS - 128)):
        index = sel[:, 128 * half:128 * half + width]
        if width < 128:
            index = jnp.concatenate([index, jnp.zeros((ROWS, 128 - width), jnp.int32)], axis=1)
        kappa = jnp.full(index.shape, ktab[0])
        bihar = jnp.full(index.shape, btab[0])
        for n in range(1, 8):
            hit = index == n
            kappa = jnp.where(hit, ktab[n], kappa)
            bihar = jnp.where(hit, btab[n], bihar)
        for table, to in ((kappa, wide_k), (bihar, wide_b)):
            wide = jnp.dot(
                jnp.concatenate(halves(table), axis=1), spread_out[...], preferred_element_type=f32)
            for k in range(8 * half, min(8 * half + 8, TILES)):
                to[k, own, :] = wide[:, 128 * (k % 8):128 * (k % 8) + 128]

    for copy in loads:
        copy.wait()
    for k in inside:
        at = slice(128 * k, 128 * k + 128)
        south, north = jnp.zeros((8, 128), f32), jnp.zeros((8, 128), f32)
        for f in range(4):
            below, above = raw[f, 0:8, at], raw[f, ROWS - 8:ROWS, at]
            south = jnp.where(sub // 2 == f, pltpu.roll(below, 2 * f, 0) if f else below, south)
            north = jnp.where(sub // 2 == f, pltpu.roll(above, 2 * f + 2, 0) if f < 3 else above, north)
        spack[k] = south * wet[k, PAD:PAD + 8, :]
        npack[k] = north * wet[k, PAD + ROWS - 8:PAD + ROWS, :]
    for row, pack, at in ((0, spack, PAD), (1, npack, PAD + ROWS - 8)):
        tail = jnp.zeros((8, 128), f32)
        for j in range(4):
            tail = jnp.where(lane // 32 == j, flags[row, j].astype(f32), tail)
        pack[TILES] = tail
        for half in range(2):
            pack[RING + half] = plane[2, half, at:at + 8, :]
    for side, pack in ((0, wpack), (1, epack)):
        w = wet[(TILES - 1) * side, own, :]
        packed = jnp.ones((ROWS, 128), f32)
        for f in range(4):
            shift = (16 * f + 64 * side) % 128
            tile = raw[f, :, (LANES - 128) * side:(LANES - 128) * side + 128]
            place = lane_c // 16 == f + 3 * side
            packed = jnp.where(place, pltpu.roll(tile, shift, 1) if shift else tile, packed)
        packed = packed * w
        top = pltpu.roll(plane[2, side, own, :], 24 if side else 64, 1)
        pack[...] = jnp.where(lane_c // 8 == (0 if side else 8), top, packed)
    near.meet()
    into = pl.ds(8, 8)

    def three(ref):
        return ref, ref.at[pl.ds(ROWS - 8, 8)], ref.at[pl.ds(0, 8)]

    def spots(ref):
        return ref.at[pl.ds(8, ROWS)], ref.at[pl.ds(0, 8)], ref.at[pl.ds(ROWS + 8, 8)]

    east, west, from_west, from_east = three(epack), three(wpack), spots(rw), spots(re)
    wires = near.wire(
        npack, spack, east, west, rn.at[:, into, :], rs.at[:, into, :], from_west, from_east, send, recv)
    near.start(wires, east, west, from_west, from_east)

    def around(ref, turned, key, k, base, ring_size):
        here, above, below = pl.ds(base, 8), pl.ds(base + 1, 8), pl.ds(base - 1, 8)

        def ring(k):
            if (key, k) not in turned:
                tile = ref[k, here, :]
                turned[key, k] = (tile, pltpu.roll(tile, 128 - LEVELS, 1), pltpu.roll(tile, LEVELS, 1))
            return turned[key, k]

        tile, left, right = ring(k)
        east = jnp.where(lane < 128 - LEVELS, left, ring((k + 1) % ring_size)[1])
        west = jnp.where(lane < LEVELS, ring((k - 1) % ring_size)[2], right)
        return tile, east, west, ref[k, above, :], ref[k, below, :]

    def at_tile(e):
        return 8 * e if isinstance(e, int) else pl.multiple_of(8 * e, 8)

    def weigh(base, tiles, same, ring_size=RING):
        turned = {}
        for k in tiles:
            w, we, ww, wn, ws = around(wet, turned, "wet", k, base, ring_size)
            total = w * ((we + ww) + (wn + ws))
            for to in same:
                count[k, to:to + 8, :] = total

    def mask(e, which):
        base = at_tile(e)
        rows, here = pl.ds(base - PAD, 8), pl.ds(base, 8)
        for k in inside:
            w = wet[k, here, :]
            for f in which:
                field[f, k, here, :] = raw[f, rows, 128 * k:128 * k + 128] * w

    def first(base, tiles, which, ring_size, whole=True):
        here = pl.ds(base, 8)
        turned = {}
        for k in tiles:
            w, total = wet[k, here, :], count[k, here, :]
            full = whole and k < TILES
            if full:
                mixing = wide_k[k, here, :] + wide_b[k, here, :] * total
                zonal_own = 0.05 * field[2, k, here, :]
                merid_own = 0.05 * field[3, k, here, :]
            for f in which:
                c, fe, fw, fn, fs = around(field.at[f], turned, f, k, base, ring_size)
                lap = w * ((fe + fw) + (fn + fs)) - total * c
                once[f, k, here, :] = lap
                if full:
                    part[f, k, here, :] = (
                        c - (zonal_own * (fe - fw) + merid_own * (fn - fs))) + mixing * lap

    def second(e, tiles, which, ring_size):
        base = at_tile(e)
        here, rows = pl.ds(base, 8), pl.ds(base - PAD, 8)
        turned = {}
        for k in tiles:
            fade = wide_b[k, here, :] * wet[k, here, :]
            for f in which:
                _, le, lw, ln, ls = around(once.at[f], turned, f, k, base, ring_size)
                results[f][rows, 128 * k:128 * k + 128] = (
                    part[f, k, here, :] - fade * ((le + lw) + (ln + ls)))

    def by_three(low, high, step):
        def body(i, carry):
            for j in range(3):
                step(low + 3 * i + j)
            return carry
        lax.fori_loop(0, (high - low) // 3, body, 0)

    def turn(f, tile_lane=None):
        at = lane if tile_lane is None else tile_lane
        return (at - 16 * f + 32 + 128) % 128

    def bring(f, last, begin):
        return jnp.where(turn(f) < 64, pltpu.roll(last, 16 * f, 1), pltpu.roll(begin, 64 + 16 * f, 1))

    def bring_field(base):
        here = pl.ds(base, 8)
        for f in flows:
            end_field[f - 2, here, :] = bring(f, field[f, TILES - 1, here, :], field[f, 0, here, :])

    def bring_rest(e):
        base = at_tile(e)
        here = pl.ds(base, 8)
        bring_field(base)
        for i in range(2):
            flow = 0.05 * end_field[i, here, :]
            end_own[i, i, here, :] = flow
            end_own[1 - i, i, here, :] = pltpu.roll(flow, 112 if i else 16, 1)
        for src, to in ((wide_k, end_k), (wide_b, end_b)):
            tile = bring(2, src[TILES - 1, here, :], src[0, here, :])
            to[0, here, :] = tile
            to[1, here, :] = pltpu.roll(tile, 16, 1)

    by_three(2, end, lambda e: mask(e, flows))
    by_three(2, end, lambda e: first(at_tile(e), inside, flows, TILES))
    by_three(3, end - 2, lambda e: second(e, inside, flows, TILES))
    second(end - 2, inside, flows, TILES)
    by_three(2, end, bring_rest)
    for half in range(2):
        width = span if half == 0 else LANES - span
        pieces = halves(un[:, span * half:span * half + width]) + halves(vn[:, span * half:span * half + width])
        means = jnp.dot(jnp.concatenate(pieces, axis=0), pick[0:width, :], preferred_element_type=f32)
        for i in range(2):
            mean[i, half] = means[256 * i:256 * i + ROWS] + means[256 * i + 128:256 * i + 128 + ROWS]

    near.finish(wires)

    @pl.when(near.x == 0)
    def _():
        rs[:, 8:16, :] = jnp.zeros((RING + 2, 8, 128), f32)
        rw[0:8, :] = jnp.zeros((8, 128), f32)
        re[0:8, :] = jnp.zeros((8, 128), f32)

    @pl.when(near.top)
    def _():
        sign = jnp.where(sub < 4, 1.0, -1.0)
        tiles = [rn[TILES - 1 - k, 8:16, :] for k in inside]
        for k in inside:
            rn[k, 8:16, :] = sign * row_xor(pick_lanes(tiles[k], lane + 120 - 16 * (lane // 8)), 1)
        rn[TILES, 8:16, :] = pick_lanes(rn[TILES, 8:16, :], lane + 96 - 64 * (lane // 32))
        start = turn_rows(pick_lanes(rn[RING + 1, 8:16, :], (239 - lane) % 128))
        last = turn_rows(pick_lanes(rn[RING, 8:16, :], (239 - lane) % 128))
        rn[RING, 8:16, :] = jnp.where(lane < 112, start, last)
        rn[RING + 1, 8:16, :] = jnp.where(lane < 112, last, start)
        swap = lane + 8 - 16 * ((lane // 8) % 2)
        index = jnp.where(
            lane < 8, 71 - lane, jnp.where(jnp.logical_and(lane >= 48, lane < 112), swap - 48, 100))
        tile = turn_rows(pick_lanes(rw[ROWS + 8:ROWS + 16, :], index))
        rw[ROWS + 8:ROWS + 16, :] = jnp.where(jnp.logical_and(lane >= 80, lane < 112), -tile, tile)
        index = jnp.where(lane < 64, swap + 48, jnp.where(lane < 72, 71 - lane, 20))
        tile = turn_rows(pick_lanes(re[ROWS + 8:ROWS + 16, :], index))
        re[ROWS + 8:ROWS + 16, :] = jnp.where(jnp.logical_and(lane >= 32, lane < 64), -tile, tile)

    halo_flags = []
    for got, base in ((rs, PAD - 8), (rn, PAD + ROWS)):
        tail = got[TILES, 8:16, :]
        flag = [jnp.broadcast_to(tail[:, 32 * j:32 * j + 1], (8, 128)) for j in range(4)]
        halo_flags.append(flag)
        for k in inside:
            low, high = (128 * k) // (BLOCK * LEVELS), (128 * k + 127) // (BLOCK * LEVELS)
            value = flag[low]
            if low != high:
                value = jnp.where(lane < BLOCK * LEVELS * high - 128 * k, value, flag[high])
            wet[k, base:base + 8, :] = value

    def halo_rows(which):
        for f in which:
            for k in inside:
                field[f, k, PAD - 8:PAD, :] = rs[k, 2 * f + 2:2 * f + 10, :]
                field[f, k, PAD + ROWS:PAD + ROWS + 8, :] = rn[k, 2 * f + 8:2 * f + 16, :]

    halo_rows(flows)

    for e in (1, end):
        bring_field(8 * e)
    for e in range(1, end + 1):
        here, rows = slice(8 * e, 8 * e + 8), slice(8 * e - 8, 8 * e)
        east, west = re[rows, :], rw[rows, :]
        wet_east = jnp.broadcast_to(east[:, 100:101], (8, 128))
        wet_west = jnp.broadcast_to(west[:, 20:21], (8, 128))
        last, begin = wet[TILES - 1, here, :], wet[0, here, :]
        for f in flows:
            at = turn(f)
            end_wet[f - 2, here, :] = jnp.where(
                at < 64, jnp.where(at < 32, last, wet_east), jnp.where(at < 96, wet_west, begin))
            end_side[f - 2, here, :] = jnp.where(
                at < 64, last + jnp.where(at < 24, last, wet_east), begin + jnp.where(at < 104, wet_west, begin))
            end_field[f - 2, here, :] = jnp.where(
                at // 16 == 2, east, jnp.where(at // 16 == 5, west, end_field[f - 2, here, :]))
    for base in range(PAD - 1, PAD + ROWS + 1, 8):
        here, above, below = slice(base, base + 8), slice(base + 1, base + 9), slice(base - 1, base + 7)
        for i in range(2):
            w = end_wet[i, here, :]
            total = w * (end_side[i, here, :] + (end_wet[i, above, :] + end_wet[i, below, :]))
            c, fn, fs = end_field[i, here, :], end_field[i, above, :], end_field[i, below, :]
            fe, fw = pltpu.roll(c, 128 - LEVELS, 1), pltpu.roll(c, LEVELS, 1)
            lap = w * ((fe + fw) + (fn + fs)) - total * c
            end_once[i, here, :] = lap
            end_part[i, here, :] = (
                c - (end_own[i, 0, here, :] * (fe - fw) + end_own[i, 1, here, :] * (fn - fs))
            ) + (end_k[i, here, :] + end_b[i, here, :] * total) * lap
    for e in range(2, end):
        here = slice(8 * e, 8 * e + 8)
        for i in range(2):
            lap = end_once[i, here, :]
            total = (pltpu.roll(lap, 128 - LEVELS, 1) + pltpu.roll(lap, LEVELS, 1)) + (
                end_once[i, 8 * e + 1:8 * e + 9, :] + end_once[i, 8 * e - 1:8 * e + 7, :])
            end_new[i, 8 * e - PAD:8 * e - PAD + 8, :] = (
                end_part[i, here, :] - end_b[i, here, :] * end_wet[i, here, :] * total)

    for base in (PAD - 4, PAD + ROWS - 4):
        weigh(base, inside, (base,), TILES)
        first(base, inside, flows, TILES)
    for e in (2, end - 1):
        second(e, inside, flows, TILES)

    for half in range(2):
        width = span if half == 0 else LANES - span
        at = slice(span * half, span * half + width)
        pieces = []
        for new in (un, vn):
            pieces += halves(jnp.concatenate([new[0:8, at], new[ROWS - 8:ROWS, at]], axis=0))
        means = jnp.dot(jnp.concatenate(pieces, axis=0), pick[0:width, :], preferred_element_type=f32)
        for i in range(2):
            value = means[32 * i:32 * i + 16] + means[32 * i + 16:32 * i + 32]
            mean[i, half, 0:8, :] = value[0:8]
            mean[i, half, ROWS - 8:ROWS, :] = value[8:16]
    from_lane = lax.broadcasted_iota(jnp.int32, (128, 256), 0)
    to_lane = lax.broadcasted_iota(jnp.int32, (128, 256), 1)
    for i in range(2):
        cell = turn(i + 2, from_lane) // LEVELS
        hit = jnp.logical_or(
            jnp.logical_and(cell - 12 == to_lane, to_lane < 2),
            jnp.logical_and(cell - 2 == to_lane - (COLS - 2), to_lane >= COLS - 2))
        hit = jnp.logical_and(hit, to_lane < COLS)
        matrix = jnp.where(hit, 1.0 / LEVELS, 0.0).astype(bf16)
        means = jnp.dot(
            jnp.concatenate(halves(end_new[i]), axis=0), matrix, preferred_element_type=f32)
        value = means[0:ROWS] + means[128:128 + ROWS]
        mean[i, 0] = jnp.where(lane_c < 2, value[:, 0:128], mean[i, 0])
        mean[i, 1] = jnp.where(lane_c // 2 == (COLS - 2 - 128) // 2, value[:, 128:256], mean[i, 1])
        for half in range(2):
            plane[i, half, own, :] = base_plane[i, half] + mean[i, half]

    for pack, side, shift in ((wpack2, 0, 0), (epack2, 1, 24)):
        for r in range(2):
            packed = jnp.zeros((8, 128), f32)
            for g in range(8 - r):
                rows = slice(PAD + 16 * g + 8 * r, PAD + 16 * g + 8 * r + 8)
                for p in range(2):
                    turned = pltpu.roll(plane[p, side, rows, :], (16 * g + 8 * p + shift) % 128, 1)
                    packed = jnp.where(lane // 8 == 2 * g + p, turned, packed)
            pack[8 * r:8 * r + 8, :] = packed

    def three2(ref):
        return ref, ref.at[pl.ds(0, 8)], ref.at[pl.ds(0, 8)]

    def spots2(ref):
        return ref.at[pl.ds(0, 16)], ref.at[pl.ds(16, 8)], ref.at[pl.ds(24, 8)]

    north = plane.at[pl.ds(0, 2), :, pl.ds(PAD + ROWS - 8, 8), :]
    south = plane.at[pl.ds(0, 2), :, pl.ds(PAD, 8), :]
    east, west, from_west, from_east = three2(epack2), three2(wpack2), spots2(rw2), spots2(re2)
    wires2 = near.wire(north, south, east, west, rn2, rs2, from_west, from_east, send2, recv2)
    near.start(wires2, east, west, from_west, from_east)

    for e in range(2, end):
        rows = slice(8 * e - PAD, 8 * e - PAD + 8)
        for i in range(2):
            tile, new, f = end_new[i, rows, :], (un, vn)[i], i + 2
            begin = pltpu.roll(tile, (64 - 16 * f) % 128, 1)
            last = pltpu.roll(tile, 128 - 16 * f, 1)
            new[rows, 0:128] = jnp.where(lane < 16, begin, new[rows, 0:128])
            new[rows, LANES - 128:LANES] = jnp.where(lane >= 112, last, new[rows, LANES - 128:LANES])

    halo_rows(tracers)
    west, east = rw[...], re[...]
    wet_east = jnp.broadcast_to(east[:, 100:101], (ROWS + 16, 128))
    wet_west = jnp.broadcast_to(west[:, 20:21], (ROWS + 16, 128))
    wet[TILES, ends, :] = jnp.where(lane_h < 64, wet_east, wet_west)
    for f in tracers:
        right = pltpu.roll(east, 128 - 16 * f, 1) if f else east
        field[f, TILES, ends, :] = jnp.where(lane_h < 64, right, pltpu.roll(west, 64 - 16 * f, 1))
    for e in (1, 2, end - 1, end):
        weigh(8 * e, everywhere, (8 * e,))
    weigh(8 * 3, rim, [8 * e for e in early[1:]])
    weigh(8 * middle, rim, (8 * middle,))
    weigh(8 * (middle + 1), rim, [8 * e for e in late[:-1]])
    by_three(2, end, lambda e: mask(e, tracers))
    for e in (1, end):
        first(8 * e, everywhere, tracers, RING, whole=False)
    by_three(2, end, lambda e: first(at_tile(e), everywhere, tracers, RING))
    by_three(2, end, lambda e: second(e, inside, tracers, RING))

    for (got, flag), at in zip(((rs, halo_flags[0]), (rn, halo_flags[1])), (PAD - 8, PAD + ROWS)):
        for half in range(2):
            plane[2, half, at:at + 8, :] = got[RING + half, 8:16, :]
        plane[3, 0, at:at + 8, :] = jnp.where(
            lane < BLOCK, flag[0], jnp.where(lane < 2 * BLOCK, flag[1], flag[2]))
        plane[3, 1, at:at + 8, :] = jnp.where(lane < 3 * BLOCK - 128, flag[2], flag[3])
    for p, beyond in (
        (2, jnp.where(lane_h < 120, pltpu.roll(east, 48, 1), pltpu.roll(west, 120, 1))),
        (3, jnp.where(lane_h < 120, wet_east, wet_west)),
    ):
        plane[p, 1, ends, :] = jnp.where(lane_h < 112, plane[p, 1, ends, :], beyond)

    near.finish(wires2)

    @pl.when(near.x == 0)
    def _():
        rs2[...] = jnp.zeros(rs2.shape, f32)
        rw2[16:24, :] = jnp.zeros((8, 128), f32)
        re2[16:24, :] = jnp.zeros((8, 128), f32)

    @pl.when(near.top)
    def _():
        for p in range(2):
            start = -turn_rows(pick_lanes(rn2[p, 1], (239 - lane) % 128))
            last = -turn_rows(pick_lanes(rn2[p, 0], (239 - lane) % 128))
            rn2[p, 0] = jnp.where(lane < 112, start, last)
            rn2[p, 1] = jnp.where(lane < 112, last, start)
        for got in (rw2, re2):
            got[24:32, :] = -turn_rows(pick_lanes(got[24:32, :], 112 + (lane // 8 % 2) * 8 + 7 - lane % 8))

    for p in range(2):
        for half in range(2):
            plane[p, half, PAD - 8:PAD, :] = rs2[p, half]
            plane[p, half, PAD + ROWS:PAD + ROWS + 8, :] = rn2[p, half]
    for e in range(1, end + 1):
        here = slice(8 * e, 8 * e + 8)
        g = 7 if e == 1 else 0 if e == end else (e - 2) // 2
        at = 16 if e == 1 else 24 if e == end else 8 * (e % 2)
        for p in range(2):
            beyond = jnp.where(
                lane < 120,
                pltpu.roll(re2[at:at + 8, :], (112 - 16 * g - 8 * p) % 128, 1),
                pltpu.roll(rw2[at:at + 8, :], (120 - 16 * g - 8 * p) % 128, 1))
            plane[p, 1, here, :] = jnp.where(lane < 112, plane[p, 1, here, :], beyond)

    def across(p, e):
        tiles = [plane[p, half, 8 * e:8 * e + 8, :] for half in range(2)]
        left = [pltpu.roll(tile, 127, 1) for tile in tiles]
        right = [pltpu.roll(tile, 1, 1) for tile in tiles]
        return [
            jnp.where(lane < 127, left[half], left[1 - half]) - jnp.where(lane < 1, right[1 - half], right[half])
            for half in range(2)
        ]

    def rows_apart(p, half, e):
        return plane[p, half, 8 * e + 1:8 * e + 9, :] - plane[p, half, 8 * e - 1:8 * e + 7, :]

    for n in range(NSUB):
        for e in range(1, end + 1):
            zonal_slope = across(0, e)
            for half in range(2):
                here = (half, slice(8 * e, 8 * e + 8), slice(None))
                flow = zonal_slope[half] + rows_apart(1, half, e)
                plane[(2,) + here] = plane[(2,) + here] - 0.3 * plane[(3,) + here] * flow
        inner = 1 if n == NSUB - 1 else 0
        for e in range(1 + inner, end + 1 - inner):
            zonal_slope = across(2, e)
            for half in range(2):
                here = (half, slice(8 * e, 8 * e + 8), slice(None))
                w = plane[(3,) + here]
                plane[(0,) + here] = w * (plane[(0,) + here] - 0.3 * zonal_slope[half])
                plane[(1,) + here] = w * (plane[(1,) + here] - 0.3 * rows_apart(2, half, e))
    for half, width in ((0, 128), (1, COLS - 128)):
        at = slice(128 * half, 128 * half + 128)
        du[:, at] = plane[0, half, own, :] - mean[0, half]
        dv[:, at] = plane[1, half, own, :] - mean[1, half]
        at = slice(128 * half, 128 * half + width)
        for p, ref in ((0, zonal), (1, merid), (2, height)):
            ref[:, at] = plane[p, half, own, 0:width]


def finish_kernel(
    tn, sn, un, vn, du, dv, height, zonal, merid,
    t_out, s_out, u_out, v_out, height_out, zonal_out, merid_out, done, sems,
):
    copies = [
        pltpu.make_async_copy(src, dst, sems.at[i])
        for i, (src, dst) in enumerate(
            ((tn, t_out), (sn, s_out), (height, height_out), (zonal, zonal_out), (merid, merid_out)))
    ]
    for copy in copies:
        copy.start()
    step = 24
    for i in range(ROWS // step):
        for f, (new, change, out) in enumerate(((un, du, u_out), (vn, dv, v_out))):
            for r in range(step * i, step * i + step, 8):
                for half in range(2):
                    tile = change[r:r + 8, 128 * half:128 * half + 128]
                    for k in range(8 * half, min(8 * half + 8, TILES)):
                        at = slice(128 * k, 128 * k + 128)
                        done[f, r:r + 8, at] = new[r:r + 8, at] + expand(tile, k % 8)
            rows = pl.ds(step * i, step)
            copies.append(pltpu.make_async_copy(done.at[f, rows, :], out.at[rows, :], sems.at[5 + 2 * i + f]))
            copies[-1].start()
    for copy in copies:
        copy.wait()


def per_device(nb, nw, t, s, u, v, elev, zavg, mavg, flags, sel, ktab, btab):
    f32 = jnp.float32
    vmem = pl.BlockSpec(memory_space=pltpu.VMEM)
    hbm = pl.BlockSpec(memory_space=pl.ANY)
    scratch = lambda *shape: pltpu.VMEM(shape, f32)
    dma = lambda *shape: pltpu.SemaphoreType.DMA(shape)
    parts = pl.pallas_call(
        functools.partial(step_kernel, nb, nw),
        out_shape=(pltpu.VMEM((ROWS, LANES), f32),) * 2
        + (pltpu.VMEM((ROWS + 8, LANES), f32),) * 2
        + (pltpu.VMEM((ROWS, 256), f32),) * 2
        + (pltpu.VMEM((ROWS, COLS), f32),) * 3,
        in_specs=[hbm] * 11,
        out_specs=(vmem,) * 9,
        scratch_shapes=[
            pltpu.SMEM((2, 4), jnp.int32),
            pltpu.SMEM((8,), f32),
            pltpu.SMEM((8,), f32),
            pltpu.VMEM((ROWS, COLS), jnp.int32),
            scratch(ROWS, COLS), scratch(ROWS, COLS), scratch(ROWS, COLS),
            scratch(4, ROWS, LANES),
            scratch(RING + 2, 8, 128), scratch(RING + 2, 8, 128), scratch(ROWS, 128), scratch(ROWS, 128),
            scratch(RING + 2, 24, 128), scratch(RING + 2, 24, 128),
            scratch(ROWS + 16, 128), scratch(ROWS + 16, 128),
            scratch(4, RING, BAND, 128), scratch(4, RING, BAND, 128), scratch(4, TILES, BAND, 128),
            scratch(RING, BAND, 128), scratch(RING, BAND, 128),
            scratch(TILES, BAND, 128), scratch(TILES, BAND, 128),
            pltpu.VMEM((128 * LEVELS, 128), jnp.bfloat16), pltpu.VMEM((256, 128 * LEVELS), jnp.bfloat16),
            scratch(2, 2, ROWS, 128), scratch(2, 2, ROWS, 128),
            scratch(2, BAND, 128), scratch(2, 2, BAND, 128), scratch(2, BAND, 128), scratch(2, BAND, 128),
            scratch(2, BAND, 128), scratch(2, BAND, 128), scratch(2, BAND, 128), scratch(2, BAND, 128),
            scratch(2, 128, 128),
            scratch(4, 2, BAND, 128), scratch(16, 128), scratch(16, 128),
            scratch(2, 2, 8, 128), scratch(2, 2, 8, 128), scratch(32, 128), scratch(32, 128),
            dma(7), dma(4), dma(8), dma(8), dma(8), dma(8),
        ],
        compiler_params=pltpu.CompilerParams(
            collective_id=0, has_side_effects=True, vmem_limit_bytes=VMEM_BYTES),
        name="step",
    )(flags, ktab, btab, sel, t, s, u, v, zavg, mavg, elev)
    parts = [pltpu.with_memory_space_constraint(part, pltpu.VMEM) for part in parts]

    big = jax.ShapeDtypeStruct((ROWS, LANES), f32)
    flat = jax.ShapeDtypeStruct((ROWS, COLS), f32)
    return pl.pallas_call(
        finish_kernel,
        out_shape=(big,) * 4 + (flat,) * 3,
        in_specs=[vmem] * 9,
        out_specs=(hbm,) * 7,
        scratch_shapes=[scratch(2, ROWS, LANES), dma(15)],
        compiler_params=pltpu.CompilerParams(vmem_limit_bytes=VMEM_BYTES),
        name="finish",
    )(*parts)


def solution(mesh):
    grid = P("wide", "blocks")
    return jax.shard_map(
        functools.partial(per_device, mesh.shape["blocks"], mesh.shape["wide"]),
        mesh=mesh,
        in_specs=(grid,) * 9 + (P(), P()),
        out_specs=(grid,) * 7,
        check_vma=False,
    )
```

```python
import functools

import jax
import jax.numpy as jnp
from jax import lax
from jax.experimental import pallas as pl
from jax.experimental.pallas import tpu as pltpu
from jax.sharding import PartitionSpec as P

BLOCK = 60
LEVELS = 8
NSUB = 4
ROWS = 120
COLS = 240
LANES = COLS * LEVELS
TILES = LANES // 128
RING = TILES + 1
PAD = 16
BAND = ROWS + 2 * PAD
MESH = pl.DeviceIdType.MESH
VMEM_BYTES = 56 * 1024 * 1024


def lanes_of(shape=(8, 128)):
    return lax.broadcasted_iota(jnp.int32, shape, 1)


def rows_of(shape=(8, 128)):
    return lax.broadcasted_iota(jnp.int32, shape, 0)


def pick_lanes(tile, index):
    return jnp.take_along_axis(tile, index, axis=1, mode="promise_in_bounds")


def row_xor(tile, bit):
    keep = (rows_of(tile.shape) // bit) % 2 == 0
    return jnp.where(keep, pltpu.roll(tile, 8 - bit, 0), pltpu.roll(tile, bit, 0))


def turn_rows(tile):
    for bit in (1, 2, 4):
        tile = row_xor(tile, bit)
    return tile


class Neighbours:
    def __init__(self, nb, nw):
        b, x = lax.axis_index("blocks"), lax.axis_index("wide")
        self.b, self.x = b, x
        self.top, self.inner, self.above = x == nw - 1, x < nw - 1, x > 0
        first, last = b == 0, b == nb - 1
        self.east, self.west = jnp.where(last, 0, b + 1), jnp.where(first, nb - 1, b - 1)
        self.fold = nb - 1 - b
        self.fold_east = jnp.where(last, nb - 1, nb - 2 - b)
        self.fold_west = jnp.where(first, 0, nb - b)
        self.own_east = jnp.logical_and(self.top, self.fold_east == b)
        self.own_west = jnp.logical_and(self.top, self.fold_west == b)
        self.far_east = jnp.logical_and(self.top, self.fold_east != b)
        self.far_west = jnp.logical_and(self.top, self.fold_west != b)

    def greet(self):
        sem = pltpu.get_barrier_semaphore()

        def greet(b, x):
            pl.semaphore_signal(sem, inc=1, device_id=(b, x), device_id_type=MESH)

        b, x = self.b, self.x
        greet(self.east, x)
        greet(self.west, x)

        @pl.when(self.inner)
        def _():
            greet(b, x + 1)
            greet(self.east, x + 1)
            greet(self.west, x + 1)

        @pl.when(self.top)
        def _():
            greet(self.fold, x)

        @pl.when(self.far_east)
        def _():
            greet(self.fold_east, x)

        @pl.when(self.far_west)
        def _():
            greet(self.fold_west, x)

        @pl.when(self.above)
        def _():
            greet(b, x - 1)
            greet(self.east, x - 1)
            greet(self.west, x - 1)

    def meet(self):
        sem = pltpu.get_barrier_semaphore()
        x = self.x
        own = jnp.logical_or(self.own_east, self.own_west)

        @pl.when(x == 0)
        def _():
            pl.semaphore_wait(sem, 5)

        @pl.when(own)
        def _():
            pl.semaphore_wait(sem, 7)

        @pl.when(jnp.logical_and(self.above, jnp.logical_not(own)))
        def _():
            pl.semaphore_wait(sem, 8)

    def wire(self, north, south, east, west, rn, rs, rw, re, send, recv):
        b, x = self.b, self.x

        def c(src, dst, way, slot, to_b, to_x):
            return pltpu.make_async_remote_copy(
                src_ref=src, dst_ref=dst, send_sem=send.at[way], recv_sem=recv.at[slot],
                device_id=(to_b, to_x), device_id_type=MESH)

        return dict(
            always=[
                c(east[0], rw[0], 0, 0, self.east, x),
                c(west[0], re[0], 1, 1, self.west, x),
            ],
            inner=[
                c(east[1], rw[1], 4, 4, self.east, x + 1),
                c(west[1], re[1], 5, 5, self.west, x + 1),
                c(north, rs, 2, 2, b, x + 1),
            ],
            above=[
                c(east[2], rw[2], 6, 6, self.east, x - 1),
                c(west[2], re[2], 7, 7, self.west, x - 1),
                c(south, rn, 3, 3, b, x - 1),
            ],
            top=[c(north, rn, 2, 3, self.fold, x)],
            far_east=[c(east[1], re[2], 4, 7, self.fold_east, x)],
            far_west=[c(west[1], rw[2], 5, 6, self.fold_west, x)],
        )

    def start(self, wires, east, west, rw, re):
        def go(name, cond):
            @pl.when(cond)
            def _():
                for copy in wires[name]:
                    copy.start()

        for copy in wires["always"]:
            copy.start()
        go("far_east", self.far_east)
        go("far_west", self.far_west)
        go("top", self.top)
        go("inner", self.inner)
        go("above", self.above)

        @pl.when(self.own_east)
        def _():
            re[2][...] = east[1][...]

        @pl.when(self.own_west)
        def _():
            rw[2][...] = west[1][...]

    def arrived(self, wires):
        w = wires
        for copy in w["always"]:
            copy.wait_recv()
        w["top"][0].wait_recv()

        @pl.when(self.above)
        def _():
            for copy in w["inner"]:
                copy.wait_recv()

        @pl.when(jnp.logical_not(self.own_east))
        def _():
            w["far_east"][0].wait_recv()

        @pl.when(jnp.logical_not(self.own_west))
        def _():
            w["far_west"][0].wait_recv()

    def sent(self, *every):
        for w in every:
            for copy in w["always"]:
                copy.wait_send()
            w["top"][0].wait_send()

        @pl.when(self.above)
        def _():
            for w in every:
                for copy in w["above"]:
                    copy.wait_send()

        @pl.when(jnp.logical_not(self.own_east))
        def _():
            for w in every:
                w["far_east"][0].wait_send()

        @pl.when(jnp.logical_not(self.own_west))
        def _():
            for w in every:
                w["far_west"][0].wait_send()


def block_row(flags, row, tile):
    low, high = (128 * tile) // (BLOCK * LEVELS), (128 * tile + 127) // (BLOCK * LEVELS)
    value = jnp.full((8, 128), flags[row, low].astype(jnp.float32))
    if low != high:
        value = jnp.where(
            lanes_of() < BLOCK * LEVELS * high - 128 * tile,
            value,
            flags[row, high].astype(jnp.float32),
        )
    return value


def expand(tile, part):
    index = lanes_of() // LEVELS + 16 * part
    return pick_lanes(tile, index)


def halves(values):
    coarse = values.astype(jnp.bfloat16)
    return [coarse, (values - coarse.astype(jnp.float32)).astype(jnp.bfloat16)]


def step_kernel(
    nb, nw, flags_in, ktab_in, btab_in, sel_in, t, s, u, v, zavg_in, mavg_in, elev_in,
    tn, sn, un, vn, du, dv, height, zonal, merid,
    flags, ktab, btab, sel, zavg, mavg, elev,
    edge_rows, edge_cols, raw, npack, spack, wpack, epack, rn, rs, rw, re,
    npack_b, spack_b, wpack_b, epack_b, rn_b, rs_b, rw_b, re_b,
    field, once, part, wet, count, wide_k, wide_b, pick, end_pick, spread_out, mean, base_plane,
    end_field, end_own, end_k, end_b, end_wet, end_side, end_once, end_part, end_new, wet_beyond, shifted,
    plane, npack2, spack2, wpack2, epack2, rn2, rs2, rw2, re2,
    small, load, send, recv, send_b, recv_b, send2, recv2,
):
    f32, bf16 = jnp.float32, jnp.bfloat16
    sources = (t, s, u, v)
    results = (tn, sn, un, vn)
    near = Neighbours(nb, nw)
    near.greet()

    tables = [
        pltpu.make_async_copy(src, dst, small.at[i])
        for i, (src, dst) in enumerate(
            ((flags_in, flags), (ktab_in, ktab), (btab_in, btab), (sel_in, sel),
             (elev_in, elev), (zavg_in, zavg), (mavg_in, mavg)))
    ]
    loads = [pltpu.make_async_copy(src, raw.at[f], load.at[f]) for f, src in enumerate(sources)]
    edges = []
    for i, src in enumerate((u, v)):
        for side, at in enumerate((0, ROWS - 8)):
            edges.append(pltpu.make_async_copy(
                src.at[pl.ds(at, 8), :], edge_rows.at[i, side], small.at[7 + 4 * i + side]))
        for side, at in enumerate((0, LANES - 128)):
            edges.append(pltpu.make_async_copy(
                src.at[:, pl.ds(at, 128)], edge_cols.at[i, side], small.at[9 + 4 * i + side]))
    tables[0].start()
    for copy in edges:
        copy.start()
    for copy in tables[1:4]:
        copy.start()
    for f in (2, 3, 0, 1):
        loads[f].start()
    for copy in tables[4:]:
        copy.start()

    lane, sub = lanes_of(), rows_of()
    lane_c, row_c = lanes_of((ROWS, 128)), rows_of((ROWS, 128))
    lane_h = lanes_of((ROWS + 16, 128))
    end = 2 + ROWS // 8
    middle = 2 + BLOCK // 8
    split = BLOCK % 8
    early, late = range(2, middle), range(middle + 1, end)
    flows, tracers = (2, 3), (0, 1)
    inside, everywhere, rim = range(TILES), range(RING), (0, TILES - 1, TILES)
    ends = slice(PAD - 8, PAD + ROWS + 8)
    own = pl.ds(PAD, ROWS)
    span = 128 * LEVELS

    pick[...] = jnp.where(
        lax.broadcasted_iota(jnp.int32, (span, 128), 0) // LEVELS
        == lax.broadcasted_iota(jnp.int32, (span, 128), 1), 1.0 / LEVELS, 0.0).astype(bf16)
    from_lane = lax.broadcasted_iota(jnp.int32, (128, 256), 0)
    to_lane = lax.broadcasted_iota(jnp.int32, (128, 256), 1)
    for i in range(2):
        cell = (from_lane - 16 * (i + 2) + 32 + 128) % 128 // LEVELS
        hit = jnp.logical_or(
            jnp.logical_and(cell - 12 == to_lane, to_lane < 2),
            jnp.logical_and(cell - 2 == to_lane - (COLS - 2), to_lane >= COLS - 2))
        hit = jnp.logical_and(hit, to_lane < COLS)
        end_pick[i] = jnp.where(hit, 1.0 / LEVELS, 0.0).astype(bf16)
    spread_out[...] = jnp.where(
        lax.broadcasted_iota(jnp.int32, (256, span), 0) % 128
        == lax.broadcasted_iota(jnp.int32, (256, span), 1) // LEVELS, 1.0, 0.0).astype(bf16)

    tables[0].wait()
    lows = [block_row(flags, 0, k) for k in inside]
    highs = [block_row(flags, 1, k) for k in inside]


    def beside(tiles, k):
        left = pltpu.roll(tiles[k], 128 - LEVELS, 1)
        next_left = pltpu.roll(tiles[(k + 1) % TILES], 128 - LEVELS, 1)
        right = pltpu.roll(tiles[k], LEVELS, 1)
        last_right = pltpu.roll(tiles[(k - 1) % TILES], LEVELS, 1)
        return jnp.where(lane < 128 - LEVELS, left, next_left) + jnp.where(lane < LEVELS, last_right, right)

    for k in inside:
        low, high = lows[k], highs[k]
        side_low, side_high = beside(lows, k), beside(highs, k)
        count_low, count_high = low * (side_low + (low + low)), high * (side_high + (high + high))
        mixed = jnp.where(sub < split, low, high)
        north = jnp.where(sub < split - 1, low, high)
        south = jnp.where(sub < split + 1, low, high)
        for e in early:
            wet[k, 8 * e:8 * e + 8, :] = low
            count[k, 8 * e:8 * e + 8, :] = count_low
        for e in late:
            wet[k, 8 * e:8 * e + 8, :] = high
            count[k, 8 * e:8 * e + 8, :] = count_high
        wet[k, 8 * middle:8 * middle + 8, :] = mixed
        count[k, 8 * middle:8 * middle + 8, :] = mixed * (
            jnp.where(sub < split, side_low, side_high) + (north + south))


    def pack_rows(packs, both, last):
        tiles = [[], []]
        for m in range(RING // 2):
            for side in range(2):
                packed = last[side]
                for k in (2 * m, 2 * m + 1):
                    if k >= TILES:
                        continue
                    for i in range(2):
                        row = 4 * (k % 2) + 2 * i
                        tile = both(i, side, k)
                        shift = (row + 2 * side) % 8
                        packed = jnp.where(sub // 2 == row // 2, pltpu.roll(tile, shift, 0) if shift else tile, packed)
                w = (lows, highs)[side]
                upper = w[2 * m + 1] if 2 * m + 1 < TILES else jnp.ones((8, 128), f32)
                packs[side][m] = packed * jnp.where(sub < 4, w[2 * m], upper)

    for copy in edges:
        copy.wait()
    tails = []
    for row in range(2):
        tail = jnp.zeros((8, 128), f32)
        for j in range(4):
            tail = jnp.where(lane // 32 == j, flags[row, j].astype(f32), tail)
        tails.append(tail)
    pack_rows((spack, npack), lambda i, side, k: edge_rows[i, side, :, 128 * k:128 * k + 128], tails)
    lane_a, row_a = lanes_of((64, 128)), rows_of((64, 128))
    lane_b = lanes_of((ROWS - 64, 128))
    for side, pack, to in ((0, wpack, 32), (1, epack, 80)):
        col = 3 * side
        w_a = jnp.where(row_a < BLOCK, flags[0, col].astype(f32), flags[1, col].astype(f32))
        w_b = jnp.full((ROWS - 64, 128), flags[1, col].astype(f32))
        parts_of = []
        for rows, at, lanes_in, w in ((slice(0, 64), to, lane_a, w_a), (slice(64, ROWS), (to + 64) % 128, lane_b, w_b)):
            packed = jnp.ones(w.shape, f32)
            for i in range(2):
                shift = (at + 16 * i - 112 * side) % 128
                packed = jnp.where(
                    lanes_in // 16 == at // 16 + i, pltpu.roll(edge_cols[i, side, rows, :], shift, 1), packed)
            parts_of.append(packed * w)
        at = (to + 64) % 128 // 16
        theirs = jnp.logical_or(lane_b // 8 == 1, jnp.logical_or(lane_b // 16 == at, lane_b // 16 == at + 1))
        pack[0:ROWS - 64, :] = jnp.where(theirs, parts_of[1], parts_of[0][0:ROWS - 64])
        pack[ROWS - 64:64, :] = parts_of[0][ROWS - 64:64]

    for copy in tables[1:4]:
        copy.wait()
    for half, width in ((0, 128), (1, COLS - 128)):
        index = sel[:, 128 * half:128 * half + width]
        if width < 128:
            index = jnp.concatenate([index, jnp.zeros((ROWS, 128 - width), jnp.int32)], axis=1)
        kappa = jnp.full(index.shape, ktab[0])
        bihar = jnp.full(index.shape, btab[0])
        for n in range(1, 8):
            hit = index == n
            kappa = jnp.where(hit, ktab[n], kappa)
            bihar = jnp.where(hit, btab[n], bihar)
        for table, to in ((kappa, wide_k), (bihar, wide_b)):
            wide = jnp.dot(
                jnp.concatenate(halves(table), axis=1), spread_out[...], preferred_element_type=f32)
            for k in range(8 * half, min(8 * half + 8, TILES)):
                to[k, own, :] = wide[:, 128 * (k % 8):128 * (k % 8) + 128]

    near.meet()
    into = pl.ds(8, 8)

    def three(ref):
        return ref, ref.at[pl.ds(ROWS - 8 - 64, 8)], ref.at[pl.ds(0, 8)]

    def spots(ref):
        return ref.at[pl.ds(0, 64)], ref.at[pl.ds(64, 8)], ref.at[pl.ds(72, 8)]

    east, west, from_west, from_east = three(epack), three(wpack), spots(rw), spots(re)
    wires = near.wire(
        npack, spack, east, west, rn.at[:, into, :], rs.at[:, into, :], from_west, from_east, send, recv)
    near.start(wires, east, west, from_west, from_east)

    for copy in tables[4:]:
        copy.wait()
    for half, width in ((0, 128), (1, COLS - 128)):
        w = jnp.zeros((ROWS, 128), f32)
        for i in range(2):
            for j in range(4):
                here = jnp.logical_and(row_c // BLOCK == i, (lane_c + 128 * half) // BLOCK == j)
                w = jnp.where(here, flags[i, j].astype(f32), w)
        plane[3, half, own, :] = w
        if width < 128:
            plane[2, half, own, :] = jnp.zeros((ROWS, 128), f32)
            base_plane[:, half] = jnp.zeros((2, ROWS, 128), f32)
        at = slice(128 * half, 128 * half + width)
        plane[2, half, own, 0:width] = w[:, 0:width] * elev[:, at]
        base_plane[0, half, :, 0:width] = w[:, 0:width] * zavg[:, at]
        base_plane[1, half, :, 0:width] = w[:, 0:width] * mavg[:, at]

    for copy in loads:
        copy.wait()
    pack_rows((spack_b, npack_b), lambda i, side, k: raw[i, (ROWS - 8) * side:(ROWS - 8) * side + 8, 128 * k:128 * k + 128],
              [jnp.zeros((8, 128), f32)] * 2)
    for pack, at in ((spack_b, PAD), (npack_b, PAD + ROWS - 8)):
        for half in range(2):
            pack[RING // 2 + half] = plane[2, half, at:at + 8, :]
    for side, pack in ((0, wpack_b), (1, epack_b)):
        w = wet[(TILES - 1) * side, own, :]
        packed = jnp.zeros((ROWS, 128), f32)
        for f in range(2):
            shift = (16 * f + 64 * side) % 128
            tile = raw[f, :, (LANES - 128) * side:(LANES - 128) * side + 128]
            place = lane_c // 16 == f + 3 * side
            packed = jnp.where(place, pltpu.roll(tile, shift, 1) if shift else tile, packed)
        packed = packed * w
        top = pltpu.roll(plane[2, side, own, :], 24 if side else 64, 1)
        pack[...] = jnp.where(lane_c // 8 == (0 if side else 8), top, packed)

    def three_b(ref):
        return ref, ref.at[pl.ds(ROWS - 8, 8)], ref.at[pl.ds(0, 8)]

    def spots_b(ref):
        return ref.at[pl.ds(8, ROWS)], ref.at[pl.ds(0, 8)], ref.at[pl.ds(ROWS + 8, 8)]

    east, west, from_west, from_east = three_b(epack_b), three_b(wpack_b), spots_b(rw_b), spots_b(re_b)
    wires_b = near.wire(
        npack_b, spack_b, east, west, rn_b.at[:, into, :], rs_b.at[:, into, :], from_west, from_east, send_b, recv_b)
    near.start(wires_b, east, west, from_west, from_east)

    def around(ref, turned, key, k, base, ring_size):
        here, above, below = pl.ds(base, 8), pl.ds(base + 1, 8), pl.ds(base - 1, 8)

        def ring(k):
            if (key, k) not in turned:
                tile = ref[k, here, :]
                turned[key, k] = (tile, pltpu.roll(tile, 128 - LEVELS, 1), pltpu.roll(tile, LEVELS, 1))
            return turned[key, k]

        tile, left, right = ring(k)
        east = jnp.where(lane < 128 - LEVELS, left, ring((k + 1) % ring_size)[1])
        west = jnp.where(lane < LEVELS, ring((k - 1) % ring_size)[2], right)
        return tile, east, west, ref[k, above, :], ref[k, below, :]

    def at_tile(e):
        return 8 * e if isinstance(e, int) else pl.multiple_of(8 * e, 8)

    def weigh(base, tiles, same, ring_size=RING):
        turned = {}
        for k in tiles:
            w, we, ww, wn, ws = around(wet, turned, "wet", k, base, ring_size)
            total = w * ((we + ww) + (wn + ws))
            for to in same:
                count[k, to:to + 8, :] = total

    def mask(e, which):
        base = at_tile(e)
        rows, here = pl.ds(base - PAD, 8), pl.ds(base, 8)
        for k in inside:
            w = wet[k, here, :]
            for f in which:
                field[f, k, here, :] = raw[f, rows, 128 * k:128 * k + 128] * w

    def first(base, tiles, which, ring_size, whole=True):
        here = pl.ds(base, 8)
        turned = {}
        for k in tiles:
            w, total = wet[k, here, :], count[k, here, :]
            full = whole and k < TILES
            if full:
                mixing = wide_k[k, here, :] + wide_b[k, here, :] * total
                zonal_own = 0.05 * field[2, k, here, :]
                merid_own = 0.05 * field[3, k, here, :]
            for f in which:
                c, fe, fw, fn, fs = around(field.at[f], turned, f, k, base, ring_size)
                lap = w * ((fe + fw) + (fn + fs)) - total * c
                once[f, k, here, :] = lap
                if full:
                    part[f, k, here, :] = (
                        c - (zonal_own * (fe - fw) + merid_own * (fn - fs))) + mixing * lap

    def second(e, tiles, which, ring_size):
        base = at_tile(e)
        here, rows = pl.ds(base, 8), pl.ds(base - PAD, 8)
        turned = {}
        for k in tiles:
            fade = wide_b[k, here, :] * wet[k, here, :]
            for f in which:
                _, le, lw, ln, ls = around(once.at[f], turned, f, k, base, ring_size)
                results[f][rows, 128 * k:128 * k + 128] = (
                    part[f, k, here, :] - fade * ((le + lw) + (ln + ls)))

    def by_three(low, high, step):
        def body(i, carry):
            for j in range(3):
                step(low + 3 * i + j)
            return carry
        lax.fori_loop(0, (high - low) // 3, body, 0)

    def turn(f, tile_lane=None):
        at = lane if tile_lane is None else tile_lane
        return (at - 16 * f + 32 + 128) % 128

    def bring(f, last, begin):
        return jnp.where(turn(f) < 64, pltpu.roll(last, 16 * f, 1), pltpu.roll(begin, 64 + 16 * f, 1))

    def bring_field(base):
        here = pl.ds(base, 8)
        for f in flows:
            end_field[f - 2, here, :] = bring(f, field[f, TILES - 1, here, :], field[f, 0, here, :])

    def bring_rest(e):
        base = at_tile(e)
        here = pl.ds(base, 8)
        bring_field(base)
        for i in range(2):
            flow = 0.05 * end_field[i, here, :]
            end_own[i, i, here, :] = flow
            end_own[1 - i, i, here, :] = pltpu.roll(flow, 112 if i else 16, 1)
        for src, to in ((wide_k, end_k), (wide_b, end_b)):
            tile = bring(2, src[TILES - 1, here, :], src[0, here, :])
            to[0, here, :] = tile
            to[1, here, :] = pltpu.roll(tile, 16, 1)

    for f in flows:
        for k in inside:
            for ref in (field, once):
                ref[f, k, PAD - 8:PAD, :] = jnp.zeros((8, 128), f32)
                ref[f, k, PAD + ROWS:PAD + ROWS + 8, :] = jnp.zeros((8, 128), f32)
    by_three(2, end, lambda e: mask(e, (0, 1, 2, 3)))
    by_three(2, end, lambda e: first(at_tile(e), inside, flows, TILES))
    by_three(2, end, lambda e: second(e, inside, flows, TILES))
    for e in range(2, end):
        bring_rest(e)
    for half in range(2):
        width = span if half == 0 else LANES - span
        pieces = halves(un[:, span * half:span * half + width]) + halves(vn[:, span * half:span * half + width])
        means = jnp.dot(jnp.concatenate(pieces, axis=0), pick[0:width, :], preferred_element_type=f32)
        for i in range(2):
            mean[i, half] = means[256 * i:256 * i + ROWS] + means[256 * i + 128:256 * i + 128 + ROWS]

    near.arrived(wires)

    @pl.when(near.x == 0)
    def _():
        rs[:, 8:16, :] = jnp.zeros((RING // 2, 8, 128), f32)
        rw[64:72, :] = jnp.zeros((8, 128), f32)
        re[64:72, :] = jnp.zeros((8, 128), f32)

    swap = lane + 8 - 16 * ((lane // 8) % 2)

    def mirror_rows(ref, sign):
        turned = [sign * row_xor(pick_lanes(ref[m, 8:16, :], lane + 120 - 16 * (lane // 8)), 1) for m in range(RING // 2)]
        tail = pick_lanes(ref[RING // 2 - 1, 8:16, :], lane + 96 - 64 * (lane // 32))
        for m in range(RING // 2):
            lower = turned[RING // 2 - 1 - m]
            upper = turned[RING // 2 - 2 - m] if m < RING // 2 - 1 else tail
            ref[m, 8:16, :] = jnp.where(sub < 4, lower, upper)

    @pl.when(near.top)
    def _():
        mirror_rows(rn, -1.0)
        for got, low, off in ((rw, 80, 16), (re, 32, -16)):
            index = jnp.where(jnp.logical_and(lane >= low, lane < low + 32), swap + off, 8)
            tile = turn_rows(pick_lanes(got[72:80, :], index))
            got[72:80, :] = jnp.where(lane < 16, tile, -tile)

    halo_flags = []
    for got, base in ((rs, PAD - 8), (rn, PAD + ROWS)):
        flag = [jnp.broadcast_to(got[RING // 2 - 1, 12:13, 32 * j:32 * j + 1], (8, 128)) for j in range(4)]
        halo_flags.append(flag)
        for k in inside:
            low, high = (128 * k) // (BLOCK * LEVELS), (128 * k + 127) // (BLOCK * LEVELS)
            value = flag[low]
            if low != high:
                value = jnp.where(lane < BLOCK * LEVELS * high - 128 * k, value, flag[high])
            wet[k, base:base + 8, :] = value

    def halo_rows(which, south, north):
        for i, f in enumerate(which):
            for k in inside:
                row = 8 + 4 * (k % 2) + 2 * i
                field[f, k, PAD - 8:PAD, :] = south[k // 2, row - 6:row + 2, :]
                field[f, k, PAD + ROWS:PAD + ROWS + 8, :] = north[k // 2, row:row + 8, :]

    halo_rows(flows, rs, rn)

    for e in (1, end):
        bring_field(8 * e)
    for e in range(1, end + 1):
        here = slice(8 * e, 8 * e + 8)
        at = 64 if e == 1 else 72 if e == end else 8 * ((e - 2) % 8)
        east, west = re[at:at + 8, :], rw[at:at + 8, :]
        further = e == 1 or 10 <= e < end
        wet_east = jnp.broadcast_to(east[:, 8 * further:8 * further + 1], (8, 128))
        wet_west = jnp.broadcast_to(west[:, 8 * further:8 * further + 1], (8, 128))
        wet_beyond[0, here, :] = wet_east
        wet_beyond[1, here, :] = wet_west
        if further:
            east, west = pltpu.roll(east, 64, 1), pltpu.roll(west, 64, 1)
        last, begin = wet[TILES - 1, here, :], wet[0, here, :]
        for f in flows:
            at = turn(f)
            end_wet[f - 2, here, :] = jnp.where(
                at < 64, jnp.where(at < 32, last, wet_east), jnp.where(at < 96, wet_west, begin))
            end_side[f - 2, here, :] = jnp.where(
                at < 64, last + jnp.where(at < 24, last, wet_east), begin + jnp.where(at < 104, wet_west, begin))
            end_field[f - 2, here, :] = jnp.where(
                at // 16 == 2, east, jnp.where(at // 16 == 5, west, end_field[f - 2, here, :]))
    for base in range(PAD - 1, PAD + ROWS + 1, 8):
        here, above, below = slice(base, base + 8), slice(base + 1, base + 9), slice(base - 1, base + 7)
        for i in range(2):
            w = end_wet[i, here, :]
            total = w * (end_side[i, here, :] + (end_wet[i, above, :] + end_wet[i, below, :]))
            c, fn, fs = end_field[i, here, :], end_field[i, above, :], end_field[i, below, :]
            fe, fw = pltpu.roll(c, 128 - LEVELS, 1), pltpu.roll(c, LEVELS, 1)
            lap = w * ((fe + fw) + (fn + fs)) - total * c
            end_once[i, here, :] = lap
            end_part[i, here, :] = (
                c - (end_own[i, 0, here, :] * (fe - fw) + end_own[i, 1, here, :] * (fn - fs))
            ) + (end_k[i, here, :] + end_b[i, here, :] * total) * lap
    for e in range(2, end):
        here = slice(8 * e, 8 * e + 8)
        for i in range(2):
            lap = end_once[i, here, :]
            total = (pltpu.roll(lap, 128 - LEVELS, 1) + pltpu.roll(lap, LEVELS, 1)) + (
                end_once[i, 8 * e + 1:8 * e + 9, :] + end_once[i, 8 * e - 1:8 * e + 7, :])
            end_new[i, 8 * e - PAD:8 * e - PAD + 8, :] = (
                end_part[i, here, :] - end_b[i, here, :] * end_wet[i, here, :] * total)

    def sides(ref, k, south, north):
        return jnp.where(sub < 4, ref[k, south:south + 8, :], ref[k, north:north + 8, :])

    def along(tiles, k):
        if k not in tiles[1]:
            tile = tiles[0](k)
            tiles[1][k] = (tile, pltpu.roll(tile, 128 - LEVELS, 1), pltpu.roll(tile, LEVELS, 1))
        return tiles[1][k]

    def along_row(tiles, k):
        tile, left, right = along(tiles, k)
        return (
            tile,
            jnp.where(lane < 128 - LEVELS, left, along(tiles, (k + 1) % TILES)[1]),
            jnp.where(lane < LEVELS, along(tiles, (k - 1) % TILES)[2], right),
        )

    def put(ref, k, south, north, value):
        ref[k, south:south + 4, :] = value[0:4]
        ref[k, north:north + 8, :] = jnp.where(sub < 4, ref[k, north:north + 8, :], value)

    low, high = PAD - 2, PAD + ROWS - 6
    wets = (lambda k: sides(wet, k, low, high), {})
    states = [(lambda k, f=f: sides(field.at[f], k, low, high), {}) for f in flows]
    for k in inside:
        w, we, ww = along_row(wets, k)
        total = w * ((we + ww) + (sides(wet, k, low + 1, high + 1) + sides(wet, k, low - 1, high - 1)))
        mixing = sides(wide_k, k, low, high) + sides(wide_b, k, low, high) * total
        zonal_own, merid_own = 0.05 * along(states[0], k)[0], 0.05 * along(states[1], k)[0]
        for i, f in enumerate(flows):
            c, fe, fw = along_row(states[i], k)
            fn, fs = sides(field.at[f], k, low + 1, high + 1), sides(field.at[f], k, low - 1, high - 1)
            lap = w * ((fe + fw) + (fn + fs)) - total * c
            put(once.at[f], k, low, high, lap)
            put(part.at[f], k, low, high, (c - (zonal_own * (fe - fw) + merid_own * (fn - fs))) + mixing * lap)
    low, high = PAD, PAD + ROWS - 8
    laps = [(lambda k, f=f: sides(once.at[f], k, low, high), {}) for f in flows]
    for k in inside:
        at = slice(128 * k, 128 * k + 128)
        fade = sides(wide_b, k, low, high) * sides(wet, k, low, high)
        for i, (f, new) in enumerate(zip(flows, (un, vn))):
            _, le, lw = along_row(laps[i], k)
            ln, ls = sides(once.at[f], k, low + 1, high + 1), sides(once.at[f], k, low - 1, high - 1)
            value = sides(part.at[f], k, low, high) - fade * ((le + lw) + (ln + ls))
            new[0:8, at] = jnp.where(sub < 4, value, new[0:8, at])
            new[ROWS - 8:ROWS, at] = jnp.where(sub < 4, new[ROWS - 8:ROWS, at], value)

    for half in range(2):
        width = span if half == 0 else LANES - span
        at = slice(span * half, span * half + width)
        pieces = []
        for new in (un, vn):
            pieces += halves(jnp.concatenate([new[0:8, at], new[ROWS - 8:ROWS, at]], axis=0))
        means = jnp.dot(jnp.concatenate(pieces, axis=0), pick[0:width, :], preferred_element_type=f32)
        for i in range(2):
            value = means[32 * i:32 * i + 16] + means[32 * i + 16:32 * i + 32]
            mean[i, half, 0:8, :] = value[0:8]
            mean[i, half, ROWS - 8:ROWS, :] = value[8:16]
    for i in range(2):
        means = jnp.dot(
            jnp.concatenate(halves(end_new[i]), axis=0), end_pick[i], preferred_element_type=f32)
        value = means[0:ROWS] + means[128:128 + ROWS]
        mean[i, 0] = jnp.where(lane_c < 2, value[:, 0:128], mean[i, 0])
        mean[i, 1] = jnp.where(lane_c // 2 == (COLS - 2 - 128) // 2, value[:, 128:256], mean[i, 1])
        for half in range(2):
            plane[i, half, own, :] = base_plane[i, half] + mean[i, half]

    for pack, side, shift in ((wpack2, 0, 0), (epack2, 1, 24)):
        for r in range(2):
            packed = jnp.zeros((8, 128), f32)
            for g in range(8 - r):
                rows = slice(PAD + 16 * g + 8 * r, PAD + 16 * g + 8 * r + 8)
                for p in range(2):
                    turned = pltpu.roll(plane[p, side, rows, :], (16 * g + 8 * p + shift) % 128, 1)
                    packed = jnp.where(lane // 8 == 2 * g + p, turned, packed)
            pack[8 * r:8 * r + 8, :] = packed

    def three2(ref):
        return ref, ref.at[pl.ds(0, 8)], ref.at[pl.ds(0, 8)]

    def spots2(ref):
        return ref.at[pl.ds(0, 16)], ref.at[pl.ds(16, 8)], ref.at[pl.ds(24, 8)]

    for p in range(2):
        for half in range(2):
            npack2[p, half] = plane[p, half, PAD + ROWS - 8:PAD + ROWS, :]
            spack2[p, half] = plane[p, half, PAD:PAD + 8, :]
    east, west, from_west, from_east = three2(epack2), three2(wpack2), spots2(rw2), spots2(re2)
    wires2 = near.wire(npack2, spack2, east, west, rn2, rs2, from_west, from_east, send2, recv2)
    near.start(wires2, east, west, from_west, from_east)

    for e in range(2, end):
        rows = slice(8 * e - PAD, 8 * e - PAD + 8)
        for i in range(2):
            tile, new, f = end_new[i, rows, :], (un, vn)[i], i + 2
            begin = pltpu.roll(tile, (64 - 16 * f) % 128, 1)
            last = pltpu.roll(tile, 128 - 16 * f, 1)
            new[rows, 0:128] = jnp.where(lane < 16, begin, new[rows, 0:128])
            new[rows, LANES - 128:LANES] = jnp.where(lane >= 112, last, new[rows, LANES - 128:LANES])

    near.arrived(wires_b)

    @pl.when(near.x == 0)
    def _():
        rs_b[:, 8:16, :] = jnp.zeros((RING // 2 + 2, 8, 128), f32)
        rw_b[0:8, :] = jnp.zeros((8, 128), f32)
        re_b[0:8, :] = jnp.zeros((8, 128), f32)

    @pl.when(near.top)
    def _():
        mirror_rows(rn_b, 1.0)
        mirror = (2 * COLS - 241 - lane) % 128
        start = turn_rows(pick_lanes(rn_b[RING // 2 + 1, 8:16, :], mirror))
        last = turn_rows(pick_lanes(rn_b[RING // 2, 8:16, :], mirror))
        rn_b[RING // 2, 8:16, :] = jnp.where(lane < 112, start, last)
        rn_b[RING // 2 + 1, 8:16, :] = jnp.where(lane < 112, last, start)
        index = jnp.where(
            lane < 8, 71 - lane, jnp.where(jnp.logical_and(lane >= 48, lane < 80), swap - 48, 100))
        rw_b[ROWS + 8:ROWS + 16, :] = turn_rows(pick_lanes(rw_b[ROWS + 8:ROWS + 16, :], index))
        index = jnp.where(lane < 64, swap + 48, jnp.where(lane < 72, 71 - lane, 20))
        re_b[ROWS + 8:ROWS + 16, :] = turn_rows(pick_lanes(re_b[ROWS + 8:ROWS + 16, :], index))

    halo_rows(tracers, rs_b, rn_b)
    west, east = rw_b[...], re_b[...]
    wet_east, wet_west = wet_beyond[0, ends, :], wet_beyond[1, ends, :]
    wet[TILES, ends, :] = jnp.where(lane_h < 64, wet_east, wet_west)
    for f in tracers:
        right = pltpu.roll(east, 128 - 16 * f, 1) if f else east
        field[f, TILES, ends, :] = jnp.where(lane_h < 64, right, pltpu.roll(west, 64 - 16 * f, 1))
    for e in (1, 2, end - 1, end):
        weigh(8 * e, everywhere, (8 * e,))
    weigh(8 * 3, rim, [8 * e for e in early[1:]])
    weigh(8 * middle, rim, (8 * middle,))
    weigh(8 * (middle + 1), rim, [8 * e for e in late[:-1]])
    for e in (1, end):
        first(8 * e, everywhere, tracers, RING, whole=False)
    by_three(2, end, lambda e: first(at_tile(e), everywhere, tracers, RING))
    by_three(2, end, lambda e: second(e, inside, tracers, RING))

    for (got, flag), at in zip(((rs_b, halo_flags[0]), (rn_b, halo_flags[1])), (PAD - 8, PAD + ROWS)):
        for half in range(2):
            plane[2, half, at:at + 8, :] = got[RING // 2 + half, 8:16, :]
        plane[3, 0, at:at + 8, :] = jnp.where(
            lane < BLOCK, flag[0], jnp.where(lane < 2 * BLOCK, flag[1], flag[2]))
        plane[3, 1, at:at + 8, :] = jnp.where(lane < 3 * BLOCK - 128, flag[2], flag[3])
    for p, beyond in (
        (2, jnp.where(lane_h < 120, pltpu.roll(east, 48, 1), pltpu.roll(west, 120, 1))),
        (3, jnp.where(lane_h < 120, wet_east, wet_west)),
    ):
        plane[p, 1, ends, :] = jnp.where(lane_h < 112, plane[p, 1, ends, :], beyond)

    def column_on(tiles):
        turned = [pltpu.roll(tile, 127, 1) for tile in tiles]
        return [jnp.where(lane < 127, turned[half], turned[1 - half]) for half in range(2)]

    for e in range(1, end + 1):
        here = slice(8 * e, 8 * e + 8)
        for half in range(2):
            plane[3, half, here, :] = 0.3 * plane[3, half, here, :]
        for p, to in ((0, 0), (3, 1)):
            if p or 1 < e < end:
                for half, tile in enumerate(column_on([plane[p, half, here, :] for half in range(2)])):
                    shifted[to, half, here, :] = tile

    near.arrived(wires2)

    @pl.when(near.x == 0)
    def _():
        rs2[...] = jnp.zeros(rs2.shape, f32)
        rw2[16:24, :] = jnp.zeros((8, 128), f32)
        re2[16:24, :] = jnp.zeros((8, 128), f32)

    @pl.when(near.top)
    def _():
        for p in range(2):
            start = -turn_rows(pick_lanes(rn2[p, 1], (239 - lane) % 128))
            last = -turn_rows(pick_lanes(rn2[p, 0], (239 - lane) % 128))
            rn2[p, 0] = jnp.where(lane < 112, start, last)
            rn2[p, 1] = jnp.where(lane < 112, last, start)
        for got in (rw2, re2):
            got[24:32, :] = -turn_rows(pick_lanes(got[24:32, :], 112 + (lane // 8 % 2) * 8 + 7 - lane % 8))

    for got, at in ((rs2, PAD - 8), (rn2, PAD + ROWS)):
        for half, tile in enumerate(column_on([got[0, half] for half in range(2)])):
            shifted[0, half, at:at + 8, :] = tile
            plane[1, half, at:at + 8, :] = got[1, half]
    for e in range(1, end + 1):
        here = slice(8 * e, 8 * e + 8)
        g = 7 if e == 1 else 0 if e == end else (e - 2) // 2
        at = 16 if e == 1 else 24 if e == end else 8 * (e % 2)
        for p, off in ((0, 1), (1, 0)):
            beyond = jnp.where(
                lane < 120 - off,
                pltpu.roll(re2[at:at + 8, :], (112 - 16 * g - 8 * p - off) % 128, 1),
                pltpu.roll(rw2[at:at + 8, :], (120 - 16 * g - 8 * p - off) % 128, 1))
            ref = plane.at[1, 1] if p else shifted.at[0, 1]
            theirs = jnp.logical_and(lane >= 112 - off, lane < 128 - off)
            ref[here, :] = jnp.where(theirs, beyond, ref[here, :])

    def apart(tiles, ahead):
        turned = [pltpu.roll(tile, 126 if ahead else 2, 1) for tile in tiles]
        if ahead:
            return [jnp.where(lane < 126, turned[half], turned[1 - half]) - tiles[half] for half in range(2)]
        return [tiles[half] - jnp.where(lane < 2, turned[1 - half], turned[half]) for half in range(2)]

    def rows_apart(p, half, e):
        return plane[p, half, 8 * e + 1:8 * e + 9, :] - plane[p, half, 8 * e - 1:8 * e + 7, :]

    for n in range(NSUB):
        for e in range(1, end + 1):
            here = slice(8 * e, 8 * e + 8)
            slope = apart([shifted[0, half, here, :] for half in range(2)], False)
            for half in range(2):
                flow = slope[half] + rows_apart(1, half, e)
                plane[2, half, here, :] = plane[2, half, here, :] - plane[3, half, here, :] * flow
        inner = 1 if n == NSUB - 1 else 0
        for e in range(1 + inner, end + 1 - inner):
            here = slice(8 * e, 8 * e + 8)
            slope = apart([plane[2, half, here, :] for half in range(2)], True)
            for half in range(2):
                shifted[0, half, here, :] = shifted[0, half, here, :] - shifted[1, half, here, :] * slope[half]
                plane[1, half, here, :] = plane[1, half, here, :] - plane[3, half, here, :] * rows_apart(2, half, e)
    for e in range(2, end):
        here = slice(8 * e, 8 * e + 8)
        turned = [pltpu.roll(shifted[0, half, here, :], 1, 1) for half in range(2)]
        for half in range(2):
            plane[0, half, here, :] = jnp.where(lane < 1, turned[1 - half], turned[half])
    for half, width in ((0, 128), (1, COLS - 128)):
        at = slice(128 * half, 128 * half + 128)
        du[:, at] = plane[0, half, own, :] - mean[0, half]
        dv[:, at] = plane[1, half, own, :] - mean[1, half]
        at = slice(128 * half, 128 * half + width)
        for p, ref in ((0, zonal), (1, merid), (2, height)):
            ref[:, at] = plane[p, half, own, 0:width]
    near.sent(wires, wires_b, wires2)


def finish_kernel(
    tn, sn, un, vn, du, dv, height, zonal, merid,
    t_out, s_out, u_out, v_out, height_out, zonal_out, merid_out, done, sems,
):
    copies = [
        pltpu.make_async_copy(src, dst, sems.at[i])
        for i, (src, dst) in enumerate(
            ((tn, t_out), (sn, s_out), (height, height_out), (zonal, zonal_out), (merid, merid_out)))
    ]
    for copy in copies:
        copy.start()
    step = 24
    for i in range(ROWS // step):
        for f, (new, change, out) in enumerate(((un, du, u_out), (vn, dv, v_out))):
            for r in range(step * i, step * i + step, 8):
                for half in range(2):
                    tile = change[r:r + 8, 128 * half:128 * half + 128]
                    for k in range(8 * half, min(8 * half + 8, TILES)):
                        at = slice(128 * k, 128 * k + 128)
                        done[f, r:r + 8, at] = new[r:r + 8, at] + expand(tile, k % 8)
            rows = pl.ds(step * i, step)
            copies.append(pltpu.make_async_copy(done.at[f, rows, :], out.at[rows, :], sems.at[5 + 2 * i + f]))
            copies[-1].start()
    for copy in copies:
        copy.wait()


def per_device(nb, nw, t, s, u, v, elev, zavg, mavg, flags, sel, ktab, btab):
    f32 = jnp.float32
    vmem = pl.BlockSpec(memory_space=pltpu.VMEM)
    hbm = pl.BlockSpec(memory_space=pl.ANY)
    scratch = lambda *shape: pltpu.VMEM(shape, f32)
    dma = lambda *shape: pltpu.SemaphoreType.DMA(shape)
    parts = pl.pallas_call(
        functools.partial(step_kernel, nb, nw),
        out_shape=(pltpu.VMEM((ROWS, LANES), f32),) * 2
        + (pltpu.VMEM((ROWS + 8, LANES), f32),) * 2
        + (pltpu.VMEM((ROWS, 256), f32),) * 2
        + (pltpu.VMEM((ROWS, COLS), f32),) * 3,
        in_specs=[hbm] * 11,
        out_specs=(vmem,) * 9,
        scratch_shapes=[
            pltpu.SMEM((2, 4), jnp.int32),
            pltpu.SMEM((8,), f32),
            pltpu.SMEM((8,), f32),
            pltpu.VMEM((ROWS, COLS), jnp.int32),
            scratch(ROWS, COLS), scratch(ROWS, COLS), scratch(ROWS, COLS),
            scratch(2, 2, 8, LANES), scratch(2, 2, ROWS, 128), scratch(4, ROWS, LANES),
            scratch(RING // 2, 8, 128), scratch(RING // 2, 8, 128), scratch(64, 128), scratch(64, 128),
            scratch(RING // 2, 24, 128), scratch(RING // 2, 24, 128), scratch(80, 128), scratch(80, 128),
            scratch(RING // 2 + 2, 8, 128), scratch(RING // 2 + 2, 8, 128), scratch(ROWS, 128), scratch(ROWS, 128),
            scratch(RING // 2 + 2, 24, 128), scratch(RING // 2 + 2, 24, 128),
            scratch(ROWS + 16, 128), scratch(ROWS + 16, 128),
            scratch(4, RING, BAND, 128), scratch(4, RING, BAND, 128), scratch(4, TILES, BAND, 128),
            scratch(RING, BAND, 128), scratch(RING, BAND, 128),
            scratch(TILES, BAND, 128), scratch(TILES, BAND, 128),
            pltpu.VMEM((128 * LEVELS, 128), jnp.bfloat16), pltpu.VMEM((2, 128, 256), jnp.bfloat16),
            pltpu.VMEM((256, 128 * LEVELS), jnp.bfloat16),
            scratch(2, 2, ROWS, 128), scratch(2, 2, ROWS, 128),
            scratch(2, BAND, 128), scratch(2, 2, BAND, 128), scratch(2, BAND, 128), scratch(2, BAND, 128),
            scratch(2, BAND, 128), scratch(2, BAND, 128), scratch(2, BAND, 128), scratch(2, BAND, 128),
            scratch(2, 128, 128), scratch(2, BAND, 128), scratch(2, 2, BAND, 128),
            scratch(4, 2, BAND, 128), scratch(2, 2, 8, 128), scratch(2, 2, 8, 128), scratch(16, 128), scratch(16, 128),
            scratch(2, 2, 8, 128), scratch(2, 2, 8, 128), scratch(32, 128), scratch(32, 128),
            dma(15), dma(4), dma(8), dma(8), dma(8), dma(8), dma(8), dma(8),
        ],
        compiler_params=pltpu.CompilerParams(
            collective_id=0, has_side_effects=True, vmem_limit_bytes=VMEM_BYTES),
        name="step",
    )(flags, ktab, btab, sel, t, s, u, v, zavg, mavg, elev)
    parts = [pltpu.with_memory_space_constraint(part, pltpu.VMEM) for part in parts]

    big = jax.ShapeDtypeStruct((ROWS, LANES), f32)
    flat = jax.ShapeDtypeStruct((ROWS, COLS), f32)
    return pl.pallas_call(
        finish_kernel,
        out_shape=(big,) * 4 + (flat,) * 3,
        in_specs=[vmem] * 9,
        out_specs=(hbm,) * 7,
        scratch_shapes=[scratch(2, ROWS, LANES), dma(15)],
        compiler_params=pltpu.CompilerParams(vmem_limit_bytes=VMEM_BYTES),
        name="finish",
    )(*parts)


def solution(mesh):
    grid = P("wide", "blocks")
    return jax.shard_map(
        functools.partial(per_device, mesh.shape["blocks"], mesh.shape["wide"]),
        mesh=mesh,
        in_specs=(grid,) * 9 + (P(), P()),
        out_specs=(grid,) * 7,
        check_vma=False,
    )
```

```python
import functools

import jax
import jax.numpy as jnp
from jax import lax
from jax.experimental import pallas as pl
from jax.experimental.pallas import tpu as pltpu
from jax.sharding import PartitionSpec as P

BLOCK = 60
LEVELS = 8
NSUB = 4
ROWS = 120
COLS = 240
LANES = COLS * LEVELS
TILES = LANES // 128
RING = TILES + 1
PAD = 16
BAND = ROWS + 2 * PAD
MESH = pl.DeviceIdType.MESH
VMEM_BYTES = 56 * 1024 * 1024


def lanes_of(shape=(8, 128)):
    return lax.broadcasted_iota(jnp.int32, shape, 1)


def rows_of(shape=(8, 128)):
    return lax.broadcasted_iota(jnp.int32, shape, 0)


def pick_lanes(tile, index):
    return jnp.take_along_axis(tile, index, axis=1, mode="promise_in_bounds")


def turn_rows(rows):
    turned = jnp.broadcast_to(rows[7:8, :], (8, 128))
    for i in range(1, 8):
        turned = jnp.where(rows_of() == i, jnp.broadcast_to(rows[7 - i:8 - i, :], (8, 128)), turned)
    return turned


class Neighbours:
    def __init__(self, nb, nw):
        b, x = lax.axis_index("blocks"), lax.axis_index("wide")
        self.b, self.x = b, x
        self.top, self.inner, self.above = x == nw - 1, x < nw - 1, x > 0
        first, last = b == 0, b == nb - 1
        self.east, self.west = jnp.where(last, 0, b + 1), jnp.where(first, nb - 1, b - 1)
        self.fold = nb - 1 - b
        self.fold_east = jnp.where(last, nb - 1, nb - 2 - b)
        self.fold_west = jnp.where(first, 0, nb - b)
        self.own_east = jnp.logical_and(self.top, self.fold_east == b)
        self.own_west = jnp.logical_and(self.top, self.fold_west == b)
        self.far_east = jnp.logical_and(self.top, self.fold_east != b)
        self.far_west = jnp.logical_and(self.top, self.fold_west != b)

    def greet(self):
        sem = pltpu.get_barrier_semaphore()

        def greet(b, x):
            pl.semaphore_signal(sem, inc=1, device_id=(b, x), device_id_type=MESH)

        b, x = self.b, self.x

        @pl.when(self.far_east)
        def _():
            greet(self.fold_east, x)

        @pl.when(self.far_west)
        def _():
            greet(self.fold_west, x)

        @pl.when(self.inner)
        def _():
            greet(self.east, x + 1)
            greet(self.west, x + 1)

        @pl.when(self.above)
        def _():
            greet(self.east, x - 1)
            greet(self.west, x - 1)

        @pl.when(self.top)
        def _():
            greet(self.fold, x)

        greet(self.east, x)
        greet(self.west, x)

        @pl.when(self.inner)
        def _():
            greet(b, x + 1)

        @pl.when(self.above)
        def _():
            greet(b, x - 1)

    def meet(self):
        sem = pltpu.get_barrier_semaphore()
        x = self.x
        own = jnp.logical_or(self.own_east, self.own_west)

        @pl.when(x == 0)
        def _():
            pl.semaphore_wait(sem, 5)

        @pl.when(own)
        def _():
            pl.semaphore_wait(sem, 7)

        @pl.when(jnp.logical_and(self.above, jnp.logical_not(own)))
        def _():
            pl.semaphore_wait(sem, 8)

    def wire(self, north, south, east, west, rn, rs, rw, re, send, recv):
        b, x = self.b, self.x

        def c(src, dst, way, slot, to_b, to_x):
            return pltpu.make_async_remote_copy(
                src_ref=src, dst_ref=dst, send_sem=send.at[way], recv_sem=recv.at[slot],
                device_id=(to_b, to_x), device_id_type=MESH)

        return dict(
            always=[
                c(east[0], rw[0], 0, 0, self.east, x),
                c(west[0], re[0], 1, 1, self.west, x),
            ],
            corner_inner=[
                c(east[1], rw[1], 4, 4, self.east, x + 1),
                c(west[1], re[1], 5, 5, self.west, x + 1),
            ],
            corner_above=[
                c(east[2], rw[2], 6, 6, self.east, x - 1),
                c(west[2], re[2], 7, 7, self.west, x - 1),
            ],
            inner=[c(north, rs, 2, 2, b, x + 1)],
            above=[c(south, rn, 3, 3, b, x - 1)],
            top=[c(north, rn, 2, 3, self.fold, x)],
            far_east=[c(east[1], re[2], 4, 7, self.fold_east, x)],
            far_west=[c(west[1], rw[2], 5, 6, self.fold_west, x)],
        )

    def start(self, wires, east, west, rw, re):
        def go(name, cond):
            @pl.when(cond)
            def _():
                for copy in wires[name]:
                    copy.start()

        go("far_east", self.far_east)
        go("far_west", self.far_west)
        go("corner_inner", self.inner)
        go("corner_above", self.above)
        go("top", self.top)
        for copy in wires["always"]:
            copy.start()
        go("inner", self.inner)
        go("above", self.above)

        @pl.when(self.own_east)
        def _():
            re[2][...] = east[1][...]

        @pl.when(self.own_west)
        def _():
            rw[2][...] = west[1][...]

    def arrived(self, wires):
        w = wires
        for copy in w["always"]:
            copy.wait_recv()
        w["top"][0].wait_recv()

        @pl.when(self.above)
        def _():
            for copy in w["inner"] + w["corner_inner"]:
                copy.wait_recv()

        @pl.when(jnp.logical_not(self.own_east))
        def _():
            w["far_east"][0].wait_recv()

        @pl.when(jnp.logical_not(self.own_west))
        def _():
            w["far_west"][0].wait_recv()

    def sent(self, *every):
        for w in every:
            for copy in w["always"]:
                copy.wait_send()
            w["top"][0].wait_send()

        @pl.when(self.above)
        def _():
            for w in every:
                for copy in w["above"] + w["corner_above"]:
                    copy.wait_send()

        @pl.when(jnp.logical_not(self.own_east))
        def _():
            for w in every:
                w["far_east"][0].wait_send()

        @pl.when(jnp.logical_not(self.own_west))
        def _():
            for w in every:
                w["far_west"][0].wait_send()


def block_row(flags, row, tile):
    low, high = (128 * tile) // (BLOCK * LEVELS), (128 * tile + 127) // (BLOCK * LEVELS)
    value = jnp.full((8, 128), flags[row, low].astype(jnp.float32))
    if low != high:
        value = jnp.where(
            lanes_of() < BLOCK * LEVELS * high - 128 * tile,
            value,
            flags[row, high].astype(jnp.float32),
        )
    return value


def expand(tile, part):
    index = lanes_of() // LEVELS + 16 * part
    return pick_lanes(tile, index)


def halves(values):
    coarse = values.astype(jnp.bfloat16)
    return [coarse, (values - coarse.astype(jnp.float32)).astype(jnp.bfloat16)]


def step_kernel(
    nb, nw, flags_in, ktab_in, btab_in, sel_in, t, s, u, v, zavg_in, mavg_in, elev_in,
    tn, sn, un, vn, du, dv, height, zonal, merid,
    flags, ktab, btab, sel, zavg, mavg, elev,
    edge_rows, edge_cols, raw, npack, spack, wpack, epack, rn, rs, rw, re,
    npack_b, spack_b, wpack_b, epack_b, rn_b, rs_b, rw_b, re_b,
    field, once, part, wet, count, wide_k, wide_b, pick, end_pick, spread_out, mean, base_plane,
    end_field, end_own, end_k, end_b, end_wet, end_side, end_once, end_part, end_new, wet_beyond, end_halo, shifted,
    plane, npack2, spack2, wpack2, epack2, rn2, rs2, rw2, re2,
    small, load, send, recv, send_b, recv_b, send2, recv2,
):
    f32, bf16 = jnp.float32, jnp.bfloat16
    sources = (t, s, u, v)
    results = (tn, sn, un, vn)
    near = Neighbours(nb, nw)
    near.greet()

    tables = [
        pltpu.make_async_copy(src, dst, small.at[i])
        for i, (src, dst) in enumerate(
            ((flags_in, flags), (ktab_in, ktab), (btab_in, btab), (sel_in, sel),
             (elev_in, elev), (zavg_in, zavg), (mavg_in, mavg)))
    ]
    loads = [pltpu.make_async_copy(src, raw.at[f], load.at[f]) for f, src in enumerate(sources)]
    edges = []
    for i, src in enumerate((u, v)):
        for side, at in enumerate((0, ROWS - 8)):
            edges.append(pltpu.make_async_copy(
                src.at[pl.ds(at, 8), :], edge_rows.at[i, side], small.at[7 + 4 * i + side]))
        for side, at in enumerate((0, LANES - 128)):
            edges.append(pltpu.make_async_copy(
                src.at[:, pl.ds(at, 128)], edge_cols.at[i, side], small.at[9 + 4 * i + side]))
    tables[0].start()
    for copy in edges:
        copy.start()
    for copy in tables[1:4]:
        copy.start()
    for f in (2, 3, 0, 1):
        loads[f].start()
    for copy in tables[4:]:
        copy.start()

    lane, sub = lanes_of(), rows_of()
    lane_c, row_c = lanes_of((ROWS, 128)), rows_of((ROWS, 128))
    lane_h = lanes_of((ROWS + 16, 128))
    end = 2 + ROWS // 8
    middle = 2 + BLOCK // 8
    split = BLOCK % 8
    early, late = range(2, middle), range(middle + 1, end)
    flows, tracers = (2, 3), (0, 1)
    inside, everywhere, rim = range(TILES), range(RING), (0, TILES - 1, TILES)
    ends = slice(PAD - 8, PAD + ROWS + 8)
    own = pl.ds(PAD, ROWS)
    span = 128 * LEVELS

    pick[...] = jnp.where(
        lax.broadcasted_iota(jnp.int32, (span, 128), 0) // LEVELS
        == lax.broadcasted_iota(jnp.int32, (span, 128), 1), 1.0 / LEVELS, 0.0).astype(bf16)
    from_lane = lax.broadcasted_iota(jnp.int32, (128, 256), 0)
    to_lane = lax.broadcasted_iota(jnp.int32, (128, 256), 1)
    for i in range(2):
        cell = (from_lane - 16 * (i + 2) + 32 + 128) % 128 // LEVELS
        hit = jnp.logical_or(
            jnp.logical_and(cell - 12 == to_lane, to_lane < 2),
            jnp.logical_and(cell - 2 == to_lane - (COLS - 2), to_lane >= COLS - 2))
        hit = jnp.logical_and(hit, to_lane < COLS)
        end_pick[i] = jnp.where(hit, 1.0 / LEVELS, 0.0).astype(bf16)
    spread_out[...] = jnp.where(
        lax.broadcasted_iota(jnp.int32, (256, span), 0) % 128
        == lax.broadcasted_iota(jnp.int32, (256, span), 1) // LEVELS, 1.0, 0.0).astype(bf16)

    tables[0].wait()
    lows = [block_row(flags, 0, k) for k in inside]
    highs = [block_row(flags, 1, k) for k in inside]


    def beside(tiles, k):
        left = pltpu.roll(tiles[k], 128 - LEVELS, 1)
        next_left = pltpu.roll(tiles[(k + 1) % TILES], 128 - LEVELS, 1)
        right = pltpu.roll(tiles[k], LEVELS, 1)
        last_right = pltpu.roll(tiles[(k - 1) % TILES], LEVELS, 1)
        return jnp.where(lane < 128 - LEVELS, left, next_left) + jnp.where(lane < LEVELS, last_right, right)

    for k in inside:
        low, high = lows[k], highs[k]
        side_low, side_high = beside(lows, k), beside(highs, k)
        count_low, count_high = low * (side_low + (low + low)), high * (side_high + (high + high))
        mixed = jnp.where(sub < split, low, high)
        north = jnp.where(sub < split - 1, low, high)
        south = jnp.where(sub < split + 1, low, high)
        for e in early:
            wet[k, 8 * e:8 * e + 8, :] = low
            count[k, 8 * e:8 * e + 8, :] = count_low
        for e in late:
            wet[k, 8 * e:8 * e + 8, :] = high
            count[k, 8 * e:8 * e + 8, :] = count_high
        wet[k, 8 * middle:8 * middle + 8, :] = mixed
        count[k, 8 * middle:8 * middle + 8, :] = mixed * (
            jnp.where(sub < split, side_low, side_high) + (north + south))


    def pack_rows(packs, both, last):
        tiles = [[], []]
        for m in range(RING // 2):
            for side in range(2):
                packed = last[side]
                for k in (2 * m, 2 * m + 1):
                    if k >= TILES:
                        continue
                    for i in range(2):
                        row = 4 * (k % 2) + 2 * i
                        tile = both(i, side, k)
                        shift = (row + 2 * side) % 8
                        packed = jnp.where(sub // 2 == row // 2, pltpu.roll(tile, shift, 0) if shift else tile, packed)
                w = (lows, highs)[side]
                upper = w[2 * m + 1] if 2 * m + 1 < TILES else jnp.ones((8, 128), f32)
                packs[side][m] = packed * jnp.where(sub < 4, w[2 * m], upper)

    for copy in edges:
        copy.wait()
    tails = []
    for row in range(2):
        tail = jnp.zeros((8, 128), f32)
        for j in range(4):
            tail = jnp.where(lane // 32 == j, flags[row, j].astype(f32), tail)
        tails.append(tail)
    pack_rows((spack, npack), lambda i, side, k: edge_rows[i, side, :, 128 * k:128 * k + 128], tails)
    lane_a, row_a = lanes_of((64, 128)), rows_of((64, 128))
    lane_b = lanes_of((ROWS - 64, 128))
    for side, pack, to in ((0, wpack, 32), (1, epack, 80)):
        col = 3 * side
        w_a = jnp.where(row_a < BLOCK, flags[0, col].astype(f32), flags[1, col].astype(f32))
        w_b = jnp.full((ROWS - 64, 128), flags[1, col].astype(f32))
        parts_of = []
        for rows, at, lanes_in, w in ((slice(0, 64), to, lane_a, w_a), (slice(64, ROWS), (to + 64) % 128, lane_b, w_b)):
            packed = jnp.ones(w.shape, f32)
            for i in range(2):
                shift = (at + 16 * i - 112 * side) % 128
                packed = jnp.where(
                    lanes_in // 16 == at // 16 + i, pltpu.roll(edge_cols[i, side, rows, :], shift, 1), packed)
            parts_of.append(packed * w)
        at = (to + 64) % 128 // 16
        theirs = jnp.logical_or(lane_b // 8 == 1, jnp.logical_or(lane_b // 16 == at, lane_b // 16 == at + 1))
        pack[0:ROWS - 64, :] = jnp.where(theirs, parts_of[1], parts_of[0][0:ROWS - 64])
        pack[ROWS - 64:64, :] = parts_of[0][ROWS - 64:64]

    for copy in tables[1:4]:
        copy.wait()
    for half, width in ((0, 128), (1, COLS - 128)):
        index = sel[:, 128 * half:128 * half + width]
        if width < 128:
            index = jnp.concatenate([index, jnp.zeros((ROWS, 128 - width), jnp.int32)], axis=1)
        kappa = jnp.full(index.shape, ktab[0])
        bihar = jnp.full(index.shape, btab[0])
        for n in range(1, 8):
            hit = index == n
            kappa = jnp.where(hit, ktab[n], kappa)
            bihar = jnp.where(hit, btab[n], bihar)
        for table, to in ((kappa, wide_k), (bihar, wide_b)):
            wide = jnp.dot(
                jnp.concatenate(halves(table), axis=1), spread_out[...], preferred_element_type=f32)
            for k in range(8 * half, min(8 * half + 8, TILES)):
                to[k, own, :] = wide[:, 128 * (k % 8):128 * (k % 8) + 128]

    def around(ref, turned, key, k, base, ring_size):
        here, above, below = pl.ds(base, 8), pl.ds(base + 1, 8), pl.ds(base - 1, 8)

        def ring(k):
            if (key, k) not in turned:
                tile = ref[k, here, :]
                turned[key, k] = (tile, pltpu.roll(tile, 128 - LEVELS, 1), pltpu.roll(tile, LEVELS, 1))
            return turned[key, k]

        tile, left, right = ring(k)
        east = jnp.where(lane < 128 - LEVELS, left, ring((k + 1) % ring_size)[1])
        west = jnp.where(lane < LEVELS, ring((k - 1) % ring_size)[2], right)
        return tile, east, west, ref[k, above, :], ref[k, below, :]

    def at_tile(e):
        return 8 * e if isinstance(e, int) else pl.multiple_of(8 * e, 8)

    def weigh(base, tiles, same, ring_size=RING):
        turned = {}
        for k in tiles:
            w, we, ww, wn, ws = around(wet, turned, "wet", k, base, ring_size)
            total = w * ((we + ww) + (wn + ws))
            for to in same:
                count[k, to:to + 8, :] = total

    def mask(e, which):
        base = at_tile(e)
        rows, here = pl.ds(base - PAD, 8), pl.ds(base, 8)
        for k in inside:
            w = wet[k, here, :]
            for f in which:
                field[f, k, here, :] = raw[f, rows, 128 * k:128 * k + 128] * w

    def first(base, tiles, which, ring_size, whole=True):
        here = pl.ds(base, 8)
        turned = {}
        for k in tiles:
            w, total = wet[k, here, :], count[k, here, :]
            full = whole and k < TILES
            if full:
                mixing = wide_k[k, here, :] + wide_b[k, here, :] * total
                zonal_own = 0.05 * field[2, k, here, :]
                merid_own = 0.05 * field[3, k, here, :]
            for f in which:
                c, fe, fw, fn, fs = around(field.at[f], turned, f, k, base, ring_size)
                lap = w * ((fe + fw) + (fn + fs)) - total * c
                once[f, k, here, :] = lap
                if full:
                    part[f, k, here, :] = (
                        c - (zonal_own * (fe - fw) + merid_own * (fn - fs))) + mixing * lap

    def second(e, tiles, which, ring_size):
        base = at_tile(e)
        here, rows = pl.ds(base, 8), pl.ds(base - PAD, 8)
        turned = {}
        for k in tiles:
            fade = wide_b[k, here, :] * wet[k, here, :]
            for f in which:
                _, le, lw, ln, ls = around(once.at[f], turned, f, k, base, ring_size)
                results[f][rows, 128 * k:128 * k + 128] = (
                    part[f, k, here, :] - fade * ((le + lw) + (ln + ls)))

    def by_three(low, high, step):
        def body(i, carry):
            for j in range(3):
                step(low + 3 * i + j)
            return carry
        lax.fori_loop(0, (high - low) // 3, body, 0)

    def turn(f, tile_lane=None):
        at = lane if tile_lane is None else tile_lane
        return (at - 16 * f + 32 + 128) % 128

    def bring(f, last, begin):
        return jnp.where(turn(f) < 64, pltpu.roll(last, 16 * f, 1), pltpu.roll(begin, 64 + 16 * f, 1))

    def bring_field(base):
        here = pl.ds(base, 8)
        for f in flows:
            end_field[f - 2, here, :] = bring(f, field[f, TILES - 1, here, :], field[f, 0, here, :])

    def bring_rest(e):
        base = at_tile(e)
        here = pl.ds(base, 8)
        bring_field(base)
        for i in range(2):
            flow = 0.05 * end_field[i, here, :]
            end_own[i, i, here, :] = flow
            end_own[1 - i, i, here, :] = pltpu.roll(flow, 112 if i else 16, 1)
        for src, to in ((wide_k, end_k), (wide_b, end_b)):
            tile = bring(2, src[TILES - 1, here, :], src[0, here, :])
            to[0, here, :] = tile
            to[1, here, :] = pltpu.roll(tile, 16, 1)

    early_start = near.b < 2

    def interior():
        for f in flows:
            for k in inside:
                for ref in (field, once):
                    ref[f, k, PAD - 8:PAD, :] = jnp.zeros((8, 128), f32)
                    ref[f, k, PAD + ROWS:PAD + ROWS + 8, :] = jnp.zeros((8, 128), f32)
        by_three(2, end, lambda e: mask(e, (0, 1, 2, 3)))
        by_three(2, end, lambda e: first(at_tile(e), inside, flows, TILES))
        by_three(2, end, lambda e: second(e, inside, flows, TILES))

    def loaded():
        for copy in loads:
            copy.wait()

    @pl.when(early_start)
    def _():
        loaded()
        interior()

    near.meet()
    into = pl.ds(8, 8)

    def three(ref):
        return ref, ref.at[pl.ds(ROWS - 8 - 64, 8)], ref.at[pl.ds(0, 8)]

    def spots(ref):
        return ref.at[pl.ds(0, 64)], ref.at[pl.ds(64, 8)], ref.at[pl.ds(72, 8)]

    east, west, from_west, from_east = three(epack), three(wpack), spots(rw), spots(re)
    wires = near.wire(
        npack, spack, east, west, rn.at[:, into, :], rs.at[:, into, :], from_west, from_east, send, recv)
    near.start(wires, east, west, from_west, from_east)

    for copy in tables[4:]:
        copy.wait()
    for half, width in ((0, 128), (1, COLS - 128)):
        w = jnp.zeros((ROWS, 128), f32)
        for i in range(2):
            for j in range(4):
                here = jnp.logical_and(row_c // BLOCK == i, (lane_c + 128 * half) // BLOCK == j)
                w = jnp.where(here, flags[i, j].astype(f32), w)
        plane[3, half, own, :] = w
        if width < 128:
            plane[2, half, own, :] = jnp.zeros((ROWS, 128), f32)
            base_plane[:, half] = jnp.zeros((2, ROWS, 128), f32)
        at = slice(128 * half, 128 * half + width)
        plane[2, half, own, 0:width] = w[:, 0:width] * elev[:, at]
        base_plane[0, half, :, 0:width] = w[:, 0:width] * zavg[:, at]
        base_plane[1, half, :, 0:width] = w[:, 0:width] * mavg[:, at]

    pl.when(jnp.logical_not(early_start))(loaded)
    pack_rows((spack_b, npack_b), lambda i, side, k: raw[i, (ROWS - 8) * side:(ROWS - 8) * side + 8, 128 * k:128 * k + 128],
              [jnp.zeros((8, 128), f32)] * 2)
    for pack, at in ((spack_b, PAD), (npack_b, PAD + ROWS - 8)):
        for half in range(2):
            pack[RING // 2 + half] = plane[2, half, at:at + 8, :]
    for side, pack in ((0, wpack_b), (1, epack_b)):
        w = wet[(TILES - 1) * side, own, :]
        packed = jnp.zeros((ROWS, 128), f32)
        for f in range(2):
            shift = (16 * f + 64 * side) % 128
            tile = raw[f, :, (LANES - 128) * side:(LANES - 128) * side + 128]
            place = lane_c // 16 == f + 3 * side
            packed = jnp.where(place, pltpu.roll(tile, shift, 1) if shift else tile, packed)
        packed = packed * w
        top = pltpu.roll(plane[2, side, own, :], 24 if side else 64, 1)
        pack[...] = jnp.where(lane_c // 8 == (0 if side else 8), top, packed)

    def three_b(ref):
        return ref, ref.at[pl.ds(ROWS - 8, 8)], ref.at[pl.ds(0, 8)]

    def spots_b(ref):
        return ref.at[pl.ds(8, ROWS)], ref.at[pl.ds(0, 8)], ref.at[pl.ds(ROWS + 8, 8)]

    east, west, from_west, from_east = three_b(epack_b), three_b(wpack_b), spots_b(rw_b), spots_b(re_b)
    wires_b = near.wire(
        npack_b, spack_b, east, west, rn_b.at[:, into, :], rs_b.at[:, into, :], from_west, from_east, send_b, recv_b)
    near.start(wires_b, east, west, from_west, from_east)

    pl.when(jnp.logical_not(early_start))(interior)
    for e in range(2, end):
        bring_rest(e)
    for half in range(2):
        width = span if half == 0 else LANES - span
        pieces = halves(un[:, span * half:span * half + width]) + halves(vn[:, span * half:span * half + width])
        means = jnp.dot(jnp.concatenate(pieces, axis=0), pick[0:width, :], preferred_element_type=f32)
        for i in range(2):
            mean[i, half] = means[256 * i:256 * i + ROWS] + means[256 * i + 128:256 * i + 128 + ROWS]

    near.arrived(wires)

    @pl.when(near.x == 0)
    def _():
        rs[:, 8:16, :] = jnp.zeros((RING // 2, 8, 128), f32)
        rw[64:72, :] = jnp.zeros((8, 128), f32)
        re[64:72, :] = jnp.zeros((8, 128), f32)

    swap = lane + 8 - 16 * ((lane // 8) % 2)

    def mirror_rows(ref, sign):
        turned = [
            sign * pick_lanes(
                jnp.where(sub % 2 == 0, ref[m, 9:17, :], ref[m, 7:15, :]), lane + 120 - 16 * (lane // 8))
            for m in range(RING // 2)
        ]
        tail = pick_lanes(ref[RING // 2 - 1, 8:16, :], lane + 96 - 64 * (lane // 32))
        for m in range(RING // 2):
            lower = turned[RING // 2 - 1 - m]
            upper = turned[RING // 2 - 2 - m] if m < RING // 2 - 1 else tail
            ref[m, 8:16, :] = jnp.where(sub < 4, lower, upper)

    @pl.when(near.top)
    def _():
        mirror_rows(rn, -1.0)
        for got, low, off in ((rw, 80, 16), (re, 32, -16)):
            index = jnp.where(jnp.logical_and(lane >= low, lane < low + 32), swap + off, 8)
            tile = pick_lanes(turn_rows(got.at[72:80, :]), index)
            got[72:80, :] = jnp.where(lane < 16, tile, -tile)

    halo_flags = []
    for got, base in ((rs, PAD - 8), (rn, PAD + ROWS)):
        flag = [jnp.broadcast_to(got[RING // 2 - 1, 12:13, 32 * j:32 * j + 1], (8, 128)) for j in range(4)]
        halo_flags.append(flag)
        for k in inside:
            low, high = (128 * k) // (BLOCK * LEVELS), (128 * k + 127) // (BLOCK * LEVELS)
            value = flag[low]
            if low != high:
                value = jnp.where(lane < BLOCK * LEVELS * high - 128 * k, value, flag[high])
            wet[k, base:base + 8, :] = value

    def halo_rows(which, south, north):
        for i, f in enumerate(which):
            for k in inside:
                row = 8 + 4 * (k % 2) + 2 * i
                field[f, k, PAD - 8:PAD, :] = south[k // 2, row - 6:row + 2, :]
                field[f, k, PAD + ROWS:PAD + ROWS + 8, :] = north[k // 2, row:row + 8, :]

    halo_rows(flows, rs, rn)

    for e in (1, end):
        bring_field(8 * e)
    for e in range(1, end + 1):
        here = slice(8 * e, 8 * e + 8)
        at = 64 if e == 1 else 72 if e == end else 8 * ((e - 2) % 8)
        east, west = re[at:at + 8, :], rw[at:at + 8, :]
        further = e == 1 or 10 <= e < end
        wet_east = jnp.broadcast_to(east[:, 8 * further:8 * further + 1], (8, 128))
        wet_west = jnp.broadcast_to(west[:, 8 * further:8 * further + 1], (8, 128))
        wet_beyond[0, here, :] = wet_east
        wet_beyond[1, here, :] = wet_west
        if further:
            east, west = pltpu.roll(east, 64, 1), pltpu.roll(west, 64, 1)
        end_halo[0, here, :] = east
        end_halo[1, here, :] = west
    for i, f in enumerate(flows):
        at = turn(f)
        last_side = at < 64
        outer = jnp.logical_and(at >= 32, at < 96)
        rim_side = jnp.logical_and(at >= 24, at < 104)
        beyond = jnp.logical_or(at // 16 == 2, at // 16 == 5)
        for e in range(1, end + 1):
            here = slice(8 * e, 8 * e + 8)
            mine = jnp.where(last_side, wet[TILES - 1, here, :], wet[0, here, :])
            theirs = jnp.where(last_side, wet_beyond[0, here, :], wet_beyond[1, here, :])
            end_wet[i, here, :] = jnp.where(outer, theirs, mine)
            end_side[i, here, :] = mine + jnp.where(rim_side, theirs, mine)
            halo = jnp.where(last_side, end_halo[0, here, :], end_halo[1, here, :])
            end_field[i, here, :] = jnp.where(beyond, halo, end_field[i, here, :])
    for base in range(PAD - 1, PAD + ROWS + 1, 8):
        here, above, below = slice(base, base + 8), slice(base + 1, base + 9), slice(base - 1, base + 7)
        for i in range(2):
            w = end_wet[i, here, :]
            total = w * (end_side[i, here, :] + (end_wet[i, above, :] + end_wet[i, below, :]))
            c, fn, fs = end_field[i, here, :], end_field[i, above, :], end_field[i, below, :]
            fe, fw = pltpu.roll(c, 128 - LEVELS, 1), pltpu.roll(c, LEVELS, 1)
            lap = w * ((fe + fw) + (fn + fs)) - total * c
            end_once[i, here, :] = lap
            end_part[i, here, :] = (
                c - (end_own[i, 0, here, :] * (fe - fw) + end_own[i, 1, here, :] * (fn - fs))
            ) + (end_k[i, here, :] + end_b[i, here, :] * total) * lap
    for e in range(2, end):
        here = slice(8 * e, 8 * e + 8)
        for i in range(2):
            lap = end_once[i, here, :]
            total = (pltpu.roll(lap, 128 - LEVELS, 1) + pltpu.roll(lap, LEVELS, 1)) + (
                end_once[i, 8 * e + 1:8 * e + 9, :] + end_once[i, 8 * e - 1:8 * e + 7, :])
            end_new[i, 8 * e - PAD:8 * e - PAD + 8, :] = (
                end_part[i, here, :] - end_b[i, here, :] * end_wet[i, here, :] * total)

    def sides(ref, k, south, north):
        return jnp.where(sub < 4, ref[k, south:south + 8, :], ref[k, north:north + 8, :])

    def along(tiles, k):
        if k not in tiles[1]:
            tile = tiles[0](k)
            tiles[1][k] = (tile, pltpu.roll(tile, 128 - LEVELS, 1), pltpu.roll(tile, LEVELS, 1))
        return tiles[1][k]

    def along_row(tiles, k):
        tile, left, right = along(tiles, k)
        return (
            tile,
            jnp.where(lane < 128 - LEVELS, left, along(tiles, (k + 1) % TILES)[1]),
            jnp.where(lane < LEVELS, along(tiles, (k - 1) % TILES)[2], right),
        )

    def put(ref, k, south, north, value):
        ref[k, south:south + 4, :] = value[0:4]
        ref[k, north:north + 8, :] = jnp.where(sub < 4, ref[k, north:north + 8, :], value)

    low, high = PAD - 2, PAD + ROWS - 6
    wets = (lambda k: sides(wet, k, low, high), {})
    states = [(lambda k, f=f: sides(field.at[f], k, low, high), {}) for f in flows]
    for k in inside:
        w, we, ww = along_row(wets, k)
        total = w * ((we + ww) + (sides(wet, k, low + 1, high + 1) + sides(wet, k, low - 1, high - 1)))
        mixing = sides(wide_k, k, low, high) + sides(wide_b, k, low, high) * total
        zonal_own, merid_own = 0.05 * along(states[0], k)[0], 0.05 * along(states[1], k)[0]
        for i, f in enumerate(flows):
            c, fe, fw = along_row(states[i], k)
            fn, fs = sides(field.at[f], k, low + 1, high + 1), sides(field.at[f], k, low - 1, high - 1)
            lap = w * ((fe + fw) + (fn + fs)) - total * c
            put(once.at[f], k, low, high, lap)
            put(part.at[f], k, low, high, (c - (zonal_own * (fe - fw) + merid_own * (fn - fs))) + mixing * lap)
    low, high = PAD, PAD + ROWS - 8
    laps = [(lambda k, f=f: sides(once.at[f], k, low, high), {}) for f in flows]
    for k in inside:
        at = slice(128 * k, 128 * k + 128)
        fade = sides(wide_b, k, low, high) * sides(wet, k, low, high)
        for i, (f, new) in enumerate(zip(flows, (un, vn))):
            _, le, lw = along_row(laps[i], k)
            ln, ls = sides(once.at[f], k, low + 1, high + 1), sides(once.at[f], k, low - 1, high - 1)
            value = sides(part.at[f], k, low, high) - fade * ((le + lw) + (ln + ls))
            new[0:8, at] = jnp.where(sub < 4, value, new[0:8, at])
            new[ROWS - 8:ROWS, at] = jnp.where(sub < 4, new[ROWS - 8:ROWS, at], value)

    for half in range(2):
        width = span if half == 0 else LANES - span
        at = slice(span * half, span * half + width)
        pieces = []
        for new in (un, vn):
            pieces += halves(jnp.concatenate([new[0:8, at], new[ROWS - 8:ROWS, at]], axis=0))
        means = jnp.dot(jnp.concatenate(pieces, axis=0), pick[0:width, :], preferred_element_type=f32)
        for i in range(2):
            value = means[32 * i:32 * i + 16] + means[32 * i + 16:32 * i + 32]
            mean[i, half, 0:8, :] = value[0:8]
            mean[i, half, ROWS - 8:ROWS, :] = value[8:16]
    for i in range(2):
        means = jnp.dot(
            jnp.concatenate(halves(end_new[i]), axis=0), end_pick[i], preferred_element_type=f32)
        value = means[0:ROWS] + means[128:128 + ROWS]
        mean[i, 0] = jnp.where(lane_c < 2, value[:, 0:128], mean[i, 0])
        mean[i, 1] = jnp.where(lane_c // 2 == (COLS - 2 - 128) // 2, value[:, 128:256], mean[i, 1])
        for half in range(2):
            plane[i, half, own, :] = base_plane[i, half] + mean[i, half]

    for pack, side, shift in ((wpack2, 0, 0), (epack2, 1, 24)):
        for r in range(2):
            packed = jnp.zeros((8, 128), f32)
            for g in range(8 - r):
                rows = slice(PAD + 16 * g + 8 * r, PAD + 16 * g + 8 * r + 8)
                for p in range(2):
                    turned = pltpu.roll(plane[p, side, rows, :], (16 * g + 8 * p + shift) % 128, 1)
                    packed = jnp.where(lane // 8 == 2 * g + p, turned, packed)
            pack[8 * r:8 * r + 8, :] = packed

    def three2(ref):
        return ref, ref.at[pl.ds(0, 8)], ref.at[pl.ds(0, 8)]

    def spots2(ref):
        return ref.at[pl.ds(0, 16)], ref.at[pl.ds(16, 8)], ref.at[pl.ds(24, 8)]

    for p in range(2):
        for half in range(2):
            npack2[p, half] = plane[p, half, PAD + ROWS - 8:PAD + ROWS, :]
            spack2[p, half] = plane[p, half, PAD:PAD + 8, :]
    east, west, from_west, from_east = three2(epack2), three2(wpack2), spots2(rw2), spots2(re2)
    wires2 = near.wire(npack2, spack2, east, west, rn2, rs2, from_west, from_east, send2, recv2)
    near.start(wires2, east, west, from_west, from_east)

    for e in range(2, end):
        rows = slice(8 * e - PAD, 8 * e - PAD + 8)
        for i in range(2):
            tile, new, f = end_new[i, rows, :], (un, vn)[i], i + 2
            begin = pltpu.roll(tile, (64 - 16 * f) % 128, 1)
            last = pltpu.roll(tile, 128 - 16 * f, 1)
            new[rows, 0:128] = jnp.where(lane < 16, begin, new[rows, 0:128])
            new[rows, LANES - 128:LANES] = jnp.where(lane >= 112, last, new[rows, LANES - 128:LANES])

    near.arrived(wires_b)

    @pl.when(near.x == 0)
    def _():
        rs_b[:, 8:16, :] = jnp.zeros((RING // 2 + 2, 8, 128), f32)
        rw_b[0:8, :] = jnp.zeros((8, 128), f32)
        re_b[0:8, :] = jnp.zeros((8, 128), f32)

    @pl.when(near.top)
    def _():
        mirror_rows(rn_b, 1.0)
        mirror = (2 * COLS - 241 - lane) % 128
        start = pick_lanes(turn_rows(rn_b.at[RING // 2 + 1, 8:16, :]), mirror)
        last = pick_lanes(turn_rows(rn_b.at[RING // 2, 8:16, :]), mirror)
        rn_b[RING // 2, 8:16, :] = jnp.where(lane < 112, start, last)
        rn_b[RING // 2 + 1, 8:16, :] = jnp.where(lane < 112, last, start)
        index = jnp.where(
            lane < 8, 71 - lane, jnp.where(jnp.logical_and(lane >= 48, lane < 80), swap - 48, 100))
        rw_b[ROWS + 8:ROWS + 16, :] = pick_lanes(turn_rows(rw_b.at[ROWS + 8:ROWS + 16, :]), index)
        index = jnp.where(lane < 64, swap + 48, jnp.where(lane < 72, 71 - lane, 20))
        re_b[ROWS + 8:ROWS + 16, :] = pick_lanes(turn_rows(re_b.at[ROWS + 8:ROWS + 16, :]), index)

    halo_rows(tracers, rs_b, rn_b)
    west, east = rw_b[...], re_b[...]
    wet_east, wet_west = wet_beyond[0, ends, :], wet_beyond[1, ends, :]
    wet[TILES, ends, :] = jnp.where(lane_h < 64, wet_east, wet_west)
    for f in tracers:
        right = pltpu.roll(east, 128 - 16 * f, 1) if f else east
        field[f, TILES, ends, :] = jnp.where(lane_h < 64, right, pltpu.roll(west, 64 - 16 * f, 1))
    for e in (1, 2, end - 1, end):
        weigh(8 * e, everywhere, (8 * e,))
    weigh(8 * 3, rim, [8 * e for e in early[1:]])
    weigh(8 * middle, rim, (8 * middle,))
    weigh(8 * (middle + 1), rim, [8 * e for e in late[:-1]])
    for e in (1, end):
        first(8 * e, everywhere, tracers, RING, whole=False)
    by_three(2, end, lambda e: first(at_tile(e), everywhere, tracers, RING))
    by_three(2, end, lambda e: second(e, inside, tracers, RING))

    for (got, flag), at in zip(((rs_b, halo_flags[0]), (rn_b, halo_flags[1])), (PAD - 8, PAD + ROWS)):
        for half in range(2):
            plane[2, half, at:at + 8, :] = got[RING // 2 + half, 8:16, :]
        plane[3, 0, at:at + 8, :] = jnp.where(
            lane < BLOCK, flag[0], jnp.where(lane < 2 * BLOCK, flag[1], flag[2]))
        plane[3, 1, at:at + 8, :] = jnp.where(lane < 3 * BLOCK - 128, flag[2], flag[3])
    for p, beyond in (
        (2, jnp.where(lane_h < 120, pltpu.roll(east, 48, 1), pltpu.roll(west, 120, 1))),
        (3, jnp.where(lane_h < 120, wet_east, wet_west)),
    ):
        plane[p, 1, ends, :] = jnp.where(lane_h < 112, plane[p, 1, ends, :], beyond)

    def column_on(tiles):
        turned = [pltpu.roll(tile, 127, 1) for tile in tiles]
        return [jnp.where(lane < 127, turned[half], turned[1 - half]) for half in range(2)]

    for e in range(1, end + 1):
        here = slice(8 * e, 8 * e + 8)
        for half in range(2):
            plane[3, half, here, :] = 0.3 * plane[3, half, here, :]
        for p, to in ((0, 0), (3, 1)):
            if p or 1 < e < end:
                for half, tile in enumerate(column_on([plane[p, half, here, :] for half in range(2)])):
                    shifted[to, half, here, :] = tile

    near.arrived(wires2)

    @pl.when(near.x == 0)
    def _():
        rs2[...] = jnp.zeros(rs2.shape, f32)
        rw2[16:24, :] = jnp.zeros((8, 128), f32)
        re2[16:24, :] = jnp.zeros((8, 128), f32)

    @pl.when(near.top)
    def _():
        for p in range(2):
            start = -pick_lanes(turn_rows(rn2.at[p, 1]), (239 - lane) % 128)
            last = -pick_lanes(turn_rows(rn2.at[p, 0]), (239 - lane) % 128)
            rn2[p, 0] = jnp.where(lane < 112, start, last)
            rn2[p, 1] = jnp.where(lane < 112, last, start)
        for got in (rw2, re2):
            got[24:32, :] = -pick_lanes(turn_rows(got.at[24:32, :]), 112 + (lane // 8 % 2) * 8 + 7 - lane % 8)

    for got, at in ((rs2, PAD - 8), (rn2, PAD + ROWS)):
        for half, tile in enumerate(column_on([got[0, half] for half in range(2)])):
            shifted[0, half, at:at + 8, :] = tile
            plane[1, half, at:at + 8, :] = got[1, half]
    for e in range(1, end + 1):
        here = slice(8 * e, 8 * e + 8)
        g = 7 if e == 1 else 0 if e == end else (e - 2) // 2
        at = 16 if e == 1 else 24 if e == end else 8 * (e % 2)
        for p, off in ((0, 1), (1, 0)):
            beyond = jnp.where(
                lane < 120 - off,
                pltpu.roll(re2[at:at + 8, :], (112 - 16 * g - 8 * p - off) % 128, 1),
                pltpu.roll(rw2[at:at + 8, :], (120 - 16 * g - 8 * p - off) % 128, 1))
            ref = plane.at[1, 1] if p else shifted.at[0, 1]
            theirs = jnp.logical_and(lane >= 112 - off, lane < 128 - off)
            ref[here, :] = jnp.where(theirs, beyond, ref[here, :])

    def apart(tiles, ahead):
        turned = [pltpu.roll(tile, 126 if ahead else 2, 1) for tile in tiles]
        if ahead:
            return [jnp.where(lane < 126, turned[half], turned[1 - half]) - tiles[half] for half in range(2)]
        return [tiles[half] - jnp.where(lane < 2, turned[1 - half], turned[half]) for half in range(2)]

    def rows_apart(p, half, e):
        return plane[p, half, 8 * e + 1:8 * e + 9, :] - plane[p, half, 8 * e - 1:8 * e + 7, :]

    for n in range(NSUB):
        for e in range(1, end + 1):
            here = slice(8 * e, 8 * e + 8)
            slope = apart([shifted[0, half, here, :] for half in range(2)], False)
            for half in range(2):
                flow = slope[half] + rows_apart(1, half, e)
                plane[2, half, here, :] = plane[2, half, here, :] - plane[3, half, here, :] * flow
        inner = 1 if n == NSUB - 1 else 0
        for e in range(1 + inner, end + 1 - inner):
            here = slice(8 * e, 8 * e + 8)
            slope = apart([plane[2, half, here, :] for half in range(2)], True)
            for half in range(2):
                shifted[0, half, here, :] = shifted[0, half, here, :] - shifted[1, half, here, :] * slope[half]
                plane[1, half, here, :] = plane[1, half, here, :] - plane[3, half, here, :] * rows_apart(2, half, e)
    for e in range(2, end):
        here = slice(8 * e, 8 * e + 8)
        turned = [pltpu.roll(shifted[0, half, here, :], 1, 1) for half in range(2)]
        for half in range(2):
            plane[0, half, here, :] = jnp.where(lane < 1, turned[1 - half], turned[half])
    for half, width in ((0, 128), (1, COLS - 128)):
        at = slice(128 * half, 128 * half + 128)
        du[:, at] = plane[0, half, own, :] - mean[0, half]
        dv[:, at] = plane[1, half, own, :] - mean[1, half]
        at = slice(128 * half, 128 * half + width)
        for p, ref in ((0, zonal), (1, merid), (2, height)):
            ref[:, at] = plane[p, half, own, 0:width]
    near.sent(wires, wires_b, wires2)


def finish_kernel(
    tn, sn, un, vn, du, dv, height, zonal, merid,
    t_out, s_out, u_out, v_out, height_out, zonal_out, merid_out, done, sems,
):
    copies = [
        pltpu.make_async_copy(src, dst, sems.at[i])
        for i, (src, dst) in enumerate(
            ((tn, t_out), (sn, s_out), (height, height_out), (zonal, zonal_out), (merid, merid_out)))
    ]
    for copy in copies:
        copy.start()
    step = 24
    for i in range(ROWS // step):
        for f, (new, change, out) in enumerate(((un, du, u_out), (vn, dv, v_out))):
            for r in range(step * i, step * i + step, 8):
                for half in range(2):
                    tile = change[r:r + 8, 128 * half:128 * half + 128]
                    for k in range(8 * half, min(8 * half + 8, TILES)):
                        at = slice(128 * k, 128 * k + 128)
                        done[f, r:r + 8, at] = new[r:r + 8, at] + expand(tile, k % 8)
            rows = pl.ds(step * i, step)
            copies.append(pltpu.make_async_copy(done.at[f, rows, :], out.at[rows, :], sems.at[5 + 2 * i + f]))
            copies[-1].start()
    for copy in copies:
        copy.wait()


def per_device(nb, nw, t, s, u, v, elev, zavg, mavg, flags, sel, ktab, btab):
    f32 = jnp.float32
    vmem = pl.BlockSpec(memory_space=pltpu.VMEM)
    hbm = pl.BlockSpec(memory_space=pl.ANY)
    scratch = lambda *shape: pltpu.VMEM(shape, f32)
    dma = lambda *shape: pltpu.SemaphoreType.DMA(shape)
    parts = pl.pallas_call(
        functools.partial(step_kernel, nb, nw),
        out_shape=(pltpu.VMEM((ROWS, LANES), f32),) * 2
        + (pltpu.VMEM((ROWS + 8, LANES), f32),) * 2
        + (pltpu.VMEM((ROWS, 256), f32),) * 2
        + (pltpu.VMEM((ROWS, COLS), f32),) * 3,
        in_specs=[hbm] * 11,
        out_specs=(vmem,) * 9,
        scratch_shapes=[
            pltpu.SMEM((2, 4), jnp.int32),
            pltpu.SMEM((8,), f32),
            pltpu.SMEM((8,), f32),
            pltpu.VMEM((ROWS, COLS), jnp.int32),
            scratch(ROWS, COLS), scratch(ROWS, COLS), scratch(ROWS, COLS),
            scratch(2, 2, 8, LANES), scratch(2, 2, ROWS, 128), scratch(4, ROWS, LANES),
            scratch(RING // 2, 8, 128), scratch(RING // 2, 8, 128), scratch(64, 128), scratch(64, 128),
            scratch(RING // 2, 24, 128), scratch(RING // 2, 24, 128), scratch(80, 128), scratch(80, 128),
            scratch(RING // 2 + 2, 8, 128), scratch(RING // 2 + 2, 8, 128), scratch(ROWS, 128), scratch(ROWS, 128),
            scratch(RING // 2 + 2, 24, 128), scratch(RING // 2 + 2, 24, 128),
            scratch(ROWS + 16, 128), scratch(ROWS + 16, 128),
            scratch(4, RING, BAND, 128), scratch(4, RING, BAND, 128), scratch(4, TILES, BAND, 128),
            scratch(RING, BAND, 128), scratch(RING, BAND, 128),
            scratch(TILES, BAND, 128), scratch(TILES, BAND, 128),
            pltpu.VMEM((128 * LEVELS, 128), jnp.bfloat16), pltpu.VMEM((2, 128, 256), jnp.bfloat16),
            pltpu.VMEM((256, 128 * LEVELS), jnp.bfloat16),
            scratch(2, 2, ROWS, 128), scratch(2, 2, ROWS, 128),
            scratch(2, BAND, 128), scratch(2, 2, BAND, 128), scratch(2, BAND, 128), scratch(2, BAND, 128),
            scratch(2, BAND, 128), scratch(2, BAND, 128), scratch(2, BAND, 128), scratch(2, BAND, 128),
            scratch(2, 128, 128), scratch(2, BAND, 128), scratch(2, BAND, 128), scratch(2, 2, BAND, 128),
            scratch(4, 2, BAND, 128), scratch(2, 2, 8, 128), scratch(2, 2, 8, 128), scratch(16, 128), scratch(16, 128),
            scratch(2, 2, 8, 128), scratch(2, 2, 8, 128), scratch(32, 128), scratch(32, 128),
            dma(15), dma(4), dma(8), dma(8), dma(8), dma(8), dma(8), dma(8),
        ],
        compiler_params=pltpu.CompilerParams(
            collective_id=0, has_side_effects=True, vmem_limit_bytes=VMEM_BYTES),
        name="step",
    )(flags, ktab, btab, sel, t, s, u, v, zavg, mavg, elev)
    parts = [pltpu.with_memory_space_constraint(part, pltpu.VMEM) for part in parts]

    big = jax.ShapeDtypeStruct((ROWS, LANES), f32)
    flat = jax.ShapeDtypeStruct((ROWS, COLS), f32)
    return pl.pallas_call(
        finish_kernel,
        out_shape=(big,) * 4 + (flat,) * 3,
        in_specs=[vmem] * 9,
        out_specs=(hbm,) * 7,
        scratch_shapes=[scratch(2, ROWS, LANES), dma(15)],
        compiler_params=pltpu.CompilerParams(vmem_limit_bytes=VMEM_BYTES),
        name="finish",
    )(*parts)


def solution(mesh):
    grid = P("wide", "blocks")
    return jax.shard_map(
        functools.partial(per_device, mesh.shape["blocks"], mesh.shape["wide"]),
        mesh=mesh,
        in_specs=(grid,) * 9 + (P(), P()),
        out_specs=(grid,) * 7,
        check_vma=False,
    )
```

```python
import functools

import jax
import jax.numpy as jnp
from jax import lax
from jax.experimental import pallas as pl
from jax.experimental.pallas import tpu as pltpu
from jax.sharding import PartitionSpec as P

BLOCK = 60
LEVELS = 8
NSUB = 4
ROWS = 120
COLS = 240
LANES = COLS * LEVELS
TILES = LANES // 128
RING = TILES + 1
PAD = 16
BAND = ROWS + 2 * PAD
MESH = pl.DeviceIdType.MESH
VMEM_BYTES = 56 * 1024 * 1024


def lanes_of(shape=(8, 128)):
    return lax.broadcasted_iota(jnp.int32, shape, 1)


def rows_of(shape=(8, 128)):
    return lax.broadcasted_iota(jnp.int32, shape, 0)


def pick_lanes(tile, index):
    return jnp.take_along_axis(tile, index, axis=1, mode="promise_in_bounds")


def turn_rows(rows):
    turned = jnp.broadcast_to(rows[7:8, :], (8, 128))
    for i in range(1, 8):
        turned = jnp.where(rows_of() == i, jnp.broadcast_to(rows[7 - i:8 - i, :], (8, 128)), turned)
    return turned


class Neighbours:
    def __init__(self, nb, nw):
        b, x = lax.axis_index("blocks"), lax.axis_index("wide")
        self.b, self.x = b, x
        self.top, self.inner, self.above = x == nw - 1, x < nw - 1, x > 0
        first, last = b == 0, b == nb - 1
        self.east, self.west = jnp.where(last, 0, b + 1), jnp.where(first, nb - 1, b - 1)
        self.fold = nb - 1 - b
        self.fold_east = jnp.where(last, nb - 1, nb - 2 - b)
        self.fold_west = jnp.where(first, 0, nb - b)
        self.own_east = jnp.logical_and(self.top, self.fold_east == b)
        self.own_west = jnp.logical_and(self.top, self.fold_west == b)
        self.far_east = jnp.logical_and(self.top, self.fold_east != b)
        self.far_west = jnp.logical_and(self.top, self.fold_west != b)

    def greet(self):
        sem = pltpu.get_barrier_semaphore()

        def greet(b, x):
            pl.semaphore_signal(sem, inc=1, device_id=(b, x), device_id_type=MESH)

        b, x = self.b, self.x

        @pl.when(self.far_east)
        def _():
            greet(self.fold_east, x)

        @pl.when(self.far_west)
        def _():
            greet(self.fold_west, x)

        @pl.when(self.inner)
        def _():
            greet(self.east, x + 1)
            greet(self.west, x + 1)

        @pl.when(self.above)
        def _():
            greet(self.east, x - 1)
            greet(self.west, x - 1)

        @pl.when(self.top)
        def _():
            greet(self.fold, x)

        greet(self.east, x)
        greet(self.west, x)

        @pl.when(self.inner)
        def _():
            greet(b, x + 1)

        @pl.when(self.above)
        def _():
            greet(b, x - 1)

    def meet(self):
        sem = pltpu.get_barrier_semaphore()
        x = self.x
        own = jnp.logical_or(self.own_east, self.own_west)

        @pl.when(x == 0)
        def _():
            pl.semaphore_wait(sem, 5)

        @pl.when(own)
        def _():
            pl.semaphore_wait(sem, 7)

        @pl.when(jnp.logical_and(self.above, jnp.logical_not(own)))
        def _():
            pl.semaphore_wait(sem, 8)

    def wire(self, north, south, east, west, rn, rs, rw, re, send, recv):
        b, x = self.b, self.x

        def c(src, dst, way, slot, to_b, to_x):
            return pltpu.make_async_remote_copy(
                src_ref=src, dst_ref=dst, send_sem=send.at[way], recv_sem=recv.at[slot],
                device_id=(to_b, to_x), device_id_type=MESH)

        return dict(
            always=[
                c(east[0], rw[0], 0, 0, self.east, x),
                c(west[0], re[0], 1, 1, self.west, x),
            ],
            corner_inner=[
                c(east[1], rw[1], 4, 4, self.east, x + 1),
                c(west[1], re[1], 5, 5, self.west, x + 1),
            ],
            corner_above=[
                c(east[2], rw[2], 6, 6, self.east, x - 1),
                c(west[2], re[2], 7, 7, self.west, x - 1),
            ],
            inner=[c(north, rs, 2, 2, b, x + 1)],
            above=[c(south, rn, 3, 3, b, x - 1)],
            top=[c(north, rn, 2, 3, self.fold, x)],
            far_east=[c(east[1], re[2], 4, 7, self.fold_east, x)],
            far_west=[c(west[1], rw[2], 5, 6, self.fold_west, x)],
        )

    def start(self, wires, east, west, rw, re):
        def go(name, cond):
            @pl.when(cond)
            def _():
                for copy in wires[name]:
                    copy.start()

        go("far_east", self.far_east)
        go("far_west", self.far_west)
        go("corner_inner", self.inner)
        go("corner_above", self.above)
        go("top", self.top)
        for copy in wires["always"]:
            copy.start()
        go("inner", self.inner)
        go("above", self.above)

        @pl.when(self.own_east)
        def _():
            re[2][...] = east[1][...]

        @pl.when(self.own_west)
        def _():
            rw[2][...] = west[1][...]

    def arrived(self, wires):
        w = wires
        for copy in w["always"]:
            copy.wait_recv()
        w["top"][0].wait_recv()

        @pl.when(self.above)
        def _():
            for copy in w["inner"] + w["corner_inner"]:
                copy.wait_recv()

        @pl.when(jnp.logical_not(self.own_east))
        def _():
            w["far_east"][0].wait_recv()

        @pl.when(jnp.logical_not(self.own_west))
        def _():
            w["far_west"][0].wait_recv()

    def sent(self, *every):
        for w in every:
            for copy in w["always"]:
                copy.wait_send()
            w["top"][0].wait_send()

        @pl.when(self.above)
        def _():
            for w in every:
                for copy in w["above"] + w["corner_above"]:
                    copy.wait_send()

        @pl.when(jnp.logical_not(self.own_east))
        def _():
            for w in every:
                w["far_east"][0].wait_send()

        @pl.when(jnp.logical_not(self.own_west))
        def _():
            for w in every:
                w["far_west"][0].wait_send()


def block_row(flags, row, tile):
    low, high = (128 * tile) // (BLOCK * LEVELS), (128 * tile + 127) // (BLOCK * LEVELS)
    value = jnp.full((8, 128), flags[row, low].astype(jnp.float32))
    if low != high:
        value = jnp.where(
            lanes_of() < BLOCK * LEVELS * high - 128 * tile,
            value,
            flags[row, high].astype(jnp.float32),
        )
    return value


def expand(tile, part):
    index = lanes_of() // LEVELS + 16 * part
    return pick_lanes(tile, index)


def halves(values):
    coarse = values.astype(jnp.bfloat16)
    return [coarse, (values - coarse.astype(jnp.float32)).astype(jnp.bfloat16)]


def step_kernel(
    nb, nw, flags_in, ktab_in, btab_in, sel_in, t, s, u, v, zavg_in, mavg_in, elev_in,
    tn, sn, un, vn, du, dv, height, zonal, merid,
    flags, ktab, btab, sel, zavg, mavg, elev,
    edge_rows, edge_cols, raw, npack, spack, wpack, epack, rn, rs, rw, re,
    npack_b, spack_b, wpack_b, epack_b, rn_b, rs_b, rw_b, re_b,
    field, once, part, wet, count, wide_k, wide_b, pick, end_pick, spread_out, mean, base_plane,
    end_field, end_own, end_k, end_b, end_wet, end_side, end_once, end_part, end_new, wet_beyond, end_halo, shifted,
    plane, npack2, spack2, wpack2, epack2, rn2, rs2, rw2, re2,
    small, load, send, recv, send_b, recv_b, send2, recv2,
):
    f32, bf16 = jnp.float32, jnp.bfloat16
    sources = (t, s, u, v)
    results = (tn, sn, un, vn)
    near = Neighbours(nb, nw)
    near.greet()

    tables = [
        pltpu.make_async_copy(src, dst, small.at[i])
        for i, (src, dst) in enumerate(
            ((flags_in, flags), (ktab_in, ktab), (btab_in, btab), (sel_in, sel),
             (elev_in, elev), (zavg_in, zavg), (mavg_in, mavg)))
    ]
    loads = [pltpu.make_async_copy(src, raw.at[f], load.at[f]) for f, src in enumerate(sources)]
    edges = []
    for i, src in enumerate((u, v)):
        for side, at in enumerate((0, ROWS - 8)):
            edges.append(pltpu.make_async_copy(
                src.at[pl.ds(at, 8), :], edge_rows.at[i, side], small.at[7 + 4 * i + side]))
        for side, at in enumerate((0, LANES - 128)):
            edges.append(pltpu.make_async_copy(
                src.at[:, pl.ds(at, 128)], edge_cols.at[i, side], small.at[9 + 4 * i + side]))
    tables[0].start()
    for copy in edges:
        copy.start()
    for copy in tables[1:4]:
        copy.start()
    for f in (2, 3, 0, 1):
        loads[f].start(priority=1)
    for copy in tables[4:]:
        copy.start()

    lane, sub = lanes_of(), rows_of()
    lane_c, row_c = lanes_of((ROWS, 128)), rows_of((ROWS, 128))
    lane_h = lanes_of((ROWS + 16, 128))
    end = 2 + ROWS // 8
    middle = 2 + BLOCK // 8
    split = BLOCK % 8
    early, late = range(2, middle), range(middle + 1, end)
    flows, tracers = (2, 3), (0, 1)
    inside, everywhere, rim = range(TILES), range(RING), (0, TILES - 1, TILES)
    ends = slice(PAD - 8, PAD + ROWS + 8)
    own = pl.ds(PAD, ROWS)
    span = 128 * LEVELS

    pick[...] = jnp.where(
        lax.broadcasted_iota(jnp.int32, (span, 128), 0) // LEVELS
        == lax.broadcasted_iota(jnp.int32, (span, 128), 1), 1.0 / LEVELS, 0.0).astype(bf16)
    from_lane = lax.broadcasted_iota(jnp.int32, (128, 256), 0)
    to_lane = lax.broadcasted_iota(jnp.int32, (128, 256), 1)
    for i in range(2):
        cell = (from_lane - 16 * (i + 2) + 32 + 128) % 128 // LEVELS
        hit = jnp.logical_or(
            jnp.logical_and(cell - 12 == to_lane, to_lane < 2),
            jnp.logical_and(cell - 2 == to_lane - (COLS - 2), to_lane >= COLS - 2))
        hit = jnp.logical_and(hit, to_lane < COLS)
        end_pick[i] = jnp.where(hit, 1.0 / LEVELS, 0.0).astype(bf16)
    spread_out[...] = jnp.where(
        lax.broadcasted_iota(jnp.int32, (256, span), 0) % 128
        == lax.broadcasted_iota(jnp.int32, (256, span), 1) // LEVELS, 1.0, 0.0).astype(bf16)

    tables[0].wait()
    lows = [block_row(flags, 0, k) for k in inside]
    highs = [block_row(flags, 1, k) for k in inside]


    def beside(tiles, k):
        left = pltpu.roll(tiles[k], 128 - LEVELS, 1)
        next_left = pltpu.roll(tiles[(k + 1) % TILES], 128 - LEVELS, 1)
        right = pltpu.roll(tiles[k], LEVELS, 1)
        last_right = pltpu.roll(tiles[(k - 1) % TILES], LEVELS, 1)
        return jnp.where(lane < 128 - LEVELS, left, next_left) + jnp.where(lane < LEVELS, last_right, right)

    for k in inside:
        low, high = lows[k], highs[k]
        side_low, side_high = beside(lows, k), beside(highs, k)
        count_low, count_high = low * (side_low + (low + low)), high * (side_high + (high + high))
        mixed = jnp.where(sub < split, low, high)
        north = jnp.where(sub < split - 1, low, high)
        south = jnp.where(sub < split + 1, low, high)
        for e in early:
            wet[k, 8 * e:8 * e + 8, :] = low
            count[k, 8 * e:8 * e + 8, :] = count_low
        for e in late:
            wet[k, 8 * e:8 * e + 8, :] = high
            count[k, 8 * e:8 * e + 8, :] = count_high
        wet[k, 8 * middle:8 * middle + 8, :] = mixed
        count[k, 8 * middle:8 * middle + 8, :] = mixed * (
            jnp.where(sub < split, side_low, side_high) + (north + south))


    def pack_rows(packs, both, last):
        tiles = [[], []]
        for m in range(RING // 2):
            for side in range(2):
                packed = last[side]
                for k in (2 * m, 2 * m + 1):
                    if k >= TILES:
                        continue
                    for i in range(2):
                        row = 4 * (k % 2) + 2 * i
                        tile = both(i, side, k)
                        shift = (row + 2 * side) % 8
                        packed = jnp.where(sub // 2 == row // 2, pltpu.roll(tile, shift, 0) if shift else tile, packed)
                w = (lows, highs)[side]
                upper = w[2 * m + 1] if 2 * m + 1 < TILES else jnp.ones((8, 128), f32)
                packs[side][m] = packed * jnp.where(sub < 4, w[2 * m], upper)

    for copy in edges:
        copy.wait()
    tails = []
    for row in range(2):
        tail = jnp.zeros((8, 128), f32)
        for j in range(4):
            tail = jnp.where(lane // 32 == j, flags[row, j].astype(f32), tail)
        tails.append(tail)
    pack_rows((spack, npack), lambda i, side, k: edge_rows[i, side, :, 128 * k:128 * k + 128], tails)
    lane_a, row_a = lanes_of((64, 128)), rows_of((64, 128))
    lane_b = lanes_of((ROWS - 64, 128))
    for side, pack, to in ((0, wpack, 32), (1, epack, 80)):
        col = 3 * side
        w_a = jnp.where(row_a < BLOCK, flags[0, col].astype(f32), flags[1, col].astype(f32))
        w_b = jnp.full((ROWS - 64, 128), flags[1, col].astype(f32))
        parts_of = []
        for rows, at, lanes_in, w in ((slice(0, 64), to, lane_a, w_a), (slice(64, ROWS), (to + 64) % 128, lane_b, w_b)):
            packed = jnp.ones(w.shape, f32)
            for i in range(2):
                shift = (at + 16 * i - 112 * side) % 128
                packed = jnp.where(
                    lanes_in // 16 == at // 16 + i, pltpu.roll(edge_cols[i, side, rows, :], shift, 1), packed)
            parts_of.append(packed * w)
        at = (to + 64) % 128 // 16
        theirs = jnp.logical_or(lane_b // 8 == 1, jnp.logical_or(lane_b // 16 == at, lane_b // 16 == at + 1))
        pack[0:ROWS - 64, :] = jnp.where(theirs, parts_of[1], parts_of[0][0:ROWS - 64])
        pack[ROWS - 64:64, :] = parts_of[0][ROWS - 64:64]

    for copy in tables[1:4]:
        copy.wait()
    for half, width in ((0, 128), (1, COLS - 128)):
        index = sel[:, 128 * half:128 * half + width]
        if width < 128:
            index = jnp.concatenate([index, jnp.zeros((ROWS, 128 - width), jnp.int32)], axis=1)
        kappa = jnp.full(index.shape, ktab[0])
        bihar = jnp.full(index.shape, btab[0])
        for n in range(1, 8):
            hit = index == n
            kappa = jnp.where(hit, ktab[n], kappa)
            bihar = jnp.where(hit, btab[n], bihar)
        for table, to in ((kappa, wide_k), (bihar, wide_b)):
            wide = jnp.dot(
                jnp.concatenate(halves(table), axis=1), spread_out[...], preferred_element_type=f32)
            for k in range(8 * half, min(8 * half + 8, TILES)):
                to[k, own, :] = wide[:, 128 * (k % 8):128 * (k % 8) + 128]

    def around(ref, turned, key, k, base, ring_size):
        here, above, below = pl.ds(base, 8), pl.ds(base + 1, 8), pl.ds(base - 1, 8)

        def ring(k):
            if (key, k) not in turned:
                tile = ref[k, here, :]
                turned[key, k] = (tile, pltpu.roll(tile, 128 - LEVELS, 1), pltpu.roll(tile, LEVELS, 1))
            return turned[key, k]

        tile, left, right = ring(k)
        east = jnp.where(lane < 128 - LEVELS, left, ring((k + 1) % ring_size)[1])
        west = jnp.where(lane < LEVELS, ring((k - 1) % ring_size)[2], right)
        return tile, east, west, ref[k, above, :], ref[k, below, :]

    def at_tile(e):
        return 8 * e if isinstance(e, int) else pl.multiple_of(8 * e, 8)

    def weigh(base, tiles, same, ring_size=RING):
        turned = {}
        for k in tiles:
            w, we, ww, wn, ws = around(wet, turned, "wet", k, base, ring_size)
            total = w * ((we + ww) + (wn + ws))
            for to in same:
                count[k, to:to + 8, :] = total

    def mask(e, which):
        base = at_tile(e)
        rows, here = pl.ds(base - PAD, 8), pl.ds(base, 8)
        for k in inside:
            w = wet[k, here, :]
            for f in which:
                field[f, k, here, :] = raw[f, rows, 128 * k:128 * k + 128] * w

    def first(base, tiles, which, ring_size, whole=True):
        here = pl.ds(base, 8)
        turned = {}
        for k in tiles:
            w, total = wet[k, here, :], count[k, here, :]
            full = whole and k < TILES
            if full:
                mixing = wide_k[k, here, :] + wide_b[k, here, :] * total
                zonal_own = 0.05 * field[2, k, here, :]
                merid_own = 0.05 * field[3, k, here, :]
            for f in which:
                c, fe, fw, fn, fs = around(field.at[f], turned, f, k, base, ring_size)
                lap = w * ((fe + fw) + (fn + fs)) - total * c
                once[f, k, here, :] = lap
                if full:
                    part[f, k, here, :] = (
                        c - (zonal_own * (fe - fw) + merid_own * (fn - fs))) + mixing * lap

    def second(e, tiles, which, ring_size):
        base = at_tile(e)
        here, rows = pl.ds(base, 8), pl.ds(base - PAD, 8)
        turned = {}
        for k in tiles:
            fade = wide_b[k, here, :] * wet[k, here, :]
            for f in which:
                _, le, lw, ln, ls = around(once.at[f], turned, f, k, base, ring_size)
                results[f][rows, 128 * k:128 * k + 128] = (
                    part[f, k, here, :] - fade * ((le + lw) + (ln + ls)))

    def by_three(low, high, step):
        def body(i, carry):
            for j in range(3):
                step(low + 3 * i + j)
            return carry
        lax.fori_loop(0, (high - low) // 3, body, 0)

    def turn(f, tile_lane=None):
        at = lane if tile_lane is None else tile_lane
        return (at - 16 * f + 32 + 128) % 128

    def bring(f, last, begin):
        return jnp.where(turn(f) < 64, pltpu.roll(last, 16 * f, 1), pltpu.roll(begin, 64 + 16 * f, 1))

    def bring_field(base):
        here = pl.ds(base, 8)
        for f in flows:
            end_field[f - 2, here, :] = bring(f, field[f, TILES - 1, here, :], field[f, 0, here, :])

    def bring_rest(e):
        base = at_tile(e)
        here = pl.ds(base, 8)
        bring_field(base)
        for i in range(2):
            flow = 0.05 * end_field[i, here, :]
            end_own[i, i, here, :] = flow
            end_own[1 - i, i, here, :] = pltpu.roll(flow, 112 if i else 16, 1)
        for src, to in ((wide_k, end_k), (wide_b, end_b)):
            tile = bring(2, src[TILES - 1, here, :], src[0, here, :])
            to[0, here, :] = tile
            to[1, here, :] = pltpu.roll(tile, 16, 1)

    early_start = near.b < 2

    def interior():
        for f in flows:
            for k in inside:
                for ref in (field, once):
                    ref[f, k, PAD - 8:PAD, :] = jnp.zeros((8, 128), f32)
                    ref[f, k, PAD + ROWS:PAD + ROWS + 8, :] = jnp.zeros((8, 128), f32)
        by_three(2, end, lambda e: mask(e, (0, 1, 2, 3)))
        by_three(2, end, lambda e: first(at_tile(e), inside, flows, TILES))
        by_three(2, end, lambda e: second(e, inside, flows, TILES))

    def loaded():
        for copy in loads:
            copy.wait()

    @pl.when(early_start)
    def _():
        loaded()
        interior()

    near.meet()
    into = pl.ds(8, 8)

    def three(ref):
        return ref, ref.at[pl.ds(ROWS - 8 - 64, 8)], ref.at[pl.ds(0, 8)]

    def spots(ref):
        return ref.at[pl.ds(0, 64)], ref.at[pl.ds(64, 8)], ref.at[pl.ds(72, 8)]

    east, west, from_west, from_east = three(epack), three(wpack), spots(rw), spots(re)
    wires = near.wire(
        npack, spack, east, west, rn.at[:, into, :], rs.at[:, into, :], from_west, from_east, send, recv)
    near.start(wires, east, west, from_west, from_east)

    for copy in tables[4:]:
        copy.wait()
    for half, width in ((0, 128), (1, COLS - 128)):
        w = jnp.zeros((ROWS, 128), f32)
        for i in range(2):
            for j in range(4):
                here = jnp.logical_and(row_c // BLOCK == i, (lane_c + 128 * half) // BLOCK == j)
                w = jnp.where(here, flags[i, j].astype(f32), w)
        plane[3, half, own, :] = w
        if width < 128:
            plane[2, half, own, :] = jnp.zeros((ROWS, 128), f32)
            base_plane[:, half] = jnp.zeros((2, ROWS, 128), f32)
        at = slice(128 * half, 128 * half + width)
        plane[2, half, own, 0:width] = w[:, 0:width] * elev[:, at]
        base_plane[0, half, :, 0:width] = w[:, 0:width] * zavg[:, at]
        base_plane[1, half, :, 0:width] = w[:, 0:width] * mavg[:, at]

    pl.when(jnp.logical_not(early_start))(loaded)
    pack_rows((spack_b, npack_b), lambda i, side, k: raw[i, (ROWS - 8) * side:(ROWS - 8) * side + 8, 128 * k:128 * k + 128],
              [jnp.zeros((8, 128), f32)] * 2)
    for pack, at in ((spack_b, PAD), (npack_b, PAD + ROWS - 8)):
        for half in range(2):
            pack[RING // 2 + half] = plane[2, half, at:at + 8, :]
    for side, pack in ((0, wpack_b), (1, epack_b)):
        w = wet[(TILES - 1) * side, own, :]
        packed = jnp.zeros((ROWS, 128), f32)
        for f in range(2):
            shift = (16 * f + 64 * side) % 128
            tile = raw[f, :, (LANES - 128) * side:(LANES - 128) * side + 128]
            place = lane_c // 16 == f + 3 * side
            packed = jnp.where(place, pltpu.roll(tile, shift, 1) if shift else tile, packed)
        packed = packed * w
        top = pltpu.roll(plane[2, side, own, :], 24 if side else 64, 1)
        pack[...] = jnp.where(lane_c // 8 == (0 if side else 8), top, packed)

    def three_b(ref):
        return ref, ref.at[pl.ds(ROWS - 8, 8)], ref.at[pl.ds(0, 8)]

    def spots_b(ref):
        return ref.at[pl.ds(8, ROWS)], ref.at[pl.ds(0, 8)], ref.at[pl.ds(ROWS + 8, 8)]

    east, west, from_west, from_east = three_b(epack_b), three_b(wpack_b), spots_b(rw_b), spots_b(re_b)
    wires_b = near.wire(
        npack_b, spack_b, east, west, rn_b.at[:, into, :], rs_b.at[:, into, :], from_west, from_east, send_b, recv_b)
    near.start(wires_b, east, west, from_west, from_east)

    pl.when(jnp.logical_not(early_start))(interior)
    for e in range(2, end):
        bring_rest(e)
    for half in range(2):
        width = span if half == 0 else LANES - span
        pieces = halves(un[:, span * half:span * half + width]) + halves(vn[:, span * half:span * half + width])
        means = jnp.dot(jnp.concatenate(pieces, axis=0), pick[0:width, :], preferred_element_type=f32)
        for i in range(2):
            mean[i, half] = means[256 * i:256 * i + ROWS] + means[256 * i + 128:256 * i + 128 + ROWS]

    near.arrived(wires)

    @pl.when(near.x == 0)
    def _():
        rs[:, 8:16, :] = jnp.zeros((RING // 2, 8, 128), f32)
        rw[64:72, :] = jnp.zeros((8, 128), f32)
        re[64:72, :] = jnp.zeros((8, 128), f32)

    swap = lane + 8 - 16 * ((lane // 8) % 2)

    def mirror_rows(ref, sign):
        turned = [
            sign * pick_lanes(
                jnp.where(sub % 2 == 0, ref[m, 9:17, :], ref[m, 7:15, :]), lane + 120 - 16 * (lane // 8))
            for m in range(RING // 2)
        ]
        tail = pick_lanes(ref[RING // 2 - 1, 8:16, :], lane + 96 - 64 * (lane // 32))
        for m in range(RING // 2):
            lower = turned[RING // 2 - 1 - m]
            upper = turned[RING // 2 - 2 - m] if m < RING // 2 - 1 else tail
            ref[m, 8:16, :] = jnp.where(sub < 4, lower, upper)

    @pl.when(near.top)
    def _():
        mirror_rows(rn, -1.0)
        for got, low, off in ((rw, 80, 16), (re, 32, -16)):
            index = jnp.where(jnp.logical_and(lane >= low, lane < low + 32), swap + off, 8)
            tile = pick_lanes(turn_rows(got.at[72:80, :]), index)
            got[72:80, :] = jnp.where(lane < 16, tile, -tile)

    halo_flags = []
    for got, base in ((rs, PAD - 8), (rn, PAD + ROWS)):
        flag = [jnp.broadcast_to(got[RING // 2 - 1, 12:13, 32 * j:32 * j + 1], (8, 128)) for j in range(4)]
        halo_flags.append(flag)
        for k in inside:
            low, high = (128 * k) // (BLOCK * LEVELS), (128 * k + 127) // (BLOCK * LEVELS)
            value = flag[low]
            if low != high:
                value = jnp.where(lane < BLOCK * LEVELS * high - 128 * k, value, flag[high])
            wet[k, base:base + 8, :] = value

    def halo_rows(which, south, north):
        for i, f in enumerate(which):
            for k in inside:
                row = 8 + 4 * (k % 2) + 2 * i
                field[f, k, PAD - 8:PAD, :] = south[k // 2, row - 6:row + 2, :]
                field[f, k, PAD + ROWS:PAD + ROWS + 8, :] = north[k // 2, row:row + 8, :]

    halo_rows(flows, rs, rn)

    for e in (1, end):
        bring_field(8 * e)
    for e in range(1, end + 1):
        here = slice(8 * e, 8 * e + 8)
        at = 64 if e == 1 else 72 if e == end else 8 * ((e - 2) % 8)
        east, west = re[at:at + 8, :], rw[at:at + 8, :]
        further = e == 1 or 10 <= e < end
        wet_east = jnp.broadcast_to(east[:, 8 * further:8 * further + 1], (8, 128))
        wet_west = jnp.broadcast_to(west[:, 8 * further:8 * further + 1], (8, 128))
        wet_beyond[0, here, :] = wet_east
        wet_beyond[1, here, :] = wet_west
        if further:
            east, west = pltpu.roll(east, 64, 1), pltpu.roll(west, 64, 1)
        end_halo[0, here, :] = east
        end_halo[1, here, :] = west
    for i, f in enumerate(flows):
        at = turn(f)
        last_side = at < 64
        outer = jnp.logical_and(at >= 32, at < 96)
        rim_side = jnp.logical_and(at >= 24, at < 104)
        beyond = jnp.logical_or(at // 16 == 2, at // 16 == 5)
        for e in range(1, end + 1):
            here = slice(8 * e, 8 * e + 8)
            mine = jnp.where(last_side, wet[TILES - 1, here, :], wet[0, here, :])
            theirs = jnp.where(last_side, wet_beyond[0, here, :], wet_beyond[1, here, :])
            end_wet[i, here, :] = jnp.where(outer, theirs, mine)
            end_side[i, here, :] = mine + jnp.where(rim_side, theirs, mine)
            halo = jnp.where(last_side, end_halo[0, here, :], end_halo[1, here, :])
            end_field[i, here, :] = jnp.where(beyond, halo, end_field[i, here, :])
    for base in range(PAD - 1, PAD + ROWS + 1, 8):
        here, above, below = slice(base, base + 8), slice(base + 1, base + 9), slice(base - 1, base + 7)
        for i in range(2):
            w = end_wet[i, here, :]
            total = w * (end_side[i, here, :] + (end_wet[i, above, :] + end_wet[i, below, :]))
            c, fn, fs = end_field[i, here, :], end_field[i, above, :], end_field[i, below, :]
            fe, fw = pltpu.roll(c, 128 - LEVELS, 1), pltpu.roll(c, LEVELS, 1)
            lap = w * ((fe + fw) + (fn + fs)) - total * c
            end_once[i, here, :] = lap
            end_part[i, here, :] = (
                c - (end_own[i, 0, here, :] * (fe - fw) + end_own[i, 1, here, :] * (fn - fs))
            ) + (end_k[i, here, :] + end_b[i, here, :] * total) * lap
    for e in range(2, end):
        here = slice(8 * e, 8 * e + 8)
        for i in range(2):
            lap = end_once[i, here, :]
            total = (pltpu.roll(lap, 128 - LEVELS, 1) + pltpu.roll(lap, LEVELS, 1)) + (
                end_once[i, 8 * e + 1:8 * e + 9, :] + end_once[i, 8 * e - 1:8 * e + 7, :])
            end_new[i, 8 * e - PAD:8 * e - PAD + 8, :] = (
                end_part[i, here, :] - end_b[i, here, :] * end_wet[i, here, :] * total)

    def sides(ref, k, south, north):
        return jnp.where(sub < 4, ref[k, south:south + 8, :], ref[k, north:north + 8, :])

    def along(tiles, k):
        if k not in tiles[1]:
            tile = tiles[0](k)
            tiles[1][k] = (tile, pltpu.roll(tile, 128 - LEVELS, 1), pltpu.roll(tile, LEVELS, 1))
        return tiles[1][k]

    def along_row(tiles, k):
        tile, left, right = along(tiles, k)
        return (
            tile,
            jnp.where(lane < 128 - LEVELS, left, along(tiles, (k + 1) % TILES)[1]),
            jnp.where(lane < LEVELS, along(tiles, (k - 1) % TILES)[2], right),
        )

    def put(ref, k, south, north, value):
        ref[k, south:south + 4, :] = value[0:4]
        ref[k, north:north + 8, :] = jnp.where(sub < 4, ref[k, north:north + 8, :], value)

    low, high = PAD - 2, PAD + ROWS - 6
    wets = (lambda k: sides(wet, k, low, high), {})
    states = [(lambda k, f=f: sides(field.at[f], k, low, high), {}) for f in flows]
    for k in inside:
        w, we, ww = along_row(wets, k)
        total = w * ((we + ww) + (sides(wet, k, low + 1, high + 1) + sides(wet, k, low - 1, high - 1)))
        mixing = sides(wide_k, k, low, high) + sides(wide_b, k, low, high) * total
        zonal_own, merid_own = 0.05 * along(states[0], k)[0], 0.05 * along(states[1], k)[0]
        for i, f in enumerate(flows):
            c, fe, fw = along_row(states[i], k)
            fn, fs = sides(field.at[f], k, low + 1, high + 1), sides(field.at[f], k, low - 1, high - 1)
            lap = w * ((fe + fw) + (fn + fs)) - total * c
            put(once.at[f], k, low, high, lap)
            put(part.at[f], k, low, high, (c - (zonal_own * (fe - fw) + merid_own * (fn - fs))) + mixing * lap)
    low, high = PAD, PAD + ROWS - 8
    laps = [(lambda k, f=f: sides(once.at[f], k, low, high), {}) for f in flows]
    for k in inside:
        at = slice(128 * k, 128 * k + 128)
        fade = sides(wide_b, k, low, high) * sides(wet, k, low, high)
        for i, (f, new) in enumerate(zip(flows, (un, vn))):
            _, le, lw = along_row(laps[i], k)
            ln, ls = sides(once.at[f], k, low + 1, high + 1), sides(once.at[f], k, low - 1, high - 1)
            value = sides(part.at[f], k, low, high) - fade * ((le + lw) + (ln + ls))
            new[0:8, at] = jnp.where(sub < 4, value, new[0:8, at])
            new[ROWS - 8:ROWS, at] = jnp.where(sub < 4, new[ROWS - 8:ROWS, at], value)

    for half in range(2):
        width = span if half == 0 else LANES - span
        at = slice(span * half, span * half + width)
        pieces = []
        for new in (un, vn):
            pieces += halves(jnp.concatenate([new[0:8, at], new[ROWS - 8:ROWS, at]], axis=0))
        means = jnp.dot(jnp.concatenate(pieces, axis=0), pick[0:width, :], preferred_element_type=f32)
        for i in range(2):
            value = means[32 * i:32 * i + 16] + means[32 * i + 16:32 * i + 32]
            mean[i, half, 0:8, :] = value[0:8]
            mean[i, half, ROWS - 8:ROWS, :] = value[8:16]
    for i in range(2):
        means = jnp.dot(
            jnp.concatenate(halves(end_new[i]), axis=0), end_pick[i], preferred_element_type=f32)
        value = means[0:ROWS] + means[128:128 + ROWS]
        mean[i, 0] = jnp.where(lane_c < 2, value[:, 0:128], mean[i, 0])
        mean[i, 1] = jnp.where(lane_c // 2 == (COLS - 2 - 128) // 2, value[:, 128:256], mean[i, 1])
        for half in range(2):
            plane[i, half, own, :] = base_plane[i, half] + mean[i, half]

    for pack, side, shift in ((wpack2, 0, 0), (epack2, 1, 24)):
        for r in range(2):
            packed = jnp.zeros((8, 128), f32)
            for g in range(8 - r):
                rows = slice(PAD + 16 * g + 8 * r, PAD + 16 * g + 8 * r + 8)
                for p in range(2):
                    turned = pltpu.roll(plane[p, side, rows, :], (16 * g + 8 * p + shift) % 128, 1)
                    packed = jnp.where(lane // 8 == 2 * g + p, turned, packed)
            pack[8 * r:8 * r + 8, :] = packed

    def three2(ref):
        return ref, ref.at[pl.ds(0, 8)], ref.at[pl.ds(0, 8)]

    def spots2(ref):
        return ref.at[pl.ds(0, 16)], ref.at[pl.ds(16, 8)], ref.at[pl.ds(24, 8)]

    for p in range(2):
        for half in range(2):
            npack2[p, half] = plane[p, half, PAD + ROWS - 8:PAD + ROWS, :]
            spack2[p, half] = plane[p, half, PAD:PAD + 8, :]
    east, west, from_west, from_east = three2(epack2), three2(wpack2), spots2(rw2), spots2(re2)
    wires2 = near.wire(npack2, spack2, east, west, rn2, rs2, from_west, from_east, send2, recv2)
    near.start(wires2, east, west, from_west, from_east)

    for e in range(2, end):
        rows = slice(8 * e - PAD, 8 * e - PAD + 8)
        for i in range(2):
            tile, new, f = end_new[i, rows, :], (un, vn)[i], i + 2
            begin = pltpu.roll(tile, (64 - 16 * f) % 128, 1)
            last = pltpu.roll(tile, 128 - 16 * f, 1)
            new[rows, 0:128] = jnp.where(lane < 16, begin, new[rows, 0:128])
            new[rows, LANES - 128:LANES] = jnp.where(lane >= 112, last, new[rows, LANES - 128:LANES])

    near.arrived(wires_b)

    @pl.when(near.x == 0)
    def _():
        rs_b[:, 8:16, :] = jnp.zeros((RING // 2 + 2, 8, 128), f32)
        rw_b[0:8, :] = jnp.zeros((8, 128), f32)
        re_b[0:8, :] = jnp.zeros((8, 128), f32)

    @pl.when(near.top)
    def _():
        mirror_rows(rn_b, 1.0)
        mirror = (2 * COLS - 241 - lane) % 128
        start = pick_lanes(turn_rows(rn_b.at[RING // 2 + 1, 8:16, :]), mirror)
        last = pick_lanes(turn_rows(rn_b.at[RING // 2, 8:16, :]), mirror)
        rn_b[RING // 2, 8:16, :] = jnp.where(lane < 112, start, last)
        rn_b[RING // 2 + 1, 8:16, :] = jnp.where(lane < 112, last, start)
        index = jnp.where(
            lane < 8, 71 - lane, jnp.where(jnp.logical_and(lane >= 48, lane < 80), swap - 48, 100))
        rw_b[ROWS + 8:ROWS + 16, :] = pick_lanes(turn_rows(rw_b.at[ROWS + 8:ROWS + 16, :]), index)
        index = jnp.where(lane < 64, swap + 48, jnp.where(lane < 72, 71 - lane, 20))
        re_b[ROWS + 8:ROWS + 16, :] = pick_lanes(turn_rows(re_b.at[ROWS + 8:ROWS + 16, :]), index)

    halo_rows(tracers, rs_b, rn_b)
    west, east = rw_b[...], re_b[...]
    wet_east, wet_west = wet_beyond[0, ends, :], wet_beyond[1, ends, :]
    wet[TILES, ends, :] = jnp.where(lane_h < 64, wet_east, wet_west)
    for f in tracers:
        right = pltpu.roll(east, 128 - 16 * f, 1) if f else east
        field[f, TILES, ends, :] = jnp.where(lane_h < 64, right, pltpu.roll(west, 64 - 16 * f, 1))
    for e in (1, 2, end - 1, end):
        weigh(8 * e, everywhere, (8 * e,))
    weigh(8 * 3, rim, [8 * e for e in early[1:]])
    weigh(8 * middle, rim, (8 * middle,))
    weigh(8 * (middle + 1), rim, [8 * e for e in late[:-1]])
    for e in (1, end):
        first(8 * e, everywhere, tracers, RING, whole=False)
    by_three(2, end, lambda e: first(at_tile(e), everywhere, tracers, RING))
    by_three(2, end, lambda e: second(e, inside, tracers, RING))

    for (got, flag), at in zip(((rs_b, halo_flags[0]), (rn_b, halo_flags[1])), (PAD - 8, PAD + ROWS)):
        for half in range(2):
            plane[2, half, at:at + 8, :] = got[RING // 2 + half, 8:16, :]
        plane[3, 0, at:at + 8, :] = jnp.where(
            lane < BLOCK, flag[0], jnp.where(lane < 2 * BLOCK, flag[1], flag[2]))
        plane[3, 1, at:at + 8, :] = jnp.where(lane < 3 * BLOCK - 128, flag[2], flag[3])
    for p, beyond in (
        (2, jnp.where(lane_h < 120, pltpu.roll(east, 48, 1), pltpu.roll(west, 120, 1))),
        (3, jnp.where(lane_h < 120, wet_east, wet_west)),
    ):
        plane[p, 1, ends, :] = jnp.where(lane_h < 112, plane[p, 1, ends, :], beyond)

    def column_on(tiles):
        turned = [pltpu.roll(tile, 127, 1) for tile in tiles]
        return [jnp.where(lane < 127, turned[half], turned[1 - half]) for half in range(2)]

    for e in range(1, end + 1):
        here = slice(8 * e, 8 * e + 8)
        for half in range(2):
            plane[3, half, here, :] = 0.3 * plane[3, half, here, :]
        for p, to in ((0, 0), (3, 1)):
            if p or 1 < e < end:
                for half, tile in enumerate(column_on([plane[p, half, here, :] for half in range(2)])):
                    shifted[to, half, here, :] = tile

    near.arrived(wires2)

    @pl.when(near.x == 0)
    def _():
        rs2[...] = jnp.zeros(rs2.shape, f32)
        rw2[16:24, :] = jnp.zeros((8, 128), f32)
        re2[16:24, :] = jnp.zeros((8, 128), f32)

    @pl.when(near.top)
    def _():
        for p in range(2):
            start = -pick_lanes(turn_rows(rn2.at[p, 1]), (239 - lane) % 128)
            last = -pick_lanes(turn_rows(rn2.at[p, 0]), (239 - lane) % 128)
            rn2[p, 0] = jnp.where(lane < 112, start, last)
            rn2[p, 1] = jnp.where(lane < 112, last, start)
        for got in (rw2, re2):
            got[24:32, :] = -pick_lanes(turn_rows(got.at[24:32, :]), 112 + (lane // 8 % 2) * 8 + 7 - lane % 8)

    for got, at in ((rs2, PAD - 8), (rn2, PAD + ROWS)):
        for half, tile in enumerate(column_on([got[0, half] for half in range(2)])):
            shifted[0, half, at:at + 8, :] = tile
            plane[1, half, at:at + 8, :] = got[1, half]
    for e in range(1, end + 1):
        here = slice(8 * e, 8 * e + 8)
        g = 7 if e == 1 else 0 if e == end else (e - 2) // 2
        at = 16 if e == 1 else 24 if e == end else 8 * (e % 2)
        for p, off in ((0, 1), (1, 0)):
            beyond = jnp.where(
                lane < 120 - off,
                pltpu.roll(re2[at:at + 8, :], (112 - 16 * g - 8 * p - off) % 128, 1),
                pltpu.roll(rw2[at:at + 8, :], (120 - 16 * g - 8 * p - off) % 128, 1))
            ref = plane.at[1, 1] if p else shifted.at[0, 1]
            theirs = jnp.logical_and(lane >= 112 - off, lane < 128 - off)
            ref[here, :] = jnp.where(theirs, beyond, ref[here, :])

    def apart(tiles, ahead):
        turned = [pltpu.roll(tile, 126 if ahead else 2, 1) for tile in tiles]
        if ahead:
            return [jnp.where(lane < 126, turned[half], turned[1 - half]) - tiles[half] for half in range(2)]
        return [tiles[half] - jnp.where(lane < 2, turned[1 - half], turned[half]) for half in range(2)]

    def rows_apart(p, half, e):
        return plane[p, half, 8 * e + 1:8 * e + 9, :] - plane[p, half, 8 * e - 1:8 * e + 7, :]

    for n in range(NSUB):
        for e in range(1, end + 1):
            here = slice(8 * e, 8 * e + 8)
            slope = apart([shifted[0, half, here, :] for half in range(2)], False)
            for half in range(2):
                flow = slope[half] + rows_apart(1, half, e)
                plane[2, half, here, :] = plane[2, half, here, :] - plane[3, half, here, :] * flow
        inner = 1 if n == NSUB - 1 else 0
        for e in range(1 + inner, end + 1 - inner):
            here = slice(8 * e, 8 * e + 8)
            slope = apart([plane[2, half, here, :] for half in range(2)], True)
            for half in range(2):
                shifted[0, half, here, :] = shifted[0, half, here, :] - shifted[1, half, here, :] * slope[half]
                plane[1, half, here, :] = plane[1, half, here, :] - plane[3, half, here, :] * rows_apart(2, half, e)
    for e in range(2, end):
        here = slice(8 * e, 8 * e + 8)
        turned = [pltpu.roll(shifted[0, half, here, :], 1, 1) for half in range(2)]
        for half in range(2):
            plane[0, half, here, :] = jnp.where(lane < 1, turned[1 - half], turned[half])
    for half, width in ((0, 128), (1, COLS - 128)):
        at = slice(128 * half, 128 * half + 128)
        du[:, at] = plane[0, half, own, :] - mean[0, half]
        dv[:, at] = plane[1, half, own, :] - mean[1, half]
        at = slice(128 * half, 128 * half + width)
        for p, ref in ((0, zonal), (1, merid), (2, height)):
            ref[:, at] = plane[p, half, own, 0:width]
    near.sent(wires, wires_b, wires2)


def finish_kernel(
    tn, sn, un, vn, du, dv, height, zonal, merid,
    t_out, s_out, u_out, v_out, height_out, zonal_out, merid_out, done, sems,
):
    copies = [
        pltpu.make_async_copy(src, dst, sems.at[i])
        for i, (src, dst) in enumerate(
            ((tn, t_out), (sn, s_out), (height, height_out), (zonal, zonal_out), (merid, merid_out)))
    ]
    for copy in copies:
        copy.start()
    step = 24
    for i in range(ROWS // step):
        for f, (new, change, out) in enumerate(((un, du, u_out), (vn, dv, v_out))):
            for r in range(step * i, step * i + step, 8):
                for half in range(2):
                    tile = change[r:r + 8, 128 * half:128 * half + 128]
                    for k in range(8 * half, min(8 * half + 8, TILES)):
                        at = slice(128 * k, 128 * k + 128)
                        done[f, r:r + 8, at] = new[r:r + 8, at] + expand(tile, k % 8)
            rows = pl.ds(step * i, step)
            copies.append(pltpu.make_async_copy(done.at[f, rows, :], out.at[rows, :], sems.at[5 + 2 * i + f]))
            copies[-1].start()
    for copy in copies:
        copy.wait()


def per_device(nb, nw, t, s, u, v, elev, zavg, mavg, flags, sel, ktab, btab):
    f32 = jnp.float32
    vmem = pl.BlockSpec(memory_space=pltpu.VMEM)
    hbm = pl.BlockSpec(memory_space=pl.ANY)
    scratch = lambda *shape: pltpu.VMEM(shape, f32)
    dma = lambda *shape: pltpu.SemaphoreType.DMA(shape)
    parts = pl.pallas_call(
        functools.partial(step_kernel, nb, nw),
        out_shape=(pltpu.VMEM((ROWS, LANES), f32),) * 2
        + (pltpu.VMEM((ROWS + 8, LANES), f32),) * 2
        + (pltpu.VMEM((ROWS, 256), f32),) * 2
        + (pltpu.VMEM((ROWS, COLS), f32),) * 3,
        in_specs=[hbm] * 11,
        out_specs=(vmem,) * 9,
        scratch_shapes=[
            pltpu.SMEM((2, 4), jnp.int32),
            pltpu.SMEM((8,), f32),
            pltpu.SMEM((8,), f32),
            pltpu.VMEM((ROWS, COLS), jnp.int32),
            scratch(ROWS, COLS), scratch(ROWS, COLS), scratch(ROWS, COLS),
            scratch(2, 2, 8, LANES), scratch(2, 2, ROWS, 128), scratch(4, ROWS, LANES),
            scratch(RING // 2, 8, 128), scratch(RING // 2, 8, 128), scratch(64, 128), scratch(64, 128),
            scratch(RING // 2, 24, 128), scratch(RING // 2, 24, 128), scratch(80, 128), scratch(80, 128),
            scratch(RING // 2 + 2, 8, 128), scratch(RING // 2 + 2, 8, 128), scratch(ROWS, 128), scratch(ROWS, 128),
            scratch(RING // 2 + 2, 24, 128), scratch(RING // 2 + 2, 24, 128),
            scratch(ROWS + 16, 128), scratch(ROWS + 16, 128),
            scratch(4, RING, BAND, 128), scratch(4, RING, BAND, 128), scratch(4, TILES, BAND, 128),
            scratch(RING, BAND, 128), scratch(RING, BAND, 128),
            scratch(TILES, BAND, 128), scratch(TILES, BAND, 128),
            pltpu.VMEM((128 * LEVELS, 128), jnp.bfloat16), pltpu.VMEM((2, 128, 256), jnp.bfloat16),
            pltpu.VMEM((256, 128 * LEVELS), jnp.bfloat16),
            scratch(2, 2, ROWS, 128), scratch(2, 2, ROWS, 128),
            scratch(2, BAND, 128), scratch(2, 2, BAND, 128), scratch(2, BAND, 128), scratch(2, BAND, 128),
            scratch(2, BAND, 128), scratch(2, BAND, 128), scratch(2, BAND, 128), scratch(2, BAND, 128),
            scratch(2, 128, 128), scratch(2, BAND, 128), scratch(2, BAND, 128), scratch(2, 2, BAND, 128),
            scratch(4, 2, BAND, 128), scratch(2, 2, 8, 128), scratch(2, 2, 8, 128), scratch(16, 128), scratch(16, 128),
            scratch(2, 2, 8, 128), scratch(2, 2, 8, 128), scratch(32, 128), scratch(32, 128),
            dma(15), dma(4), dma(8), dma(8), dma(8), dma(8), dma(8), dma(8),
        ],
        compiler_params=pltpu.CompilerParams(
            collective_id=0, has_side_effects=True, vmem_limit_bytes=VMEM_BYTES),
        name="step",
    )(flags, ktab, btab, sel, t, s, u, v, zavg, mavg, elev)
    parts = [pltpu.with_memory_space_constraint(part, pltpu.VMEM) for part in parts]

    big = jax.ShapeDtypeStruct((ROWS, LANES), f32)
    flat = jax.ShapeDtypeStruct((ROWS, COLS), f32)
    return pl.pallas_call(
        finish_kernel,
        out_shape=(big,) * 4 + (flat,) * 3,
        in_specs=[vmem] * 9,
        out_specs=(hbm,) * 7,
        scratch_shapes=[scratch(2, ROWS, LANES), dma(15)],
        compiler_params=pltpu.CompilerParams(vmem_limit_bytes=VMEM_BYTES),
        name="finish",
    )(*parts)


def solution(mesh):
    grid = P("wide", "blocks")
    return jax.shard_map(
        functools.partial(per_device, mesh.shape["blocks"], mesh.shape["wide"]),
        mesh=mesh,
        in_specs=(grid,) * 9 + (P(), P()),
        out_specs=(grid,) * 7,
        check_vma=False,
    )
```
